32 devices in a mesh: samp: 4 (over y, x), seq: 8 (over z, core).
Axes of the slice: x: 2, y: 2, z: 4, core: 2. Of those that a mesh axis runs over, the one named last changes fastest.
Arguments:
- tokens: bfloat16 [4, 1024, 1024], P('samp', 'seq'), may hold values from -6 to 6
- lead_hours: int32 [4], P('samp'), may hold values from 0 to 168
- var_mask: int32 [4, 48], P('samp'), may hold values 0 or 1
- var_table: bfloat16 [48, 1024], P(None, ('samp', 'seq')), may hold values from -0.875 to 0.875
- lead_weight: bfloat16 [1024], P(('samp', 'seq')), may hold values from -3 to 3
- norm_gain: bfloat16 [2, 1024], P(None, ('samp', 'seq')), may hold values from 0.5 to 1.5
- norm_shift: bfloat16 [2, 1024], P(None, ('samp', 'seq')), may hold values from -2 to 2
- w_qkv: bfloat16 [1024, 3072], P(('samp', 'seq')), may hold values from -0.25 to 0.25
- qv_bias: bfloat16 [2, 1024], P(None, ('samp', 'seq')), may hold values from -2 to 2
- w_out: bfloat16 [1024, 1024], P(('samp', 'seq')), may hold values from -1 to 1
- branch_bias: bfloat16 [2, 1024], P(None, ('samp', 'seq')), may hold values from -2 to 2
- w_up: bfloat16 [1024, 4096], P(('samp', 'seq')), may hold values from -0.1875 to 0.1875
- up_bias: bfloat16 [4096], P(('samp', 'seq')), may hold values from -2 to 2
- w_down: bfloat16 [4096, 1024], P(('samp', 'seq')), may hold values from -0.1875 to 0.1875
- cotangent: bfloat16 [4, 1024, 1024], P('samp', 'seq'), may hold values from -6 to 6
Outputs:
- mixed: bfloat16 [4, 1024, 1024], P('samp', 'seq')
- tokens_grad: float32 [4, 1024, 1024], P('samp', 'seq')
- var_table_grad: float32 [48, 1024], P(None, ('samp', 'seq'))
- lead_weight_grad: float32 [1024], P(('samp', 'seq'))
- norm_gain_grad: float32 [2, 1024], P(None, ('samp', 'seq'))
- norm_shift_grad: float32 [2, 1024], P(None, ('samp', 'seq'))
- w_qkv_grad: float32 [1024, 3072], P(('samp', 'seq'))
- qv_bias_grad: float32 [2, 1024], P(None, ('samp', 'seq'))
- w_out_grad: float32 [1024, 1024], P(('samp', 'seq'))
- branch_bias_grad: float32 [2, 1024], P(None, ('samp', 'seq'))
- w_up_grad: float32 [1024, 4096], P(('samp', 'seq'))
- up_bias_grad: float32 [4096], P(('samp', 'seq'))
- w_down_grad: float32 [4096, 1024], P(('samp', 'seq'))
The draws below stay inside these ranges and needn't reach their ends.
Inputs may be any that keep to these rules, and one draw needn't show every extreme that they name: `lead_hours`: lead time of each sample in whole hours. `var_mask`: 1 where a sample holds a variable, else 0.
All inputs are finite; a program needn't handle non-finite values. No bound on the sum of `var_mask` on one device may be relied on, other than what follows from the above.
Results may differ from the reference program's by a relative error of at most 0.014.
Values may be sent and summed in bfloat16 or wider, within the bound.
A program may use at most 192 MiB of HBM per device.

```python
import jax
import jax.numpy as jnp
from jax import lax

D = 1024
HEADS = 16
HEAD_DIM = 64
FF = 4096
VARS = 48
SAMPLES = 4
LENGTH = 1024


def plant(array, rng, smallest, top_value):
    spot = [jax.random.randint(jax.random.fold_in(rng, axis), (), 0, length) for axis, length in enumerate(array.shape)]
    main_axis = array.shape.index(max(array.shape))
    neighbour = spot[:main_axis] + [(spot[main_axis] + 1) % array.shape[main_axis]] + spot[main_axis + 1:]
    return array.at[tuple(spot)].set(smallest).at[tuple(neighbour)].set(top_value)


def block_levels(stream_key, shape, cuts, smallest, top_value):
    def one(position, parts):
        steps = jax.random.uniform(jax.random.fold_in(jax.random.fold_in(stream_key, 6), position), (parts,), jnp.float32, smallest / len(cuts), top_value / len(cuts))
        return jnp.repeat(jnp.exp(steps), shape[position] // parts).reshape((-1,) + (1,) * (len(shape) - position - 1))

    loudness = one(*cuts[0])
    for cut in cuts[1:]:
        loudness = loudness * one(*cut)
    return loudness


def gaussian(own_key, dims, width, most, cuts=(), kind=jnp.bfloat16):
    values = width * jax.random.normal(own_key, dims, jnp.float32)
    if cuts:
        values = values * block_levels(own_key, dims, cuts, -0.22, 0.18)
    return jnp.clip(values, -most, most).astype(kind)


def setup_inputs(seed: int = 0) -> dict:
    arg_keys = jax.random.split(jax.random.key(seed), 16)
    tokens = gaussian(arg_keys[0], (SAMPLES, LENGTH, D), 1.0, 6.0, ((0, 4), (1, 8)))
    lead_hours = plant(jax.random.randint(arg_keys[1], (SAMPLES,), 0, 169), jax.random.fold_in(arg_keys[1], 1), 0, 168).astype(jnp.int32)
    var_mask = plant((jax.random.randint(arg_keys[2], (SAMPLES, VARS), 0, 2) < 1).astype(jnp.int32), jax.random.fold_in(arg_keys[2], 1), 0, 1)
    var_table = gaussian(arg_keys[3], (VARS, D), VARS ** -0.5, 0.875, ((1, 32),))
    lead_weight = gaussian(arg_keys[4], (D,), 0.5, 3.0, ((0, 32),))
    norm_gain = jnp.clip(1.0 + 0.1 * jax.random.normal(arg_keys[5], (2, D), jnp.float32), 0.5, 1.5).astype(jnp.bfloat16)
    norm_shift = gaussian(arg_keys[6], (2, D), 0.3, 2.0, ((1, 32),))
    w_qkv = gaussian(arg_keys[7], (D, 3 * D), (D // 2) ** -0.5, 0.25, ((0, 32),))
    qv_bias = gaussian(arg_keys[8], (2, D), 0.3, 2.0, ((1, 32),))
    w_out = gaussian(arg_keys[9], (D, D), 32 ** -0.5, 1.0, ((0, 32),))
    branch_bias = gaussian(arg_keys[10], (2, D), 0.3, 2.0, ((1, 32),))
    w_up = gaussian(arg_keys[11], (D, FF), D ** -0.5, 0.1875, ((0, 32),))
    up_bias = gaussian(arg_keys[12], (FF,), 0.3, 2.0, ((0, 32),))
    w_down = gaussian(arg_keys[13], (FF, D), (FF // 4) ** -0.5, 0.1875, ((0, 32),))
    cotangent = gaussian(arg_keys[14], (SAMPLES, LENGTH, D), 1.0, 6.0, ((0, 4), (1, 8)))
    return {"tokens": tokens, "lead_hours": lead_hours, "var_mask": var_mask, "var_table": var_table, "lead_weight": lead_weight, "norm_gain": norm_gain, "norm_shift": norm_shift, "w_qkv": w_qkv, "qv_bias": qv_bias, "w_out": w_out, "branch_bias": branch_bias, "w_up": w_up, "up_bias": up_bias, "w_down": w_down, "cotangent": cotangent}


@jax.custom_vjp
def low(v):
    return lax.optimization_barrier(v.astype(jnp.bfloat16)).astype(jnp.float32)

@jax.custom_vjp
def low_back(v):
    return v

def low_keep(v):
    return (low(v), None)

def low_pass(kept, grad):
    return (grad,)

def back_keep(v):
    return (v, None)

def back_low(kept, grad):
    return (low(grad),)
low.defvjp(low_keep, low_pass)
low_back.defvjp(back_keep, back_low)
epsilon = 1e-05
hours_scale = 1.0 / 168.0
highest = lax.Precision.HIGHEST

def normalize(field, scaling, offsets):
    average = lax.optimization_barrier(jnp.mean(field, axis=-1, keepdims=True))
    centred = field - average
    variance = lax.optimization_barrier(jnp.mean(centred * centred, axis=-1, keepdims=True))
    return centred * lax.rsqrt(variance + epsilon) * scaling + offsets

def attend_block(query_block, keys_all, values_all):
    scores = low_back(jnp.einsum('qhd,khd->hqk', query_block, keys_all, precision=highest))
    shares = low(jax.nn.softmax(scores, axis=-1))
    return jnp.einsum('hqk,khd->qhd', shares, values_all, precision=highest)

def layer(params, sample, lead_value, present):
    var_table, lead_weight, norm_gain, norm_shift, w_qkv, qv_bias, w_out, branch_bias, w_up, up_bias, w_down = params
    length = sample.shape[0]
    stream = sample + lead_value * hours_scale * lead_weight + jnp.dot(present, var_table, precision=highest)
    normed = low(normalize(stream, norm_gain[0], norm_shift[0]))
    projected = jnp.dot(normed, w_qkv, precision=highest)
    factor = HEAD_DIM ** (-0.5)
    queries = low(low_back((projected[:, :D] + qv_bias[0]) * factor))
    keys_all = low(low_back(projected[:, D:2 * D]))
    values_all = low(low_back(projected[:, 2 * D:] + qv_bias[1]))
    block_rows = min(512, length)
    query_blocks = queries.reshape(length // block_rows, block_rows, HEADS, HEAD_DIM)
    key_heads = keys_all.reshape(length, HEADS, HEAD_DIM)
    value_heads = values_all.reshape(length, HEADS, HEAD_DIM)

    def one_block(query_block):
        return jax.checkpoint(attend_block)(query_block, key_heads, value_heads)
    attended = lax.map(one_block, query_blocks)
    attended = low(low_back(attended.reshape(length, D)))
    branch = low_back(jnp.dot(attended, w_out, precision=highest) + branch_bias[0])
    middle = stream + branch
    normed_two = low(normalize(middle, norm_gain[1], norm_shift[1]))
    upward = low_back(jnp.dot(normed_two, w_up, precision=highest) + up_bias)
    activated = low(jax.nn.gelu(upward, approximate=False))
    downward = low_back(jnp.dot(activated, w_down, precision=highest) + branch_bias[1])
    return middle + downward

def reference(tokens, lead_hours, var_mask, var_table, lead_weight, norm_gain, norm_shift, w_qkv, qv_bias, w_out, branch_bias, w_up, up_bias, w_down, cotangent):
    params = tuple((item.astype(jnp.float32) for item in (var_table, lead_weight, norm_gain, norm_shift, w_qkv, qv_bias, w_out, branch_bias, w_up, up_bias, w_down)))

    def one_sample(totals, inputs):
        sample, lead_value, present, seed_grad = inputs

        def forward(params_in, sample_in):
            return layer(params_in, sample_in, lead_value, present)
        result, pullback = jax.vjp(forward, params, sample)
        gradients, sample_grad = pullback(seed_grad)
        totals = jax.tree.map(lambda a, b: a + b, totals, gradients)
        return (totals, (result.astype(jnp.bfloat16), sample_grad))
    initial = jax.tree.map(jnp.zeros_like, params)
    inputs = (tokens.astype(jnp.float32), lead_hours.astype(jnp.float32), var_mask.astype(jnp.float32), cotangent.astype(jnp.float32))
    totals, outputs = lax.scan(one_sample, initial, inputs)
    mixed, tokens_grad = outputs
    return (mixed, tokens_grad, totals[0], totals[1], totals[2], totals[3], totals[4], totals[5], totals[6], totals[7], totals[8], totals[9], totals[10])
```

```python
import jax
import jax.numpy as jnp
from jax import lax
from jax.experimental import pallas as pl
from jax.experimental.pallas import tpu as pltpu
from jax.sharding import PartitionSpec as P

HEADS = 16
HEAD_DIM = 64


epsilon = 1e-05
hours_scale = 1.0 / 168.0


def from_behind(block, axis, distance):
    devices = range(lax.axis_size(axis))
    route = [((i - distance) % len(devices), i) for i in devices]
    return lax.ppermute(block, axis, route)


def normalize(field, scaling, offsets):
    average = jnp.mean(field, axis=-1, keepdims=True)
    centred = field - average
    variance = jnp.mean(centred * centred, axis=-1, keepdims=True)
    return centred * lax.rsqrt(variance + epsilon) * scaling + offsets


def block_size(length):
    size_now = length
    while size_now > 512 and size_now % 2 == 0:
        size_now = size_now // 2
    return size_now


def over_blocks(advance, carried, segments):
    length = segments[0].shape[1]
    size_now = block_size(length)
    number = length // size_now
    stacked = tuple(
        (
            jnp.moveaxis(
                segment.reshape(segment.shape[0], number, size_now, segment.shape[2]), 1, 0
            )
            for segment in segments
        )
    )

    def visit(current, blocks):
        return (advance(current, blocks), None)

    carried, _ = lax.scan(visit, carried, stacked)
    return carried


def split_heads(matrix):
    return matrix.reshape(matrix.shape[0], matrix.shape[1], HEADS, HEAD_DIM)


def gelu_slope(upward):
    normal_cdf = 0.5 * (1.0 + lax.erf(upward * 0.7071067811865476))
    density = jnp.exp(-0.5 * upward * upward) * 0.3989422804014327
    return normal_cdf + upward * density


def pair_terms(query_heads, grad_heads, log_total, offset, key_heads, value_heads):
    scores = jnp.einsum(
        "sqhd,skhd->shqk", query_heads, key_heads, preferred_element_type=jnp.float32
    )
    shares = jnp.exp(scores - log_total[..., None])
    pressure = jnp.einsum(
        "sqhd,skhd->shqk", grad_heads, value_heads, preferred_element_type=jnp.float32
    )
    score_grad = (shares * (pressure - offset[..., None])).astype(jnp.bfloat16)
    query_part = jnp.einsum(
        "shqk,skhd->sqhd", score_grad, key_heads, preferred_element_type=jnp.float32
    )
    key_part = jnp.einsum(
        "shqk,sqhd->skhd", score_grad, query_heads, preferred_element_type=jnp.float32
    )
    value_part = jnp.einsum(
        "shqk,sqhd->skhd",
        shares.astype(jnp.bfloat16),
        grad_heads,
        preferred_element_type=jnp.float32,
    )
    return (query_part, key_part, value_part)


def local(
    tokens,
    lead_hours,
    var_mask,
    var_table,
    lead_weight,
    norm_gain,
    norm_shift,
    w_qkv,
    qv_bias,
    w_out,
    branch_bias,
    w_up,
    up_bias,
    w_down,
    cotangent,
):
    samples, patches, features = tokens.shape
    row_count = samples * patches
    factor = HEAD_DIM ** (-0.5)
    (
        table_full,
        lead_full,
        gain_all,
        shift_all,
        qkv_full,
        qv_all,
        out_full,
        bias_all,
        up_full,
        upb_full,
        down_full,
    ) = (
        lax.all_gather(var_table, ("samp", "seq"), axis=1, tiled=True),
        lax.all_gather(lead_weight, ("samp", "seq"), axis=0, tiled=True),
        lax.all_gather(norm_gain, ("samp", "seq"), axis=1, tiled=True),
        lax.all_gather(norm_shift, ("samp", "seq"), axis=1, tiled=True),
        lax.all_gather(w_qkv, ("samp", "seq"), axis=0, tiled=True),
        lax.all_gather(qv_bias, ("samp", "seq"), axis=1, tiled=True),
        lax.all_gather(w_out, ("samp", "seq"), axis=0, tiled=True),
        lax.all_gather(branch_bias, ("samp", "seq"), axis=1, tiled=True),
        lax.all_gather(w_up, ("samp", "seq"), axis=0, tiled=True),
        lax.all_gather(up_bias, ("samp", "seq"), axis=0, tiled=True),
        lax.all_gather(w_down, ("samp", "seq"), axis=0, tiled=True),
    )
    gain_full = gain_all.astype(jnp.float32)
    shift_full = shift_all.astype(jnp.float32)
    qv_full = qv_all.astype(jnp.float32)
    bias_full = bias_all.astype(jnp.float32)
    lead_value = lead_hours.astype(jnp.float32) * hours_scale
    present = var_mask.astype(jnp.float32)
    variable_sum = jnp.dot(present, table_full.astype(jnp.float32), precision=lax.Precision.HIGHEST)
    stream = (
        tokens.astype(jnp.float32)
        + lead_value[:, None, None] * lead_full.astype(jnp.float32)
        + variable_sum[:, None, :]
    )
    stream_rows = stream.reshape(row_count, features)
    normed = normalize(stream_rows, gain_full[0], shift_full[0]).astype(jnp.bfloat16)
    projected = jnp.dot(normed, qkv_full, preferred_element_type=jnp.float32)
    queries = (
        ((projected[:, :features] + qv_full[0]) * factor)
        .astype(jnp.bfloat16)
        .reshape(samples, patches, features)
    )
    keys_all = (
        projected[:, features : 2 * features]
        .astype(jnp.bfloat16)
        .reshape(samples, patches, features)
    )
    values_all = (
        (projected[:, 2 * features :] + qv_full[1])
        .astype(jnp.bfloat16)
        .reshape(samples, patches, features)
    )
    query_heads = split_heads(queries)

    def scores_of(keys_block):
        return jnp.einsum(
            "sqhd,skhd->shqk",
            query_heads,
            split_heads(keys_block),
            preferred_element_type=jnp.float32,
        )

    def stats_step(carried, blocks):
        running_max, running_sum = carried
        scores = scores_of(blocks[0])
        new_max = jnp.maximum(running_max, jnp.max(scores, axis=-1))
        running_sum = running_sum * jnp.exp(running_max - new_max) + jnp.sum(
            jnp.exp(scores - new_max[..., None]), axis=-1
        )
        return (new_max, running_sum)

    stats_start = (
        jnp.full((samples, HEADS, patches), -jnp.inf, jnp.float32),
        jnp.zeros((samples, HEADS, patches), jnp.float32),
    )
    running_max, running_sum = over_blocks(
        stats_step, stats_start, (lax.all_gather(keys_all, "seq", axis=1, tiled=True),)
    )
    log_total = running_max + jnp.log(running_sum)

    def mix_step(collected, blocks):
        shares = jnp.exp(scores_of(blocks[0]) - log_total[..., None]).astype(jnp.bfloat16)
        return collected + jnp.einsum(
            "shqk,skhd->sqhd", shares, split_heads(blocks[1]), preferred_element_type=jnp.float32
        )

    zero_heads = jnp.zeros((samples, patches, HEADS, HEAD_DIM), jnp.float32)
    attended_f = over_blocks(
        mix_step,
        zero_heads,
        (
            lax.all_gather(keys_all, "seq", axis=1, tiled=True),
            lax.all_gather(values_all, "seq", axis=1, tiled=True),
        ),
    )
    attended = attended_f.reshape(row_count, features).astype(jnp.bfloat16)
    middle = stream_rows + (
        jnp.dot(attended, out_full, preferred_element_type=jnp.float32) + bias_full[0]
    )
    normed_two = normalize(middle, gain_full[1], shift_full[1]).astype(jnp.bfloat16)
    upward = jnp.dot(normed_two, up_full, preferred_element_type=jnp.float32) + upb_full.astype(
        jnp.float32
    )
    activated = jax.nn.gelu(upward, approximate=False).astype(jnp.bfloat16)
    downward = jnp.dot(activated, down_full, preferred_element_type=jnp.float32) + bias_full[1]
    mixed = (middle + downward).astype(jnp.bfloat16).reshape(samples, patches, features)
    gain_back, qkv_back, out_back, up_back, down_back = (
        lax.all_gather(norm_gain, ("samp", "seq"), axis=1, tiled=True),
        lax.all_gather(w_qkv, ("samp", "seq"), axis=0, tiled=True),
        lax.all_gather(w_out, ("samp", "seq"), axis=0, tiled=True),
        lax.all_gather(w_up, ("samp", "seq"), axis=0, tiled=True),
        lax.all_gather(w_down, ("samp", "seq"), axis=0, tiled=True),
    )
    gain_back = gain_back.astype(jnp.float32)
    incoming = cotangent.astype(jnp.float32).reshape(row_count, features)
    incoming_low = incoming.astype(jnp.bfloat16)
    down_grad = jnp.einsum("tf,td->fd", activated, incoming_low, preferred_element_type=jnp.float32)
    down_bias_grad = jnp.sum(incoming_low.astype(jnp.float32), axis=0)
    gelu_grad = jnp.einsum(
        "td,fd->tf", incoming_low, down_back, preferred_element_type=jnp.float32
    ) * gelu_slope(upward)
    up_low = gelu_grad.astype(jnp.bfloat16)
    up_grad = jnp.einsum("td,tf->df", normed_two, up_low, preferred_element_type=jnp.float32)
    up_bias_grad = jnp.sum(up_low.astype(jnp.float32), axis=0)
    normed_two_grad = jnp.einsum("tf,df->td", up_low, up_back, preferred_element_type=jnp.float32)
    _, pull_second = jax.vjp(normalize, middle, gain_back[1], shift_full[1])
    middle_part, gain_two_grad, shift_two_grad = pull_second(normed_two_grad)
    middle_grad = incoming + middle_part
    middle_low = middle_grad.astype(jnp.bfloat16)
    out_grad = jnp.einsum("te,td->ed", attended, middle_low, preferred_element_type=jnp.float32)
    out_bias_grad = jnp.sum(middle_low.astype(jnp.float32), axis=0)
    attended_grad = jnp.einsum(
        "td,ed->te", middle_low, out_back, preferred_element_type=jnp.float32
    ).astype(jnp.bfloat16)
    grad_rows = attended_grad.reshape(samples, patches, features)
    grad_heads = split_heads(grad_rows)
    offset = jnp.transpose(jnp.sum(grad_heads.astype(jnp.float32) * attended_f, axis=-1), (0, 2, 1))
    grads_start = jnp.zeros((2, samples, patches, HEADS, HEAD_DIM), jnp.float32)

    def visit_block(blocks, partial_grads, query_acc):
        query_part, key_part, value_part = pair_terms(
            query_heads,
            grad_heads,
            log_total,
            offset,
            split_heads(blocks[0]),
            split_heads(blocks[1]),
        )
        return (partial_grads + jnp.stack([key_part, value_part]), query_acc + query_part)

    def turn_grads(partial_grads):
        return from_behind(partial_grads.astype(jnp.bfloat16), "seq", 1).astype(partial_grads.dtype)

    def cycle_step(counter, carried):
        blocks, partial_grads, query_acc = carried
        partial_grads, query_acc = visit_block(blocks, partial_grads, query_acc)
        partial_grads = turn_grads(partial_grads)
        blocks = from_behind(blocks, "seq", 1)
        return (blocks, partial_grads, query_acc)

    blocks_start = jnp.stack([keys_all, values_all])
    blocks, partial_grads, query_acc = lax.fori_loop(
        0, lax.axis_size("seq") - 1, cycle_step, (blocks_start, grads_start, zero_heads)
    )
    partial_grads, query_acc = visit_block(blocks, partial_grads, query_acc)
    partial_grads = turn_grads(partial_grads)
    query_low = query_acc.astype(jnp.bfloat16).reshape(row_count, features) * factor
    key_low = partial_grads[0].astype(jnp.bfloat16).reshape(row_count, features)
    value_low = partial_grads[1].astype(jnp.bfloat16).reshape(row_count, features)
    proj_grad = jnp.concatenate([query_low, key_low, value_low], axis=1)
    qkv_grad = jnp.einsum("td,te->de", normed, proj_grad, preferred_element_type=jnp.float32)
    qv_bias_grad = jnp.stack(
        [
            jnp.sum(query_low.astype(jnp.float32), axis=0),
            jnp.sum(value_low.astype(jnp.float32), axis=0),
        ]
    )
    normed_grad = jnp.einsum("te,de->td", proj_grad, qkv_back, preferred_element_type=jnp.float32)
    _, pull_first = jax.vjp(normalize, stream_rows, gain_back[0], shift_full[0])
    stream_part, gain_one_grad, shift_one_grad = pull_first(normed_grad)
    stream_grad = (middle_grad + stream_part).reshape(samples, patches, features)
    per_sample = jnp.sum(stream_grad, axis=1)
    lead_grad = jnp.sum(lead_value[:, None] * per_sample, axis=0)
    table_grad = jnp.dot(present.T, per_sample, precision=lax.Precision.HIGHEST)
    gain_grad = jnp.stack([gain_one_grad, gain_two_grad])
    shift_grad = jnp.stack([shift_one_grad, shift_two_grad])
    bias_grad = jnp.stack([out_bias_grad, down_bias_grad])
    owned = (
        lax.psum_scatter(table_grad, ("samp", "seq"), scatter_dimension=1, tiled=True),
        lax.psum_scatter(lead_grad, ("samp", "seq"), scatter_dimension=0, tiled=True),
        lax.psum_scatter(gain_grad, ("samp", "seq"), scatter_dimension=1, tiled=True),
        lax.psum_scatter(shift_grad, ("samp", "seq"), scatter_dimension=1, tiled=True),
        lax.psum_scatter(qkv_grad, ("samp", "seq"), scatter_dimension=0, tiled=True),
        lax.psum_scatter(qv_bias_grad, ("samp", "seq"), scatter_dimension=1, tiled=True),
        lax.psum_scatter(out_grad, ("samp", "seq"), scatter_dimension=0, tiled=True),
        lax.psum_scatter(bias_grad, ("samp", "seq"), scatter_dimension=1, tiled=True),
        lax.psum_scatter(up_grad, ("samp", "seq"), scatter_dimension=0, tiled=True),
        lax.psum_scatter(up_bias_grad, ("samp", "seq"), scatter_dimension=0, tiled=True),
        lax.psum_scatter(down_grad, ("samp", "seq"), scatter_dimension=0, tiled=True),
    )
    return (
        mixed,
        stream_grad,
        owned[0],
        owned[1],
        owned[2],
        owned[3],
        owned[4],
        owned[5],
        owned[6],
        owned[7],
        owned[8],
        owned[9],
        owned[10],
    )


MESH = pl.DeviceIdType.MESH
BF = jnp.bfloat16
F32 = jnp.float32
D = 1024
ROWS = 128
LANES = 8
FFL = 512


def dot_nn(a, b):
    return lax.dot_general(a, b, (((1,), (0,)), ((), ())), preferred_element_type=F32)


def dot_nt(a, b):
    return lax.dot_general(a, b, (((1,), (1,)), ((), ())), preferred_element_type=F32)


def dot_tn(a, b):
    return lax.dot_general(a, b, (((0,), (0,)), ((), ())), preferred_element_type=F32)


def erf(v):
    v = jnp.clip(v, -4.0, 4.0)
    s = v * v
    p = jnp.full_like(s, -2.72614225801306e-10)
    for a in (2.77068142495902e-08, -2.10102402082508e-06, -5.69250639462346e-05,
              -7.34990630326855e-04, -2.95459980854025e-03, -1.60960333262415e-02):
        p = p * s + a
    q = jnp.full_like(s, -1.45660718464996e-05)
    for b in (-2.13374055278905e-04, -1.68282697438203e-03, -7.37332916720468e-03, -1.42647390514189e-02):
        q = q * s + b
    return v * p / q


def flip(a, d):
    return 1 - a if d else a


def many(n, m=1):
    return pl.ds(pl.multiple_of(n, m), m)


def center(v):
    mean = jnp.mean(v, axis=-1, keepdims=True)
    centred = v - mean
    var = jnp.mean(centred * centred, axis=-1, keepdims=True)
    rstd = lax.rsqrt(var + epsilon)
    return centred * rstd, rstd


def norm_back(xhat, rstd, gain, grad):
    dx = grad * gain
    return rstd * (dx - jnp.mean(dx, axis=-1, keepdims=True) - xhat * jnp.mean(dx * xhat, axis=-1, keepdims=True))


def fast_kernel(
    tokens, cot, wqkv_in, wout_in, wup_in, wdown_in, pack_in,
    mixed_o, tg_o, gq_o, go_o, gu_o, gd_o, small_o,
    tok_all, cot_all, n2_all, ml_all,
    wqkv, wup, wdown, wout, pack_all, full,
    normed, q_s, k_s, v_s, shares, attf, att,
    rs_s1, rs_r1, rs_s2, rs_r2, own,
    middle, mgrad, act, uplow, dproj, dog, dk_acc, dv_acc,
    gqkv, gup, gdown, gout, rqkv, rup, rdown, rout, sq2, su2, rq2, ru2, so2, ro2,
    tgs, tgr, smallp, s_a, r_a, s_b, r_b, r_c, upb_g, r_upb,
    ss, rs,
):
    s_i = lax.axis_index("samp")
    q_i = lax.axis_index("seq")
    y, x = s_i // 2, s_i % 2
    z, c = q_i // 2, q_i % 2
    k, w = z // 2, z % 2
    idx = 16 * y + 8 * x + 4 * k + 2 * w + c
    lane = 4 * y + 2 * w + c
    rank = 2 * x + k
    sample = 2 * k + x
    off_diag = y + k - 2 * y * k
    is_home = 1 - (x + w - 2 * x * w) - (k + c - 2 * k * c) + (x + w - 2 * x * w) * (k + c - 2 * k * c)
    my_rows = many(ROWS * lane, ROWS)

    def dev(y_, x_, k_, w_, c_):
        return (2 * y_ + x_, 4 * k_ + 2 * w_ + c_)

    count = [0, 0]
    pending = []

    def sems(n):
        a, b = count
        count[0] += n
        count[1] += n
        return a, b

    def rc(src, dst, a, b, device):
        return pltpu.make_async_remote_copy(src_ref=src, dst_ref=dst, send_sem=ss.at[a], recv_sem=rs.at[b], device_id=device, device_id_type=MESH)

    group = [(d // 4, (d // 2) % 2, d % 2) for d in range(1, 8)]
    chips = [(0, 0), (0, 1), (1, 0), (1, 1)]
    ranks = [(0, 1), (1, 0), (1, 1)]

    def peer(d):
        dy, dw, dc = d
        y_, w_, c_ = flip(y, dy), flip(w, dw), flip(c, dc)
        return y_, w_, c_, 4 * y_ + 2 * w_ + c_, dev(y_, x, k, w_, c_)

    def partner(d):
        dx, dk = d
        x_, k_ = flip(x, dx), flip(k, dk)
        return x_, k_, 2 * x_ + k_, dev(y, x_, k_, w, c)

    swap_dev = dev(k, x, y, w, c)

    barrier = pltpu.get_barrier_semaphore()
    for d in group:
        pl.semaphore_signal(barrier, inc=1, device_id=peer(d)[4], device_id_type=MESH)
    for d in ranks:
        pl.semaphore_signal(barrier, inc=1, device_id=partner(d)[3], device_id_type=MESH)

    @pl.when(off_diag == 1)
    def _():
        pl.semaphore_signal(barrier, inc=1, device_id=swap_dev, device_id_type=MESH)

    pl.semaphore_wait(barrier, 10 + off_diag)

    def swap_start(src, dst, a, b):
        @pl.when(off_diag == 1)
        def _():
            rc(src, dst, a, b, swap_dev).start()

    def swap_wait(src, dst, a, b):
        @pl.when(off_diag == 1)
        def _():
            rc(src, dst, a, b, swap_dev).wait()

    class Gather:
        def __init__(self, buf):
            self.buf = buf
            self.a, self.b = sems(8)

        def copy(self, i, forward):
            dy, dw = chips[i]
            if i == 0:
                return rc(self.buf.at[my_rows], self.buf.at[my_rows], self.a, self.b, peer((0, 0, 1))[4])
            y_, w_, c_, l_, dv = peer((dy, dw, 0))
            if forward:
                rows = many(ROWS * l_, ROWS)
                return rc(self.buf.at[rows], self.buf.at[rows], self.a + 4 + i, self.b + 4 + i, peer((0, 0, 1))[4])
            return rc(self.buf.at[my_rows], self.buf.at[my_rows], self.a + i, self.b + i, dv)

        def start(self):
            for i in (3, 1, 2, 0):
                self.copy(i, False).start()

        def pass_on(self):
            for i in (1, 2, 3):
                self.copy(i, False).wait_recv()
                self.copy(i, True).start()

        def finish(self):
            self.copy(0, False).wait_recv()
            for i in (1, 2, 3):
                self.copy(i, True).wait_recv()

        def drain(self):
            for i in range(4):
                self.copy(i, False).wait_send()
            for i in (1, 2, 3):
                self.copy(i, True).wait_send()

    class Scatter:
        def __init__(self, slot, partial):
            self.slot = slot
            self.partial = partial
            self.a1, self.b1 = sems(4)
            self.a2, self.b2 = sems(4)

        def far(self, i):
            dy, dw = i // 2, i % 2
            y_, w_ = y + dy - 2 * y * dy, w + dw - 2 * w * dw
            return y_, w_

        def first(self, i):
            return rc(rs_s1.at[self.slot, i], rs_r1.at[self.slot, i], self.a1 + i, self.b1 + i, dev(y, x, k, w, 1 - c))

        def second(self, i):
            y_, w_ = self.far(i)
            return rc(rs_s2.at[self.slot, i - 1], rs_r2.at[self.slot, i - 1], self.a2 + i, self.b2 + i, dev(y_, x, k, w_, c))

        def start(self):
            @pl.loop(0, 4)
            def _(n):
                i = 3 - n
                y_, w_ = self.far(i)
                rs_s1[self.slot, i] = self.partial(4 * y_ + 2 * w_ + 1 - c).astype(BF)
                self.first(i).start()

            @pl.loop(0, 4)
            def _(n):
                i = 3 - n
                y_, w_ = self.far(i)
                part = self.partial(4 * y_ + 2 * w_ + c)
                self.first(i).wait_recv()
                total = part + rs_r1[self.slot, i].astype(F32)

                @pl.when(i > 0)
                def _():
                    rs_s2[self.slot, i - 1] = total.astype(BF)
                    self.second(i).start()

                @pl.when(i == 0)
                def _():
                    own[self.slot] = total

        def finish(self):
            for i in (1, 2, 3):
                self.second(i).wait_recv()
            total = own[self.slot]
            for i in (1, 2, 3):
                total = total + rs_r2[self.slot, i - 1].astype(F32)
            return total

        def drain(self):
            for i in range(4):
                self.first(i).wait_send()
            for i in (1, 2, 3):
                self.second(i).wait_send()

    class Batch:
        def __init__(self, copies):
            self.copies = copies
            self.a, self.b = sems(len(copies))

        def copy(self, n):
            src, dst, device = self.copies[n]
            return rc(src, dst, self.a + n, self.b + n, device)

        def start(self):
            for n in range(len(self.copies)):
                self.copy(n).start()

        def wait(self):
            for n in range(len(self.copies)):
                self.copy(n).wait_recv()

        def drain(self):
            for n in range(len(self.copies)):
                self.copy(n).wait_send()

    tok_swap = sems(1)
    cot_swap = sems(1)
    swap_rows = many(ROWS * (4 * k + 2 * w + c), ROWS)
    swap_start(tokens, tok_all.at[swap_rows], *tok_swap)

    own_rows = many(32 * idx, 32)
    copies = []
    for d in group:
        y_, w_, c_, l_, dv = peer(d)
        copies.append((pack_in, pack_all.at[idx], dv))
        for p in range(3):
            copies.append((wqkv_in.at[:, many(128 * (8 * p + l_), 128)], wqkv.at[own_rows, pl.ds(128 * p, 128)], dv))
    in_qkv = Batch(copies)
    copies = []
    for d in group:
        y_, w_, c_, l_, dv = peer(d)
        for r in range(4):
            copies.append((wup_in.at[:, many(128 * (16 * y_ + 8 * (r // 2) + 4 * (r % 2) + 2 * w_ + c_), 128)], wup.at[own_rows, pl.ds(128 * r, 128)], dv))
    in_up = Batch(copies)
    in_qkv.start()
    cot_send = cot

    @pl.when(off_diag == 0)
    def _():
        tok_all[my_rows, :] = tokens[...]

    pack_all[idx] = pack_in[...]
    for p in range(3):
        wqkv[own_rows, 128 * p : 128 * p + 128] = wqkv_in[:, many(128 * (8 * p + lane), 128)]

    swap_wait(tokens, tok_all.at[swap_rows], *tok_swap)
    tok = Gather(tok_all)
    tok.start()

    out_a, out_b = sems(4)
    place = 2 * w + c
    out_rows = many(32 * place, 32)
    home_dev = dev(y, x, k, x, k)
    send_out = rc(wout_in, wout.at[out_rows], out_a, out_b + place, home_dev)

    @pl.when(is_home == 0)
    def _():
        send_out.start()

    @pl.when(is_home == 1)
    def _():
        wout[out_rows, :] = wout_in[...]

    in_qkv.wait()

    def between(pieces):
        copies = []
        for d in ranks:
            x_, k_, r_, dv = partner(d)
            for ref in pieces:
                copies.append((ref, ref, dv))
        return Batch(copies)

    base = 16 * 0 + 8 * x + 4 * k
    pack_pieces = [pack_all.at[pl.ds(base + 16 * y_, 4)] for y_ in range(2)]
    qkv_pieces = [wqkv.at[many(512 * y_ + 256 * x + 128 * k, 128)] for y_ in range(2)]
    up_pieces = [wup.at[many(512 * y_ + 256 * x + 128 * k, 128)] for y_ in range(2)]
    rank_rows = many(128 * rank, 128)
    dp_qkv = between(pack_pieces + qkv_pieces)
    dp_qkv.start()
    in_up.start()
    for r in range(4):
        wup[own_rows, 128 * r : 128 * r + 128] = wup_in[:, many(128 * (16 * y + 8 * (r // 2) + 4 * (r % 2) + 2 * w + c), 128)]
    wdown[rank_rows, :] = wdown_in[...]

    dpo_a, dpo_b = sems(3)
    dp_out = [rc(wout, wout, dpo_a + n, dpo_b, partner(d)[3]) for n, d in enumerate(ranks)]

    @pl.when(is_home == 1)
    def _():
        for dw, dc in ((0, 1), (1, 0), (1, 1)):
            m = 2 * flip(w, dw) + flip(c, dc)
            rows = many(32 * m, 32)
            rc(wout_in, wout.at[rows], out_a, out_b + m, home_dev).wait_recv()
        for copy in dp_out:
            copy.start()

    tok.pass_on()
    swap_start(cot, cot_all.at[swap_rows], *cot_swap)

    @pl.when(off_diag == 0)
    def _():
        cot_all[my_rows, :] = cot[...]

    in_up.wait()
    dp_up = between(up_pieces)
    dp_up.start()
    dp_down = Batch([(wdown_in, wdown.at[rank_rows], partner(d)[3]) for d in ranks])
    dp_down.start()

    dp_qkv.wait()
    lane_id = lax.broadcasted_iota(jnp.int32, (16, 128), 1)
    for b in range(8):
        for t in range(4):
            block = None
            for m in range(4):
                piece = pack_all[4 * b + m].astype(F32)
                shift = (32 * (m - t)) % 128
                if shift:
                    piece = pltpu.roll(piece, shift, 1)
                block = piece if block is None else jnp.where(lane_id // 32 == m, piece, block)
            full[16 * t : 16 * t + 16, 128 * b : 128 * b + 128] = block

    gain0, gain1 = full[54:55, :], full[55:56, :]
    shift0, shift1 = full[56:57, :], full[57:58, :]
    lane_cols = many(128 * lane, 128)
    bias_q, bias_v = full[58:59, lane_cols], full[59:60, lane_cols]
    bias_out, bias_down = full[60:61, :], full[61:62, :]
    bias_up = jnp.concatenate(
        [pack_all[16 * y + 8 * (r // 2) + 4 * (r % 2) + 2 * w + c].astype(F32)[15:16, :] for r in range(4)], axis=1
    )
    facts = pack_all[8 * sample].astype(F32)[14:15, :]
    one_lane = lax.broadcasted_iota(jnp.int32, (1, 128), 1)
    present = jnp.where(one_lane < 64, facts, 0.0)
    hours = jnp.sum(jnp.where(one_lane == 64, facts, 0.0), axis=-1, keepdims=True) * hours_scale
    present8 = jnp.broadcast_to(present, (8, 128))[:, :64].astype(BF)
    extra = dot_nn(present8, full[...].astype(BF))[0:1, :] + hours * full[62:63, :]

    tok.finish()

    @pl.loop(0, 8)
    def _(n):
        rows = many(128 * n, 128)
        xhat, _ = center(tok_all[rows, :].astype(F32) + extra)
        normed[rows, :] = (xhat * gain0 + shift0).astype(BF)

    @pl.loop(0, 4)
    def _(n):
        rows = many(256 * n, 256)
        proj = dot_nn(normed[rows, :], wqkv[...])
        q_s[rows, :] = ((proj[:, :128] + bias_q) * 0.125).astype(BF)
        k_s[rows, :] = proj[:, 128:256].astype(BF)
        v_s[rows, :] = (proj[:, 256:384] + bias_v).astype(BF)

    QB = 256
    head_lane = lax.broadcasted_iota(jnp.int32, (1, 128), 1) // 64

    def of_head(v, h):
        return jnp.where(head_lane == h, v, jnp.zeros_like(v))

    @pl.loop(0, D // QB)
    def _(n):
        rows = many(QB * n, QB)
        queries = q_s[rows, :]
        total = None
        for h in range(2):
            scores = dot_nt(of_head(queries, h), k_s[...])
            top = jnp.max(scores, axis=-1, keepdims=True)
            e = jnp.exp(scores - top)
            share = (e * (1.0 / jnp.sum(e, axis=-1, keepdims=True))).astype(BF)
            shares[h, rows, :] = share
            got = of_head(dot_nn(share, v_s[...]), h)
            total = got if total is None else total + got
        attf[rows, :] = total
        att[rows, :] = total.astype(BF)

    @pl.when(is_home == 0)
    def _():
        rc(wout, wout, dpo_a, dpo_b, home_dev).wait_recv()

    def rows_of(l_):
        return many(ROWS * l_, ROWS)

    rs_out = Scatter(0, lambda l_: dot_nn(att[rows_of(l_), :], wout[...]))
    rs_out.start()

    swap_wait(cot, cot_all.at[swap_rows], *cot_swap)
    cg = Gather(cot_all)
    cg.start()

    stream = tok_all[my_rows, :].astype(F32) + extra
    mid = stream + (rs_out.finish() + bias_out)
    middle[...] = mid
    xhat2, rstd2 = center(mid)
    n2_all[my_rows, :] = (xhat2 * gain1 + shift1).astype(BF)
    n2 = Gather(n2_all)
    n2.start()
    cg.pass_on()
    n2.pass_on()
    dp_up.wait()
    dp_down.wait()
    cg.finish()
    n2.finish()

    upb_g[...] = jnp.zeros_like(upb_g)

    @pl.loop(0, 8)
    def _(n):
        rows = many(128 * n, 128)
        up = dot_nn(n2_all[rows, :], wup[...]) + bias_up
        cdf = 0.5 * (1.0 + erf(up * 0.7071067811865476))
        act[rows, :] = (up * cdf).astype(BF)
        slope = cdf + up * (jnp.exp(-0.5 * up * up) * 0.3989422804014327)
        low = (dot_nt(cot_all[rows, :], wdown[...]) * slope).astype(BF)
        uplow[rows, :] = low
        upb_g[0:1, :] += jnp.sum(low.astype(F32), axis=0, keepdims=True)

    rs_n2 = Scatter(1, lambda l_: dot_nt(uplow[rows_of(l_), :], wup[...]))
    rs_n2.start()
    rs_mix = Scatter(2, lambda l_: dot_nn(act[rows_of(l_), :], wdown[...]))
    rs_mix.start()

    n2_grad = rs_n2.finish()
    incoming = cot_all[my_rows, :].astype(F32)
    xhat2, rstd2 = center(middle[...])
    mg = incoming + norm_back(xhat2, rstd2, gain1, n2_grad)
    mgrad[...] = mg
    ml_all[my_rows, :] = mg.astype(BF)
    ml = Gather(ml_all)
    ml.start()
    smallp[2:3, :] = jnp.sum(n2_grad * xhat2, axis=0, keepdims=True)
    smallp[4:5, :] = jnp.sum(n2_grad, axis=0, keepdims=True)
    smallp[5:6, :] = jnp.sum(mg.astype(BF).astype(F32), axis=0, keepdims=True)
    smallp[6:7, :] = jnp.sum(incoming, axis=0, keepdims=True)

    @pl.loop(0, 4)
    def _(r):
        cols = many(128 * r, 128)
        gdown[cols, :] = dot_tn(act[:, cols], cot_all[...]).astype(BF)

    down_sends = Batch([(gdown.at[many(128 * partner(d)[2], 128)], rdown.at[n], partner(d)[3]) for n, d in enumerate(ranks)])
    down_sends.start()
    upb_sends_src = upb_g
    upb_sends = Batch([(upb_g.at[:, many(128 * partner(d)[2], 128)], r_upb.at[n], partner(d)[3]) for n, d in enumerate(ranks)])
    upb_sends.start()
    ml.pass_on()

    @pl.loop(0, 4)
    def _(n):
        cols = many(256 * n, 256)
        gup[cols, :] = dot_tn(n2_all[:, cols], uplow[...]).astype(BF)

    def spread(src, recv):
        copies = []
        for n, d in enumerate(ranks):
            x_, k_, r_, dv = partner(d)
            for y_ in range(2):
                copies.append((src.at[many(512 * y_ + 256 * x_ + 128 * k_, 128)], recv.at[n, pl.ds(128 * y_, 128)], dv))
        return Batch(copies)

    up_sends = spread(gup, rup)
    up_sends.start()
    ml.finish()

    @pl.loop(0, 4)
    def _(n):
        rows = many(256 * n, 256)
        dog[rows, :] = dot_nt(ml_all[rows, :], wout[...]).astype(BF)

    dk_acc[...] = jnp.zeros_like(dk_acc)
    dv_acc[...] = jnp.zeros_like(dv_acc)

    @pl.loop(0, D // QB)
    def _(n):
        rows = many(QB * n, QB)
        queries = q_s[rows, :]
        grads = dog[rows, :]
        both = grads.astype(F32) * attf[rows, :]
        dq = None
        for h in range(2):
            share = shares[h, rows, :]
            pressure = dot_nt(of_head(grads, h), v_s[...])
            offset = jnp.sum(of_head(both, h), axis=-1, keepdims=True)
            ds = (share.astype(F32) * (pressure - offset)).astype(BF)
            got = of_head(dot_nn(ds, k_s[...]), h)
            dq = got if dq is None else dq + got
            dk_acc[...] += dot_tn(ds, of_head(queries, h))
            dv_acc[...] += dot_tn(share, of_head(grads, h))
        dproj[rows, 0:128] = (dq.astype(BF).astype(F32) * 0.125).astype(BF)

    dproj[:, 128:256] = dk_acc[...].astype(BF)
    dproj[:, 256:384] = dv_acc[...].astype(BF)

    rs_n1 = Scatter(3, lambda l_: dot_nt(dproj[rows_of(l_), :], wqkv[...]))
    rs_n1.start()

    @pl.loop(0, 4)
    def _(n):
        cols = many(256 * n, 256)
        gqkv[cols, :] = dot_tn(normed[:, cols], dproj[...]).astype(BF)

    qkv_sends = spread(gqkv, rqkv)
    qkv_sends.start()

    n1_grad = rs_n1.finish()
    xhat1, rstd1 = center(tok_all[my_rows, :].astype(F32) + extra)
    tg = mgrad[...] + norm_back(xhat1, rstd1, gain0, n1_grad)
    tgs[...] = tg
    tg_swap = sems(1)
    tgs_b = tgr.at[0]
    tgr[0] = tg.astype(BF)
    swap_start(tgr.at[0], tgr.at[1], *tg_swap)
    smallp[0:1, :] = jnp.sum(tg, axis=0, keepdims=True)
    smallp[1:2, :] = jnp.sum(n1_grad * xhat1, axis=0, keepdims=True)
    smallp[3:4, :] = jnp.sum(n1_grad, axis=0, keepdims=True)
    smallp[7:8, :] = jnp.zeros((1, D), F32)

    gout[...] = dot_tn(att[...], ml_all[...]).astype(BF)
    go_a, go_b = sems(4)
    hx, hk = x + w - 2 * x * w, k + c - 2 * k * c
    apart = 2 * hx + hk
    send_home = rc(gout, rout.at[apart], go_a, go_b + apart, dev(y, w, c, w, c))

    @pl.when(is_home == 0)
    def _():
        send_home.start()

    small_group = Batch([(smallp.at[:, many(128 * peer(d)[3], 128)], r_a.at[n], peer(d)[4]) for n, d in enumerate(group)])
    small_group.start()

    mix_swap = sems(1)
    mixed_low = (middle[...] + (rs_mix.finish() + bias_down)).astype(BF)
    tgr[2] = mixed_low
    swap_start(tgr.at[2], tgr.at[3], *mix_swap)

    small_group.wait()
    total = smallp[:, lane_cols]
    for n in range(7):
        total = total + r_a[n]
    s_b[0:8, :] = total
    low = dproj[...].astype(F32)
    s_b[8:9, :] = jnp.sum(low[:, 0:128], axis=0, keepdims=True)
    s_b[9:10, :] = jnp.sum(low[:, 256:384], axis=0, keepdims=True)
    s_b[10:16, :] = jnp.zeros((6, 128), F32)
    small_ranks = Batch([(s_b, r_b.at[n], partner(d)[3]) for n, d in enumerate(ranks)])
    small_ranks.start()

    down_sends.wait()
    sum_down = gdown[rank_rows, :].astype(F32)
    for n in range(3):
        sum_down = sum_down + rdown[n].astype(F32)
    gd_o[...] = sum_down
    mine = [many(512 * y_ + 256 * x + 128 * k, 128) for y_ in range(2)]

    def collect(src, recv, low_sum):
        for y_ in range(2):
            part = src[mine[y_], :].astype(F32)
            for n in range(3):
                part = part + recv[n, 128 * y_ : 128 * y_ + 128, :].astype(F32)
            low_sum[128 * y_ : 128 * y_ + 128, :] = part.astype(BF)

    def deal(low_sum, recv):
        copies = []
        for n, d in enumerate(group):
            y_, w_, c_, l_, dv = peer(d)
            copies.append((low_sum.at[many(128 * y_ + 64 * w_ + 32 * c_, 32)], recv.at[lane], dv))
        return Batch(copies)

    my_deal = many(128 * y + 64 * w + 32 * c, 32)
    up_sends.wait()
    collect(gup, rup, su2)
    up_deal = deal(su2, ru2)
    up_deal.start()
    ru2[lane] = su2[my_deal, :]

    @pl.when(is_home == 1)
    def _():
        for n, d in enumerate(ranks):
            slot = 2 * d[0] + d[1]
            rc(gout, rout.at[slot], go_a, go_b + slot, partner(d)[3]).wait_recv()
        sum_out = gout[...].astype(F32)
        for slot in range(1, 4):
            sum_out = sum_out + rout[slot].astype(F32)
        so2[...] = sum_out.astype(BF)

    outs_a, outs_b = sems(3)
    home_copies = []
    for n, (dw, dc) in enumerate(((0, 1), (1, 0), (1, 1))):
        w_, c_ = flip(w, dw), flip(c, dc)
        home_copies.append(rc(so2.at[many(32 * (2 * w_ + c_), 32)], ro2, outs_a + n, outs_b, dev(y, x, k, w_, c_)))

    @pl.when(is_home == 1)
    def _():
        for copy in home_copies:
            copy.start()
        go_o[...] = so2[out_rows, :].astype(F32)

    qkv_sends.wait()
    collect(gqkv, rqkv, sq2)
    qkv_deal = deal(sq2, rq2)
    qkv_deal.start()
    rq2[lane] = sq2[my_deal, :]

    small_ranks.wait()
    blocks = [None] * 4
    rows_sum = s_b[...]
    for n in range(3):
        rows_sum = rows_sum + r_b[n]
    own_facts = [facts] + [pack_all[8 * (2 * partner(d)[1] + partner(d)[0])].astype(F32)[14:15, :] for d in ranks]
    own_sums = [s_b[0:1, :]] + [r_b[n, 0:1, :] for n in range(3)]
    facts8 = jnp.concatenate(own_facts + [jnp.zeros((4, 128), F32)], axis=0)
    facts_t = jnp.transpose(facts8)
    table = None
    for n in range(4):
        part = facts_t[:, n : n + 1] * own_sums[n]
        table = part if table is None else table + part
    s_a[0:64, :] = table[0:64, :]
    s_a[64:80, :] = rows_sum
    s_a[80:81, :] = table[64:65, :] * hours_scale
    s_a[81:88, :] = jnp.zeros((7, 128), F32)
    sm_a, sm_b = sems(3)
    small_copies = []
    for n, (dw, dc) in enumerate(((0, 1), (1, 0), (1, 1))):
        w_, c_ = flip(w, dw), flip(c, dc)
        small_copies.append(rc(s_a, r_c, sm_a + n, sm_b, dev(y, x, k, w_, c_)))

    @pl.when(is_home == 1)
    def _():
        for copy in small_copies:
            copy.start()
        small_o[0:88, :] = s_a[...]

    @pl.when(is_home == 0)
    def _():
        rc(s_a, r_c, sm_a, sm_b, home_dev).wait_recv()
        small_o[0:88, :] = r_c[...]

    upb_sends.wait()
    sum_upb = upb_g[:, rank_rows]
    for n in range(3):
        sum_upb = sum_upb + r_upb[n]
    small_o[88:96, :] = sum_upb

    @pl.when(is_home == 0)
    def _():
        rc(so2.at[pl.ds(0, 32)], ro2, outs_a, outs_b, home_dev).wait_recv()
        go_o[...] = ro2[...].astype(F32)

    @pl.when(off_diag == 0)
    def _():
        tg_o[...] = tgs[...]
        mixed_o[...] = tgr[2]

    swap_wait(tgr.at[2], tgr.at[3], *mix_swap)
    swap_wait(tgr.at[0], tgr.at[1], *tg_swap)

    @pl.when(off_diag == 1)
    def _():
        tg_o[...] = tgr[1].astype(F32)
        mixed_o[...] = tgr[3]

    up_deal.wait()
    for l_ in range(8):
        part = ru2[l_].astype(F32)
        y_, w_, c_ = l_ // 4, (l_ // 2) % 2, l_ % 2
        for r in range(4):
            at = 128 * (16 * y_ + 8 * (r // 2) + 4 * (r % 2) + 2 * w_ + c_)
            gu_o[:, at : at + 128] = part[:, 128 * r : 128 * r + 128]
    qkv_deal.wait()
    for l_ in range(8):
        part = rq2[l_].astype(F32)
        for p in range(3):
            at = 128 * (8 * p + l_)
            gq_o[:, at : at + 128] = part[:, 128 * p : 128 * p + 128]

    for item in (in_qkv, in_up, dp_qkv, dp_up, dp_down, tok, cg, n2, ml, rs_out, rs_n2, rs_mix, rs_n1,
                 down_sends, upb_sends, up_sends, qkv_sends, small_group, small_ranks, up_deal, qkv_deal):
        item.drain()

    @pl.when(is_home == 0)
    def _():
        send_out.wait_send()
        send_home.wait_send()

    @pl.when(is_home == 1)
    def _():
        for copy in dp_out + home_copies + small_copies:
            copy.wait_send()


def local_fast(
    tokens, lead_hours, var_mask, var_table, lead_weight, norm_gain, norm_shift, w_qkv, qv_bias, w_out,
    branch_bias, w_up, up_bias, w_down, cotangent,
):
    mask = var_mask.astype(BF)[0]
    zero = jnp.zeros((1, 2), BF)
    parts = [mask[14 * t : min(14 * t + 14, 48)] for t in range(4)]
    slots = jnp.concatenate([parts[0], zero[0], parts[1], zero[0], parts[2], zero[0], parts[3], jnp.zeros((10,), BF)])
    hours = jnp.concatenate([lead_hours.astype(BF), jnp.zeros((31,), BF)])
    ub = up_bias.reshape(4, 32)
    rows = jnp.concatenate(
        [
            var_table[0:14], slots[None, 0:32], ub[0:1],
            var_table[14:28], slots[None, 32:64], ub[1:2],
            var_table[28:42], hours[None], ub[2:3],
            var_table[42:48], norm_gain, norm_shift, qv_bias, branch_bias, lead_weight[None], ub[3:4],
        ],
        axis=0,
    )
    pack = rows.reshape(4, 16, 32).transpose(1, 0, 2).reshape(16, 128)

    vm = pltpu.VMEM
    scratch = [
        vm((D, D), BF), vm((D, D), BF), vm((D, D), BF), vm((D, D), BF),
        vm((D, 384), BF), vm((D, FFL), BF), vm((FFL, D), BF), vm((128, D), BF), vm((32, 16, 128), BF), vm((64, D), F32),
        vm((D, D), BF), vm((D, 128), BF), vm((D, 128), BF), vm((D, 128), BF), vm((2, D, D), BF), vm((D, 128), F32), vm((D, 128), BF),
        vm((4, 4, 128, D), BF), vm((4, 4, 128, D), BF), vm((4, 3, 128, D), BF), vm((4, 3, 128, D), BF), vm((4, 128, D), F32),
        vm((128, D), F32), vm((128, D), F32), vm((D, FFL), BF), vm((D, FFL), BF), vm((D, 384), BF), vm((D, 128), BF), vm((D, 128), F32), vm((D, 128), F32),
        vm((D, 384), BF), vm((D, FFL), BF), vm((FFL, D), BF), vm((128, D), BF),
        vm((3, 256, 384), BF), vm((3, 256, FFL), BF), vm((3, 128, D), BF), vm((4, 128, D), BF),
        vm((256, 384), BF), vm((256, FFL), BF), vm((8, 32, 384), BF), vm((8, 32, FFL), BF), vm((128, D), BF), vm((32, D), BF),
        vm((128, D), F32), vm((4, 128, D), BF), vm((8, D), F32), vm((88, 128), F32), vm((7, 8, 128), F32), vm((16, 128), F32), vm((3, 16, 128), F32), vm((88, 128), F32),
        vm((8, FFL), F32), vm((3, 8, 128), F32),
        pltpu.SemaphoreType.DMA((260,)), pltpu.SemaphoreType.DMA((260,)),
    ]
    outs = [
        jax.ShapeDtypeStruct((128, D), BF), jax.ShapeDtypeStruct((128, D), F32), jax.ShapeDtypeStruct((32, 3 * D), F32),
        jax.ShapeDtypeStruct((32, D), F32), jax.ShapeDtypeStruct((32, 4 * D), F32), jax.ShapeDtypeStruct((128, D), F32),
        jax.ShapeDtypeStruct((96, 128), F32),
    ]
    mixed, tg, gq, go, gu, gd, small = pl.pallas_call(
        fast_kernel,
        out_shape=outs,
        in_specs=[pl.BlockSpec(memory_space=vm)] * 7,
        out_specs=[pl.BlockSpec(memory_space=vm)] * 7,
        scratch_shapes=scratch,
        compiler_params=pltpu.CompilerParams(collective_id=0, has_side_effects=True, vmem_limit_bytes=62 * 2**20),
        cost_estimate=pl.CostEstimate(flops=14_000_000_000, bytes_accessed=4_000_000, transcendentals=6_000_000),
    )(tokens[0], cotangent[0], w_qkv, w_out, w_up, w_down, pack)
    place = lax.axis_index("seq") % 4
    mine = lax.dynamic_slice(small, (0, 32 * place), (88, 32))
    table = jnp.concatenate([mine[0:14], mine[16:30], mine[32:46], mine[48:54]], axis=0)
    tail = mine[64:80]
    return (
        mixed[None], tg[None], table, mine[80],
        tail[1:3], tail[3:5], gq, tail[8:10], go, tail[5:7], gu, small[88], gd,
    )


def solution(mesh):
    sizes = dict(mesh.shape)
    fast = sizes == {"samp": 4, "seq": 8}
    return jax.shard_map(
        local_fast if fast else local,
        mesh=mesh,
        in_specs=(
            P("samp", "seq", None),
            P("samp"),
            P("samp", None),
            P(None, ("samp", "seq")),
            P(("samp", "seq")),
            P(None, ("samp", "seq")),
            P(None, ("samp", "seq")),
            P(("samp", "seq"), None),
            P(None, ("samp", "seq")),
            P(("samp", "seq"), None),
            P(None, ("samp", "seq")),
            P(("samp", "seq"), None),
            P(("samp", "seq")),
            P(("samp", "seq"), None),
            P("samp", "seq", None),
        ),
        out_specs=(
            P("samp", "seq", None),
            P("samp", "seq", None),
            P(None, ("samp", "seq")),
            P(("samp", "seq")),
            P(None, ("samp", "seq")),
            P(None, ("samp", "seq")),
            P(("samp", "seq"), None),
            P(None, ("samp", "seq")),
            P(("samp", "seq"), None),
            P(None, ("samp", "seq")),
            P(("samp", "seq"), None),
            P(("samp", "seq")),
            P(("samp", "seq"), None),
        ),
        check_vma=False,
    )
```

```python
import jax
import jax.numpy as jnp
from jax import lax
from jax.experimental import pallas as pl
from jax.experimental.pallas import tpu as pltpu
from jax.sharding import PartitionSpec as P

HEADS = 16
HEAD_DIM = 64


epsilon = 1e-05
hours_scale = 1.0 / 168.0


def from_behind(block, axis, distance):
    devices = range(lax.axis_size(axis))
    route = [((i - distance) % len(devices), i) for i in devices]
    return lax.ppermute(block, axis, route)


def normalize(field, scaling, offsets):
    average = jnp.mean(field, axis=-1, keepdims=True)
    centred = field - average
    variance = jnp.mean(centred * centred, axis=-1, keepdims=True)
    return centred * lax.rsqrt(variance + epsilon) * scaling + offsets


def block_size(length):
    size_now = length
    while size_now > 512 and size_now % 2 == 0:
        size_now = size_now // 2
    return size_now


def over_blocks(advance, carried, segments):
    length = segments[0].shape[1]
    size_now = block_size(length)
    number = length // size_now
    stacked = tuple(
        (
            jnp.moveaxis(
                segment.reshape(segment.shape[0], number, size_now, segment.shape[2]), 1, 0
            )
            for segment in segments
        )
    )

    def visit(current, blocks):
        return (advance(current, blocks), None)

    carried, _ = lax.scan(visit, carried, stacked)
    return carried


def split_heads(matrix):
    return matrix.reshape(matrix.shape[0], matrix.shape[1], HEADS, HEAD_DIM)


def gelu_slope(upward):
    normal_cdf = 0.5 * (1.0 + lax.erf(upward * 0.7071067811865476))
    density = jnp.exp(-0.5 * upward * upward) * 0.3989422804014327
    return normal_cdf + upward * density


def pair_terms(query_heads, grad_heads, log_total, offset, key_heads, value_heads):
    scores = jnp.einsum(
        "sqhd,skhd->shqk", query_heads, key_heads, preferred_element_type=jnp.float32
    )
    shares = jnp.exp(scores - log_total[..., None])
    pressure = jnp.einsum(
        "sqhd,skhd->shqk", grad_heads, value_heads, preferred_element_type=jnp.float32
    )
    score_grad = (shares * (pressure - offset[..., None])).astype(jnp.bfloat16)
    query_part = jnp.einsum(
        "shqk,skhd->sqhd", score_grad, key_heads, preferred_element_type=jnp.float32
    )
    key_part = jnp.einsum(
        "shqk,sqhd->skhd", score_grad, query_heads, preferred_element_type=jnp.float32
    )
    value_part = jnp.einsum(
        "shqk,sqhd->skhd",
        shares.astype(jnp.bfloat16),
        grad_heads,
        preferred_element_type=jnp.float32,
    )
    return (query_part, key_part, value_part)


def local(
    tokens,
    lead_hours,
    var_mask,
    var_table,
    lead_weight,
    norm_gain,
    norm_shift,
    w_qkv,
    qv_bias,
    w_out,
    branch_bias,
    w_up,
    up_bias,
    w_down,
    cotangent,
):
    samples, patches, features = tokens.shape
    row_count = samples * patches
    factor = HEAD_DIM ** (-0.5)
    (
        table_full,
        lead_full,
        gain_all,
        shift_all,
        qkv_full,
        qv_all,
        out_full,
        bias_all,
        up_full,
        upb_full,
        down_full,
    ) = (
        lax.all_gather(var_table, ("samp", "seq"), axis=1, tiled=True),
        lax.all_gather(lead_weight, ("samp", "seq"), axis=0, tiled=True),
        lax.all_gather(norm_gain, ("samp", "seq"), axis=1, tiled=True),
        lax.all_gather(norm_shift, ("samp", "seq"), axis=1, tiled=True),
        lax.all_gather(w_qkv, ("samp", "seq"), axis=0, tiled=True),
        lax.all_gather(qv_bias, ("samp", "seq"), axis=1, tiled=True),
        lax.all_gather(w_out, ("samp", "seq"), axis=0, tiled=True),
        lax.all_gather(branch_bias, ("samp", "seq"), axis=1, tiled=True),
        lax.all_gather(w_up, ("samp", "seq"), axis=0, tiled=True),
        lax.all_gather(up_bias, ("samp", "seq"), axis=0, tiled=True),
        lax.all_gather(w_down, ("samp", "seq"), axis=0, tiled=True),
    )
    gain_full = gain_all.astype(jnp.float32)
    shift_full = shift_all.astype(jnp.float32)
    qv_full = qv_all.astype(jnp.float32)
    bias_full = bias_all.astype(jnp.float32)
    lead_value = lead_hours.astype(jnp.float32) * hours_scale
    present = var_mask.astype(jnp.float32)
    variable_sum = jnp.dot(present, table_full.astype(jnp.float32), precision=lax.Precision.HIGHEST)
    stream = (
        tokens.astype(jnp.float32)
        + lead_value[:, None, None] * lead_full.astype(jnp.float32)
        + variable_sum[:, None, :]
    )
    stream_rows = stream.reshape(row_count, features)
    normed = normalize(stream_rows, gain_full[0], shift_full[0]).astype(jnp.bfloat16)
    projected = jnp.dot(normed, qkv_full, preferred_element_type=jnp.float32)
    queries = (
        ((projected[:, :features] + qv_full[0]) * factor)
        .astype(jnp.bfloat16)
        .reshape(samples, patches, features)
    )
    keys_all = (
        projected[:, features : 2 * features]
        .astype(jnp.bfloat16)
        .reshape(samples, patches, features)
    )
    values_all = (
        (projected[:, 2 * features :] + qv_full[1])
        .astype(jnp.bfloat16)
        .reshape(samples, patches, features)
    )
    query_heads = split_heads(queries)

    def scores_of(keys_block):
        return jnp.einsum(
            "sqhd,skhd->shqk",
            query_heads,
            split_heads(keys_block),
            preferred_element_type=jnp.float32,
        )

    def stats_step(carried, blocks):
        running_max, running_sum = carried
        scores = scores_of(blocks[0])
        new_max = jnp.maximum(running_max, jnp.max(scores, axis=-1))
        running_sum = running_sum * jnp.exp(running_max - new_max) + jnp.sum(
            jnp.exp(scores - new_max[..., None]), axis=-1
        )
        return (new_max, running_sum)

    stats_start = (
        jnp.full((samples, HEADS, patches), -jnp.inf, jnp.float32),
        jnp.zeros((samples, HEADS, patches), jnp.float32),
    )
    running_max, running_sum = over_blocks(
        stats_step, stats_start, (lax.all_gather(keys_all, "seq", axis=1, tiled=True),)
    )
    log_total = running_max + jnp.log(running_sum)

    def mix_step(collected, blocks):
        shares = jnp.exp(scores_of(blocks[0]) - log_total[..., None]).astype(jnp.bfloat16)
        return collected + jnp.einsum(
            "shqk,skhd->sqhd", shares, split_heads(blocks[1]), preferred_element_type=jnp.float32
        )

    zero_heads = jnp.zeros((samples, patches, HEADS, HEAD_DIM), jnp.float32)
    attended_f = over_blocks(
        mix_step,
        zero_heads,
        (
            lax.all_gather(keys_all, "seq", axis=1, tiled=True),
            lax.all_gather(values_all, "seq", axis=1, tiled=True),
        ),
    )
    attended = attended_f.reshape(row_count, features).astype(jnp.bfloat16)
    middle = stream_rows + (
        jnp.dot(attended, out_full, preferred_element_type=jnp.float32) + bias_full[0]
    )
    normed_two = normalize(middle, gain_full[1], shift_full[1]).astype(jnp.bfloat16)
    upward = jnp.dot(normed_two, up_full, preferred_element_type=jnp.float32) + upb_full.astype(
        jnp.float32
    )
    activated = jax.nn.gelu(upward, approximate=False).astype(jnp.bfloat16)
    downward = jnp.dot(activated, down_full, preferred_element_type=jnp.float32) + bias_full[1]
    mixed = (middle + downward).astype(jnp.bfloat16).reshape(samples, patches, features)
    gain_back, qkv_back, out_back, up_back, down_back = (
        lax.all_gather(norm_gain, ("samp", "seq"), axis=1, tiled=True),
        lax.all_gather(w_qkv, ("samp", "seq"), axis=0, tiled=True),
        lax.all_gather(w_out, ("samp", "seq"), axis=0, tiled=True),
        lax.all_gather(w_up, ("samp", "seq"), axis=0, tiled=True),
        lax.all_gather(w_down, ("samp", "seq"), axis=0, tiled=True),
    )
    gain_back = gain_back.astype(jnp.float32)
    incoming = cotangent.astype(jnp.float32).reshape(row_count, features)
    incoming_low = incoming.astype(jnp.bfloat16)
    down_grad = jnp.einsum("tf,td->fd", activated, incoming_low, preferred_element_type=jnp.float32)
    down_bias_grad = jnp.sum(incoming_low.astype(jnp.float32), axis=0)
    gelu_grad = jnp.einsum(
        "td,fd->tf", incoming_low, down_back, preferred_element_type=jnp.float32
    ) * gelu_slope(upward)
    up_low = gelu_grad.astype(jnp.bfloat16)
    up_grad = jnp.einsum("td,tf->df", normed_two, up_low, preferred_element_type=jnp.float32)
    up_bias_grad = jnp.sum(up_low.astype(jnp.float32), axis=0)
    normed_two_grad = jnp.einsum("tf,df->td", up_low, up_back, preferred_element_type=jnp.float32)
    _, pull_second = jax.vjp(normalize, middle, gain_back[1], shift_full[1])
    middle_part, gain_two_grad, shift_two_grad = pull_second(normed_two_grad)
    middle_grad = incoming + middle_part
    middle_low = middle_grad.astype(jnp.bfloat16)
    out_grad = jnp.einsum("te,td->ed", attended, middle_low, preferred_element_type=jnp.float32)
    out_bias_grad = jnp.sum(middle_low.astype(jnp.float32), axis=0)
    attended_grad = jnp.einsum(
        "td,ed->te", middle_low, out_back, preferred_element_type=jnp.float32
    ).astype(jnp.bfloat16)
    grad_rows = attended_grad.reshape(samples, patches, features)
    grad_heads = split_heads(grad_rows)
    offset = jnp.transpose(jnp.sum(grad_heads.astype(jnp.float32) * attended_f, axis=-1), (0, 2, 1))
    grads_start = jnp.zeros((2, samples, patches, HEADS, HEAD_DIM), jnp.float32)

    def visit_block(blocks, partial_grads, query_acc):
        query_part, key_part, value_part = pair_terms(
            query_heads,
            grad_heads,
            log_total,
            offset,
            split_heads(blocks[0]),
            split_heads(blocks[1]),
        )
        return (partial_grads + jnp.stack([key_part, value_part]), query_acc + query_part)

    def turn_grads(partial_grads):
        return from_behind(partial_grads.astype(jnp.bfloat16), "seq", 1).astype(partial_grads.dtype)

    def cycle_step(counter, carried):
        blocks, partial_grads, query_acc = carried
        partial_grads, query_acc = visit_block(blocks, partial_grads, query_acc)
        partial_grads = turn_grads(partial_grads)
        blocks = from_behind(blocks, "seq", 1)
        return (blocks, partial_grads, query_acc)

    blocks_start = jnp.stack([keys_all, values_all])
    blocks, partial_grads, query_acc = lax.fori_loop(
        0, lax.axis_size("seq") - 1, cycle_step, (blocks_start, grads_start, zero_heads)
    )
    partial_grads, query_acc = visit_block(blocks, partial_grads, query_acc)
    partial_grads = turn_grads(partial_grads)
    query_low = query_acc.astype(jnp.bfloat16).reshape(row_count, features) * factor
    key_low = partial_grads[0].astype(jnp.bfloat16).reshape(row_count, features)
    value_low = partial_grads[1].astype(jnp.bfloat16).reshape(row_count, features)
    proj_grad = jnp.concatenate([query_low, key_low, value_low], axis=1)
    qkv_grad = jnp.einsum("td,te->de", normed, proj_grad, preferred_element_type=jnp.float32)
    qv_bias_grad = jnp.stack(
        [
            jnp.sum(query_low.astype(jnp.float32), axis=0),
            jnp.sum(value_low.astype(jnp.float32), axis=0),
        ]
    )
    normed_grad = jnp.einsum("te,de->td", proj_grad, qkv_back, preferred_element_type=jnp.float32)
    _, pull_first = jax.vjp(normalize, stream_rows, gain_back[0], shift_full[0])
    stream_part, gain_one_grad, shift_one_grad = pull_first(normed_grad)
    stream_grad = (middle_grad + stream_part).reshape(samples, patches, features)
    per_sample = jnp.sum(stream_grad, axis=1)
    lead_grad = jnp.sum(lead_value[:, None] * per_sample, axis=0)
    table_grad = jnp.dot(present.T, per_sample, precision=lax.Precision.HIGHEST)
    gain_grad = jnp.stack([gain_one_grad, gain_two_grad])
    shift_grad = jnp.stack([shift_one_grad, shift_two_grad])
    bias_grad = jnp.stack([out_bias_grad, down_bias_grad])
    owned = (
        lax.psum_scatter(table_grad, ("samp", "seq"), scatter_dimension=1, tiled=True),
        lax.psum_scatter(lead_grad, ("samp", "seq"), scatter_dimension=0, tiled=True),
        lax.psum_scatter(gain_grad, ("samp", "seq"), scatter_dimension=1, tiled=True),
        lax.psum_scatter(shift_grad, ("samp", "seq"), scatter_dimension=1, tiled=True),
        lax.psum_scatter(qkv_grad, ("samp", "seq"), scatter_dimension=0, tiled=True),
        lax.psum_scatter(qv_bias_grad, ("samp", "seq"), scatter_dimension=1, tiled=True),
        lax.psum_scatter(out_grad, ("samp", "seq"), scatter_dimension=0, tiled=True),
        lax.psum_scatter(bias_grad, ("samp", "seq"), scatter_dimension=1, tiled=True),
        lax.psum_scatter(up_grad, ("samp", "seq"), scatter_dimension=0, tiled=True),
        lax.psum_scatter(up_bias_grad, ("samp", "seq"), scatter_dimension=0, tiled=True),
        lax.psum_scatter(down_grad, ("samp", "seq"), scatter_dimension=0, tiled=True),
    )
    return (
        mixed,
        stream_grad,
        owned[0],
        owned[1],
        owned[2],
        owned[3],
        owned[4],
        owned[5],
        owned[6],
        owned[7],
        owned[8],
        owned[9],
        owned[10],
    )


MESH = pl.DeviceIdType.MESH
BF = jnp.bfloat16
F32 = jnp.float32
D = 1024
ROWS = 128
LANES = 8
FFL = 512


def dot_nn(a, b):
    return lax.dot_general(a, b, (((1,), (0,)), ((), ())), preferred_element_type=F32)


def dot_nt(a, b):
    return lax.dot_general(a, b, (((1,), (1,)), ((), ())), preferred_element_type=F32)


def dot_tn(a, b):
    return lax.dot_general(a, b, (((0,), (0,)), ((), ())), preferred_element_type=F32)


def erf(v):
    v = jnp.clip(v, -4.0, 4.0)
    s = v * v
    p = jnp.full_like(s, -2.72614225801306e-10)
    for a in (2.77068142495902e-08, -2.10102402082508e-06, -5.69250639462346e-05,
              -7.34990630326855e-04, -2.95459980854025e-03, -1.60960333262415e-02):
        p = p * s + a
    q = jnp.full_like(s, -1.45660718464996e-05)
    for b in (-2.13374055278905e-04, -1.68282697438203e-03, -7.37332916720468e-03, -1.42647390514189e-02):
        q = q * s + b
    return v * p / q


def flip(a, d):
    return 1 - a if d else a


def many(n, m=1):
    return pl.ds(pl.multiple_of(n, m), m)


def center(v):
    mean = jnp.mean(v, axis=-1, keepdims=True)
    centred = v - mean
    var = jnp.mean(centred * centred, axis=-1, keepdims=True)
    rstd = lax.rsqrt(var + epsilon)
    return centred * rstd, rstd


def norm_back(xhat, rstd, gain, grad):
    dx = grad * gain
    return rstd * (dx - jnp.mean(dx, axis=-1, keepdims=True) - xhat * jnp.mean(dx * xhat, axis=-1, keepdims=True))


def fast_kernel(
    tokens, lead_hours, var_mask, var_table, lead_weight, norm_gain, norm_shift, wqkv_in, qv_bias, wout_in,
    branch_bias, wup_in, up_bias, wdown_in, cot,
    mixed_o, tg_o, gq_o, go_o, gu_o, gd_o, small_o,
    tok_all, cot_all, n2_all, ml_all,
    wqkv, wup, wdown, wout, raw, pack_in, pack_all, full,
    normed, q_s, k_s, v_s, shares, attf, att,
    rs_s1, rs_r1, rs_s2, rs_r2, own,
    middle, mgrad, act, uplow, dproj, dog, dk_acc, dv_acc,
    gqkv, gup, gdown, gout, xqkv, xup, xdown, zqkv_s, zup_s, zdown_s, zqkv, zup, zdown,
    out_x, out_s, out_z, sq2, su2, rq2, ru2, so2, ro2,
    tgr, smallp, s_a, r_a, s_b, r_b, r_c, upb_g, r_upb,
    ss, rs,
):
    s_i = lax.axis_index("samp")
    q_i = lax.axis_index("seq")
    y, x = s_i // 2, s_i % 2
    z, c = q_i // 2, q_i % 2
    k, w = z // 2, z % 2
    idx = 16 * y + 8 * x + 4 * k + 2 * w + c
    lane = 4 * y + 2 * w + c
    rank = 2 * x + k
    sample = 2 * k + x
    off_diag = y + k - 2 * y * k
    is_home = 1 - (x + w - 2 * x * w) - (k + c - 2 * k * c) + (x + w - 2 * x * w) * (k + c - 2 * k * c)
    my_rows = many(ROWS * lane, ROWS)

    def dev(y_, x_, k_, w_, c_):
        return (2 * y_ + x_, 4 * k_ + 2 * w_ + c_)

    count = [0, 0]
    items = []

    def sems(n):
        a, b = count
        count[0] += n
        count[1] += n
        return a, b

    def rc(src, dst, a, b, device):
        return pltpu.make_async_remote_copy(src_ref=src, dst_ref=dst, send_sem=ss.at[a], recv_sem=rs.at[b], device_id=device, device_id_type=MESH)

    group = [(d // 4, (d // 2) % 2, d % 2) for d in range(1, 8)]
    chips = [(0, 0), (0, 1), (1, 0), (1, 1)]
    ranks = [(0, 1), (1, 0), (1, 1)]

    def peer(d):
        dy, dw, dc = d
        y_, w_, c_ = flip(y, dy), flip(w, dw), flip(c, dc)
        return y_, w_, c_, 4 * y_ + 2 * w_ + c_, dev(y_, x, k, w_, c_)

    def partner(d):
        dx, dk = d
        x_, k_ = flip(x, dx), flip(k, dk)
        return x_, k_, 2 * x_ + k_, dev(y, x_, k_, w, c)

    swap_dev = dev(k, x, y, w, c)

    barrier = pltpu.get_barrier_semaphore()
    for d in group:
        pl.semaphore_signal(barrier, inc=1, device_id=peer(d)[4], device_id_type=MESH)
    for d in ranks:
        pl.semaphore_signal(barrier, inc=1, device_id=partner(d)[3], device_id_type=MESH)

    @pl.when(off_diag == 1)
    def _():
        pl.semaphore_signal(barrier, inc=1, device_id=swap_dev, device_id_type=MESH)

    pl.semaphore_wait(barrier, 10 + off_diag)

    def begun(item):
        items.append(item)
        item.got = False

    class Swap:
        def __init__(self, src, dst):
            self.copy = rc(src, dst, *sems(1), swap_dev)

        def start(self):
            begun(self)
            pl.when(off_diag == 1)(self.copy.start)

        def wait(self):
            self.got = True
            pl.when(off_diag == 1)(self.copy.wait_recv)

        def drain(self):
            pl.when(off_diag == 1)(self.copy.wait_send)

    class Only:
        def __init__(self, sends, outgoing, takes, incoming):
            self.sends, self.outgoing, self.takes, self.incoming = sends, outgoing, takes, incoming

        def each(self, flag, copies, name):
            @pl.when(flag == 1)
            def _():
                for copy in copies:
                    getattr(copy, name)()

        def start(self):
            begun(self)
            self.each(self.sends, self.outgoing, "start")

        def wait(self):
            self.got = True
            self.each(self.takes, self.incoming, "wait_recv")

        def drain(self):
            self.each(self.sends, self.outgoing, "wait_send")

    def finish_all():
        for item in items:
            if not item.got:
                item.wait()
        for item in items:
            item.drain()

    class Gather:
        def __init__(self, buf):
            self.buf = buf
            self.a, self.b = sems(8)

        def copy(self, i, forward):
            dy, dw = chips[i]
            if i == 0:
                return rc(self.buf.at[my_rows], self.buf.at[my_rows], self.a, self.b, peer((0, 0, 1))[4])
            y_, w_, c_, l_, dv = peer((dy, dw, 0))
            if forward:
                rows = many(ROWS * l_, ROWS)
                return rc(self.buf.at[rows], self.buf.at[rows], self.a + 4 + i, self.b + 4 + i, peer((0, 0, 1))[4])
            return rc(self.buf.at[my_rows], self.buf.at[my_rows], self.a + i, self.b + i, dv)

        def start(self):
            begun(self)
            self.passed = False
            for i in (3, 1, 2, 0):
                self.copy(i, False).start()

        def pass_on(self):
            self.passed = True
            for i in (1, 2, 3):
                self.copy(i, False).wait_recv()
                self.copy(i, True).start()

        def wait(self):
            if not self.passed:
                self.pass_on()
            self.got = True
            self.copy(0, False).wait_recv()
            for i in (1, 2, 3):
                self.copy(i, True).wait_recv()

        def drain(self):
            for i in range(4):
                self.copy(i, False).wait_send()
            for i in (1, 2, 3):
                self.copy(i, True).wait_send()

    class Scatter:
        def __init__(self, slot, partial):
            self.slot = slot
            self.partial = partial
            self.a1, self.b1 = sems(4)
            self.a2, self.b2 = sems(4)

        def far(self, i):
            dy, dw = i // 2, i % 2
            y_, w_ = y + dy - 2 * y * dy, w + dw - 2 * w * dw
            return y_, w_

        def first(self, i):
            return rc(rs_s1.at[self.slot, i], rs_r1.at[self.slot, i], self.a1 + i, self.b1 + i, dev(y, x, k, w, 1 - c))

        def second(self, i):
            y_, w_ = self.far(i)
            return rc(rs_s2.at[self.slot, i - 1], rs_r2.at[self.slot, i - 1], self.a2 + i, self.b2 + i, dev(y_, x, k, w_, c))

        def start(self):
            begun(self)

            @pl.loop(0, 4)
            def _(n):
                i = 3 - n
                y_, w_ = self.far(i)
                rs_s1[self.slot, i] = self.partial(4 * y_ + 2 * w_ + 1 - c).astype(BF)
                self.first(i).start()

            @pl.loop(0, 4)
            def _(n):
                i = 3 - n
                y_, w_ = self.far(i)
                part = self.partial(4 * y_ + 2 * w_ + c)
                self.first(i).wait_recv()
                total = part + rs_r1[self.slot, i].astype(F32)

                @pl.when(i > 0)
                def _():
                    rs_s2[self.slot, i - 1] = total.astype(BF)
                    self.second(i).start()

                @pl.when(i == 0)
                def _():
                    own[self.slot] = total

        def wait(self):
            self.got = True
            for i in (1, 2, 3):
                self.second(i).wait_recv()
            total = own[self.slot]
            for i in (1, 2, 3):
                total = total + rs_r2[self.slot, i - 1].astype(F32)
            return total

        def drain(self):
            for i in range(4):
                self.first(i).wait_send()
            for i in (1, 2, 3):
                self.second(i).wait_send()

    class Batch:
        def __init__(self, copies):
            self.copies = copies
            self.a, self.b = sems(len(copies))

        def copy(self, n):
            src, dst, device = self.copies[n]
            return rc(src, dst, self.a + n, self.b + n, device)

        def start(self):
            begun(self)
            for n in range(len(self.copies)):
                self.copy(n).start()

        def wait(self):
            self.got = True
            for n in range(len(self.copies)):
                self.copy(n).wait_recv()

        def drain(self):
            for n in range(len(self.copies)):
                self.copy(n).wait_send()

    hx, hk = x + w - 2 * x * w, k + c - 2 * k * c
    z_dev, x_dev = partner((0, 1))[3], partner((1, 0))[3]

    class Across:
        def __init__(self, views):
            self.views = views
            self.n = len(views(x, k))
            self.a, self.b = sems(3 * self.n)

        def copies(self, leg):
            refs = self.views(x, 1 - k) if leg == 2 else self.views(x, k)
            at = self.n * leg
            return [rc(v, v, self.a + at + i, self.b + at + i, z_dev if leg == 0 else x_dev) for i, v in enumerate(refs)]

        def arrivals(self, leg):
            refs = self.views(*((x, 1 - k), (1 - x, k), (1 - x, 1 - k))[leg])
            at = self.n * leg
            return [rc(v, v, self.a + at + i, self.b + at + i, z_dev if leg == 0 else x_dev) for i, v in enumerate(refs)]

        def start(self):
            begun(self)
            self.passed = False
            for leg in (0, 1):
                for copy in self.copies(leg):
                    copy.start()

        def pass_on(self):
            self.passed = True
            for copy in self.arrivals(0):
                copy.wait_recv()
            for copy in self.copies(2):
                copy.start()

        def wait(self):
            if not self.passed:
                self.pass_on()
            self.got = True
            for leg in (1, 2):
                for copy in self.arrivals(leg):
                    copy.wait_recv()

        def drain(self):
            for leg in range(3):
                for copy in self.copies(leg):
                    copy.wait_send()

    class Reduce:
        def __init__(self, grad, rx, sz, rz):
            self.grad, self.rx, self.sz, self.rz = grad, rx, sz, rz
            self.runs = rx.shape[0]
            self.a, self.b = sems(self.runs + 1)

        def run(self, n):
            return rc(self.grad.at[many(512 * n + 256 * (1 - x), 256)], self.rx.at[n], self.a + n, self.b + n, x_dev)

        def last(self):
            return rc(self.sz, self.rz, self.a + self.runs, self.b + self.runs, z_dev)

        def start(self):
            begun(self)
            self.passed = False
            for n in range(self.runs):
                self.run(n).start()

        def part(self, n, k_):
            return (
                self.grad[many(512 * n + 256 * x + 128 * k_, 128), :].astype(F32)
                + self.rx[n, many(128 * k_, 128), :].astype(F32)
            )

        def pass_on(self):
            self.passed = True
            for n in range(self.runs):
                self.run(n).wait_recv()
            for n in range(self.runs):
                self.sz[n] = self.part(n, 1 - k).astype(BF)
            self.last().start()

        def wait(self):
            if not self.passed:
                self.pass_on()
            self.got = True
            self.last().wait_recv()

        def total(self, n):
            return self.part(n, k) + self.rz[n].astype(F32)

        def drain(self):
            for n in range(self.runs):
                self.run(n).wait_send()
            self.last().wait_send()

    swap_rows = many(ROWS * (4 * k + 2 * w + c), ROWS)
    tok_swap = Swap(tokens, tok_all.at[swap_rows])
    cot_swap = Swap(cot, cot_all.at[swap_rows])
    tok_swap.start()
    raw[...] = jnp.zeros_like(raw)
    raw[0:48, 0:32] = var_table[...].astype(F32)
    for n, rows in ((48, norm_gain), (50, norm_shift), (52, qv_bias), (54, branch_bias)):
        raw[n : n + 2, 0:32] = rows[...].astype(F32)
    raw[56:57, 0:32] = lead_weight[...].astype(F32)
    raw[64:65, :] = up_bias[...].astype(F32)
    raw[65:66, 0:48] = var_mask[...].astype(F32)
    raw[65:66, 64:65] = lead_hours[...].astype(F32)
    packed = raw[0:16, :]
    for t in range(1, 4):
        packed = packed + pltpu.roll(raw[16 * t : 16 * t + 16, :], 32 * t, 1)
    pack_in[0:16, :] = packed.astype(BF)
    pack_in[16:32, :] = raw[64:80, :].astype(BF)

    own_rows = many(32 * idx, 32)
    copies = []
    for d in group:
        y_, w_, c_, l_, dv = peer(d)
        copies.append((pack_in, pack_all.at[idx], dv))
        for p in range(3):
            copies.append((wqkv_in.at[:, many(128 * (8 * p + l_), 128)], wqkv.at[own_rows, pl.ds(128 * p, 128)], dv))
    in_qkv = Batch(copies)
    copies = []
    for d in group:
        y_, w_, c_, l_, dv = peer(d)
        for r in range(4):
            copies.append((wup_in.at[:, many(128 * (16 * y_ + 8 * (r // 2) + 4 * (r % 2) + 2 * w_ + c_), 128)], wup.at[own_rows, pl.ds(128 * r, 128)], dv))
    in_up = Batch(copies)
    in_qkv.start()

    @pl.when(off_diag == 0)
    def _():
        tok_all[my_rows, :] = tokens[...]

    pack_all[idx] = pack_in[...]
    for p in range(3):
        wqkv[own_rows, 128 * p : 128 * p + 128] = wqkv_in[:, many(128 * (8 * p + lane), 128)]

    tok_swap.wait()
    tok = Gather(tok_all)
    tok.start()

    out_a, out_b = sems(4)
    place = 2 * w + c
    out_rows = many(32 * place, 32)
    home_dev = dev(y, x, k, x, k)
    pairs = ((0, 1), (1, 0), (1, 1))
    away = 1 - is_home
    out_in = []
    for dw, dc in pairs:
        m = 2 * flip(w, dw) + flip(c, dc)
        out_in.append(rc(wout_in, wout.at[many(32 * m, 32)], out_a, out_b + m, home_dev))
    to_home = Only(away, [rc(wout_in, wout.at[out_rows], out_a, out_b + place, home_dev)], is_home, out_in)
    to_home.start()

    @pl.when(is_home == 1)
    def _():
        wout[out_rows, :] = wout_in[...]

    in_qkv.wait()

    def runs_of(ref, *more):
        def views(x_, k_):
            refs = [more[0].at[pl.ds(16 * y_ + 8 * x_ + 4 * k_, 4)] for y_ in range(2)] if more else []
            return refs + [ref.at[many(512 * y_ + 256 * x_ + 128 * k_, 128)] for y_ in range(2)]

        return views

    rank_rows = many(128 * rank, 128)
    dp_qkv = Across(runs_of(wqkv, pack_all))
    dp_up = Across(runs_of(wup))
    dp_down = Across(lambda x_, k_: [wdown.at[many(128 * (2 * x_ + k_), 128)]])
    dp_qkv.start()
    cot_swap.start()
    in_up.start()
    for r in range(4):
        wup[own_rows, 128 * r : 128 * r + 128] = wup_in[:, many(128 * (16 * y + 8 * (r // 2) + 4 * (r % 2) + 2 * w + c), 128)]
    wdown[rank_rows, :] = wdown_in[...]

    @pl.when(off_diag == 0)
    def _():
        cot_all[my_rows, :] = cot[...]

    dpo_a, dpo_b = sems(2)
    out_z_copy = rc(wout, wout, dpo_a, dpo_b, z_dev)
    out_x_copy = rc(wout, wout, dpo_a + 1, dpo_b + 1, x_dev)
    dp_out = Only(is_home, [out_z_copy, out_x_copy], (1 - hx) * hk, [out_z_copy])
    dp_out_more = Only((1 - hx) * hk, [out_x_copy], hx, [out_x_copy])
    to_home.wait()
    dp_out.start()
    tok.pass_on()
    in_up.wait()
    dp_up.start()
    dp_qkv.pass_on()
    dp_out.wait()
    dp_out_more.start()
    dp_down.start()
    cot_swap.wait()
    cg = Gather(cot_all)
    cg.start()

    dp_qkv.wait()
    lane_id = lax.broadcasted_iota(jnp.int32, (16, 128), 1)
    for b in range(8):
        for t in range(4):
            block = None
            for m in range(4):
                piece = pack_all[4 * b + m].astype(F32)[0:16, :]
                shift = (32 * (m - t)) % 128
                if shift:
                    piece = pltpu.roll(piece, shift, 1)
                block = piece if block is None else jnp.where(lane_id // 32 == m, piece, block)
            full[16 * t : 16 * t + 16, 128 * b : 128 * b + 128] = block

    gain0, gain1 = full[48:49, :], full[49:50, :]
    shift0, shift1 = full[50:51, :], full[51:52, :]
    lane_cols = many(128 * lane, 128)
    bias_q, bias_v = full[52:53, lane_cols], full[53:54, lane_cols]
    bias_out, bias_down = full[54:55, :], full[55:56, :]
    bias_up = jnp.concatenate(
        [pack_all[16 * y + 8 * (r // 2) + 4 * (r % 2) + 2 * w + c].astype(F32)[16:17, :] for r in range(4)], axis=1
    )
    facts = pack_all[8 * sample].astype(F32)[17:18, :]
    one_lane = lax.broadcasted_iota(jnp.int32, (1, 128), 1)
    present = jnp.where(one_lane < 64, facts, 0.0)
    hours = jnp.sum(jnp.where(one_lane == 64, facts, 0.0), axis=-1, keepdims=True) * hours_scale
    present8 = jnp.broadcast_to(present, (8, 128))[:, :64].astype(BF)
    extra = dot_nn(present8, full[...].astype(BF))[0:1, :] + hours * full[56:57, :]

    tok.wait()

    @pl.loop(0, 8)
    def _(n):
        rows = many(128 * n, 128)
        xhat, _ = center(tok_all[rows, :].astype(F32) + extra)
        normed[rows, :] = (xhat * gain0 + shift0).astype(BF)

    @pl.loop(0, 4)
    def _(n):
        rows = many(256 * n, 256)
        proj = dot_nn(normed[rows, :], wqkv[...])
        q_s[rows, :] = ((proj[:, :128] + bias_q) * 0.125).astype(BF)
        k_s[rows, :] = proj[:, 128:256].astype(BF)
        v_s[rows, :] = (proj[:, 256:384] + bias_v).astype(BF)

    QB = 256
    head_lane = lax.broadcasted_iota(jnp.int32, (1, 128), 1) // 64

    def of_head(v, h):
        return jnp.where(head_lane == h, v, jnp.zeros_like(v))

    @pl.loop(0, D // QB)
    def _(n):
        rows = many(QB * n, QB)
        queries = q_s[rows, :]
        total = None
        for h in range(2):
            scores = dot_nt(of_head(queries, h), k_s[...])
            top = jnp.max(scores, axis=-1, keepdims=True)
            e = jnp.exp(scores - top)
            share = (e * (1.0 / jnp.sum(e, axis=-1, keepdims=True))).astype(BF)
            shares[h, rows, :] = share
            got = of_head(dot_nn(share, v_s[...]), h)
            total = got if total is None else total + got
        attf[rows, :] = total
        att[rows, :] = total.astype(BF)

    dp_out_more.wait()

    def rows_of(l_):
        return many(ROWS * l_, ROWS)

    cg.pass_on()
    rs_out = Scatter(0, lambda l_: dot_nn(att[rows_of(l_), :], wout[...]))
    rs_out.start()

    dp_up.pass_on()
    dp_down.pass_on()

    stream = tok_all[my_rows, :].astype(F32) + extra
    mid = stream + (rs_out.wait() + bias_out)
    middle[...] = mid
    xhat2, rstd2 = center(mid)
    n2_all[my_rows, :] = (xhat2 * gain1 + shift1).astype(BF)
    n2 = Gather(n2_all)
    n2.start()
    n2.pass_on()
    dp_up.wait()
    dp_down.wait()
    cg.wait()
    n2.wait()

    upb_g[...] = jnp.zeros_like(upb_g)

    @pl.loop(0, 8)
    def _(n):
        rows = many(128 * n, 128)
        up = dot_nn(n2_all[rows, :], wup[...]) + bias_up
        cdf = 0.5 * (1.0 + erf(up * 0.7071067811865476))
        act[rows, :] = (up * cdf).astype(BF)
        slope = cdf + up * (jnp.exp(-0.5 * up * up) * 0.3989422804014327)
        low = (dot_nt(cot_all[rows, :], wdown[...]) * slope).astype(BF)
        uplow[rows, :] = low
        upb_g[0:1, :] += jnp.sum(low.astype(F32), axis=0, keepdims=True)

    rs_n2 = Scatter(1, lambda l_: dot_nt(uplow[rows_of(l_), :], wup[...]))
    rs_n2.start()

    @pl.loop(0, 4)
    def _(r):
        cols = many(128 * r, 128)
        gdown[cols, :] = dot_tn(act[:, cols], cot_all[...]).astype(BF)

    down_red = Reduce(gdown, xdown, zdown_s, zdown)
    down_red.start()
    upb_sends = Batch([(upb_g.at[:, many(128 * partner(d)[2], 128)], r_upb.at[n], partner(d)[3]) for n, d in enumerate(ranks)])
    upb_sends.start()

    @pl.loop(0, 4)
    def _(n):
        cols = many(256 * n, 256)
        gup[cols, :] = dot_tn(n2_all[:, cols], uplow[...]).astype(BF)

    up_red = Reduce(gup, xup, zup_s, zup)
    up_red.start()

    n2_grad = rs_n2.wait()
    incoming = cot_all[my_rows, :].astype(F32)
    xhat2, rstd2 = center(middle[...])
    mg = incoming + norm_back(xhat2, rstd2, gain1, n2_grad)
    mgrad[...] = mg
    ml_all[my_rows, :] = mg.astype(BF)
    ml = Gather(ml_all)
    ml.start()
    smallp[2:3, :] = jnp.sum(n2_grad * xhat2, axis=0, keepdims=True)
    smallp[4:5, :] = jnp.sum(n2_grad, axis=0, keepdims=True)
    smallp[5:6, :] = jnp.sum(mg.astype(BF).astype(F32), axis=0, keepdims=True)
    smallp[6:7, :] = jnp.sum(incoming, axis=0, keepdims=True)

    down_red.pass_on()
    ml.pass_on()
    up_red.pass_on()
    ml.wait()
    rs_mix = Scatter(2, lambda l_: dot_nn(act[rows_of(l_), :], wdown[...]))
    rs_mix.start()

    @pl.loop(0, 4)
    def _(n):
        rows = many(256 * n, 256)
        dog[rows, :] = dot_nt(ml_all[rows, :], wout[...]).astype(BF)

    dk_acc[...] = jnp.zeros_like(dk_acc)
    dv_acc[...] = jnp.zeros_like(dv_acc)

    @pl.loop(0, D // QB)
    def _(n):
        rows = many(QB * n, QB)
        queries = q_s[rows, :]
        grads = dog[rows, :]
        both = grads.astype(F32) * attf[rows, :]
        dq = None
        for h in range(2):
            share = shares[h, rows, :]
            pressure = dot_nt(of_head(grads, h), v_s[...])
            offset = jnp.sum(of_head(both, h), axis=-1, keepdims=True)
            ds = (share.astype(F32) * (pressure - offset)).astype(BF)
            got = of_head(dot_nn(ds, k_s[...]), h)
            dq = got if dq is None else dq + got
            dk_acc[...] += dot_tn(ds, of_head(queries, h))
            dv_acc[...] += dot_tn(share, of_head(grads, h))
        dproj[rows, 0:128] = (dq.astype(BF).astype(F32) * 0.125).astype(BF)

    dproj[:, 128:256] = dk_acc[...].astype(BF)
    dproj[:, 256:384] = dv_acc[...].astype(BF)

    rs_n1 = Scatter(3, lambda l_: dot_nt(dproj[rows_of(l_), :], wqkv[...]))
    rs_n1.start()

    @pl.loop(0, 4)
    def _(n):
        cols = many(256 * n, 256)
        gqkv[cols, :] = dot_tn(normed[:, cols], dproj[...]).astype(BF)

    qkv_red = Reduce(gqkv, xqkv, zqkv_s, zqkv)
    qkv_red.start()
    gout[...] = dot_tn(att[...], ml_all[...]).astype(BF)
    go_a, go_b = sems(2)
    grad_x = Only(hx, [rc(gout, out_x, go_a, go_b, x_dev)], 1 - hx, [rc(gout, out_x, go_a, go_b, x_dev)])
    grad_z = Only((1 - hx) * hk, [rc(out_s, out_z, go_a + 1, go_b + 1, z_dev)], is_home, [rc(out_s, out_z, go_a + 1, go_b + 1, z_dev)])
    grad_x.start()
    mixed_low = (middle[...] + (rs_mix.wait() + bias_down)).astype(BF)
    tgr[2] = mixed_low
    mix_swap = Swap(tgr.at[2], tgr.at[3])
    mix_swap.start()
    qkv_red.pass_on()
    grad_x.wait()

    @pl.when(hx == 0)
    def _():
        out_s[...] = (gout[...].astype(F32) + out_x[...].astype(F32)).astype(BF)

    grad_z.start()

    n1_grad = rs_n1.wait()
    xhat1, rstd1 = center(tok_all[my_rows, :].astype(F32) + extra)
    tg = mgrad[...] + norm_back(xhat1, rstd1, gain0, n1_grad)
    tgr[0] = tg.astype(BF)
    tg_swap = Swap(tgr.at[0], tgr.at[1])
    tg_swap.start()
    smallp[0:1, :] = jnp.sum(tg, axis=0, keepdims=True)
    smallp[1:2, :] = jnp.sum(n1_grad * xhat1, axis=0, keepdims=True)
    smallp[3:4, :] = jnp.sum(n1_grad, axis=0, keepdims=True)
    smallp[7:8, :] = jnp.zeros((1, D), F32)

    small_group = Batch([(smallp.at[:, many(128 * peer(d)[3], 128)], r_a.at[n], peer(d)[4]) for n, d in enumerate(group)])
    small_group.start()

    small_group.wait()
    total = smallp[:, lane_cols]
    for n in range(7):
        total = total + r_a[n]
    s_b[0:8, :] = total
    low = dproj[...].astype(F32)
    s_b[8:9, :] = jnp.sum(low[:, 0:128], axis=0, keepdims=True)
    s_b[9:10, :] = jnp.sum(low[:, 256:384], axis=0, keepdims=True)
    s_b[10:16, :] = jnp.zeros((6, 128), F32)
    small_ranks = Batch([(s_b, r_b.at[n], partner(d)[3]) for n, d in enumerate(ranks)])
    small_ranks.start()

    down_red.wait()
    gd_o[...] = down_red.total(0).astype(BF)

    def deal(low_sum, recv):
        copies = []
        for n, d in enumerate(group):
            y_, w_, c_, l_, dv = peer(d)
            copies.append((low_sum.at[many(128 * y_ + 64 * w_ + 32 * c_, 32)], recv.at[lane], dv))
        return Batch(copies)

    def collect(red, low_sum, recv):
        red.wait()
        for y_ in range(2):
            low_sum[128 * y_ : 128 * y_ + 128, :] = red.total(y_).astype(BF)
        batch = deal(low_sum, recv)
        batch.start()
        recv[lane] = low_sum[many(128 * y + 64 * w + 32 * c, 32), :]
        return batch

    up_deal = collect(up_red, su2, ru2)
    grad_z.wait()

    @pl.when(is_home == 1)
    def _():
        so2[...] = (out_s[...].astype(F32) + out_z[...].astype(F32)).astype(BF)
        go_o[...] = so2[out_rows, :]

    outs_a, outs_b = sems(3)
    copies = []
    for n, (dw, dc) in enumerate(pairs):
        w_, c_ = flip(w, dw), flip(c, dc)
        copies.append(rc(so2.at[many(32 * (2 * w_ + c_), 32)], ro2, outs_a + n, outs_b, dev(y, x, k, w_, c_)))
    out_deal = Only(is_home, copies, away, [rc(so2.at[pl.ds(0, 32)], ro2, outs_a, outs_b, home_dev)])
    out_deal.start()
    qkv_deal = collect(qkv_red, sq2, rq2)

    small_ranks.wait()
    blocks = [None] * 4
    rows_sum = s_b[...]
    for n in range(3):
        rows_sum = rows_sum + r_b[n]
    own_facts = [facts] + [pack_all[8 * (2 * partner(d)[1] + partner(d)[0])].astype(F32)[17:18, :] for d in ranks]
    own_sums = [s_b[0:1, :]] + [r_b[n, 0:1, :] for n in range(3)]
    facts8 = jnp.concatenate(own_facts + [jnp.zeros((4, 128), F32)], axis=0)
    facts_t = jnp.transpose(facts8)
    table = None
    for n in range(4):
        part = facts_t[:, n : n + 1] * own_sums[n]
        table = part if table is None else table + part
    s_a[0:64, :] = table[0:64, :]
    s_a[64:80, :] = rows_sum
    s_a[80:81, :] = table[64:65, :] * hours_scale
    s_a[81:88, :] = jnp.zeros((7, 128), F32)
    sm_a, sm_b = sems(3)
    copies = []
    for n, (dw, dc) in enumerate(pairs):
        w_, c_ = flip(w, dw), flip(c, dc)
        copies.append(rc(s_a, r_c, sm_a + n, sm_b, dev(y, x, k, w_, c_)))
    small_deal = Only(is_home, copies, away, [rc(s_a, r_c, sm_a, sm_b, home_dev)])
    small_deal.start()
    small_deal.wait()

    @pl.when(is_home == 1)
    def _():
        small_o[0:88, :] = s_a[...]

    @pl.when(is_home == 0)
    def _():
        small_o[0:88, :] = r_c[...]

    upb_sends.wait()
    sum_upb = upb_g[:, rank_rows]
    for n in range(3):
        sum_upb = sum_upb + r_upb[n]
    small_o[88:96, :] = sum_upb

    out_deal.wait()

    @pl.when(is_home == 0)
    def _():
        go_o[...] = ro2[...]

    @pl.when(off_diag == 0)
    def _():
        tg_o[...] = tgr[0]
        mixed_o[...] = tgr[2]

    mix_swap.wait()
    tg_swap.wait()

    @pl.when(off_diag == 1)
    def _():
        tg_o[...] = tgr[1]
        mixed_o[...] = tgr[3]

    up_deal.wait()
    gu_o[...] = ru2[...]
    qkv_deal.wait()
    gq_o[...] = rq2[...]

    finish_all()


def finish_kernel(
    mixed_i, tg_i, gq_i, go_i, gu_i, gd_i, small_i,
    mixed_o, tg_o, table_o, lead_o, gain_o, shift_o, gq_o, qv_o, go_o, bias_o, gu_o, upb_o, gd_o,
):
    mixed_o[0] = mixed_i[...]
    tg_o[0] = tg_i[...].astype(F32)
    gd_o[...] = gd_i[...].astype(F32)
    go_o[...] = go_i[...].astype(F32)
    for l_ in range(8):
        part = gu_i[l_].astype(F32)
        y_, w_, c_ = l_ // 4, (l_ // 2) % 2, l_ % 2
        for r in range(4):
            at = 128 * (16 * y_ + 8 * (r // 2) + 4 * (r % 2) + 2 * w_ + c_)
            gu_o[:, at : at + 128] = part[:, 128 * r : 128 * r + 128]
        part = gq_i[l_].astype(F32)
        for p in range(3):
            at = 128 * (8 * p + l_)
            gq_o[:, at : at + 128] = part[:, 128 * p : 128 * p + 128]
    place = lax.rem(lax.axis_index("seq"), 4)
    small = small_i[0:88, :]
    mine = small
    for m in range(1, 4):
        mine = jnp.where(place == m, pltpu.roll(small, 128 - 32 * m, 1), mine)
    table_o[...] = mine[0:48, 0:32]
    gain_o[...] = mine[65:67, 0:32]
    shift_o[...] = mine[67:69, 0:32]
    bias_o[...] = mine[69:71, 0:32]
    qv_o[...] = mine[72:74, 0:32]
    lead_o[...] = mine[80:81, 0:32]
    upb_o[...] = small_i[88:89, :]


def local_fast(
    tokens, lead_hours, var_mask, var_table, lead_weight, norm_gain, norm_shift, w_qkv, qv_bias, w_out,
    branch_bias, w_up, up_bias, w_down, cotangent,
):
    vm = pltpu.VMEM
    scratch = [
        vm((D, D), BF), vm((D, D), BF), vm((D, D), BF), vm((D, D), BF),
        vm((D, 384), BF), vm((D, FFL), BF), vm((FFL, D), BF), vm((128, D), BF), vm((80, 128), F32), vm((32, 128), BF), vm((32, 32, 128), BF), vm((64, D), F32),
        vm((D, D), BF), vm((D, 128), BF), vm((D, 128), BF), vm((D, 128), BF), vm((2, D, D), BF), vm((D, 128), F32), vm((D, 128), BF),
        vm((4, 4, 128, D), BF), vm((4, 4, 128, D), BF), vm((4, 3, 128, D), BF), vm((4, 3, 128, D), BF), vm((4, 128, D), F32),
        vm((128, D), F32), vm((128, D), F32), vm((D, FFL), BF), vm((D, FFL), BF), vm((D, 384), BF), vm((D, 128), BF), vm((D, 128), F32), vm((D, 128), F32),
        vm((D, 384), BF), vm((D, FFL), BF), vm((FFL, D), BF), vm((128, D), BF),
        vm((2, 256, 384), BF), vm((2, 256, FFL), BF), vm((1, 256, D), BF),
        vm((2, 128, 384), BF), vm((2, 128, FFL), BF), vm((1, 128, D), BF),
        vm((2, 128, 384), BF), vm((2, 128, FFL), BF), vm((1, 128, D), BF),
        vm((128, D), BF), vm((128, D), BF), vm((128, D), BF),
        vm((256, 384), BF), vm((256, FFL), BF), vm((8, 32, 384), BF), vm((8, 32, FFL), BF), vm((128, D), BF), vm((32, D), BF),
        vm((4, 128, D), BF), vm((8, D), F32), vm((88, 128), F32), vm((7, 8, 128), F32), vm((16, 128), F32), vm((3, 16, 128), F32), vm((88, 128), F32),
        vm((8, FFL), F32), vm((3, 8, 128), F32),
        pltpu.SemaphoreType.DMA((260,)), pltpu.SemaphoreType.DMA((260,)),
    ]
    shape = jax.ShapeDtypeStruct
    raw = pl.pallas_call(
        fast_kernel,
        out_shape=[
            shape((128, D), BF), shape((128, D), BF), shape((8, 32, 384), BF), shape((32, D), BF), shape((8, 32, FFL), BF),
            shape((128, D), BF), shape((96, 128), F32),
        ],
        in_specs=[pl.BlockSpec(memory_space=vm)] * 15,
        out_specs=[pl.BlockSpec(memory_space=vm)] * 7,
        scratch_shapes=scratch,
        compiler_params=pltpu.CompilerParams(collective_id=0, has_side_effects=True, vmem_limit_bytes=62 * 2**20),
        cost_estimate=pl.CostEstimate(flops=14_000_000_000, bytes_accessed=4_000_000, transcendentals=6_000_000),
    )(
        tokens[0], lead_hours[None], var_mask, var_table, lead_weight[None], norm_gain, norm_shift, w_qkv, qv_bias, w_out,
        branch_bias, w_up, up_bias[None], w_down, cotangent[0],
    )
    out = pl.pallas_call(
        finish_kernel,
        out_shape=[
            shape((1, 128, D), BF), shape((1, 128, D), F32), shape((48, 32), F32), shape((1, 32), F32), shape((2, 32), F32),
            shape((2, 32), F32), shape((32, 3 * D), F32), shape((2, 32), F32), shape((32, D), F32), shape((2, 32), F32),
            shape((32, 4 * D), F32), shape((1, 128), F32), shape((128, D), F32),
        ],
        in_specs=[pl.BlockSpec(memory_space=vm)] * 7,
        out_specs=[pl.BlockSpec(memory_space=vm)] * 13,
        compiler_params=pltpu.CompilerParams(vmem_limit_bytes=32 * 2**20),
        cost_estimate=pl.CostEstimate(flops=1_000_000, bytes_accessed=4_000_000, transcendentals=0),
    )(*raw)
    mixed, tg, table, lead, gain, shift, gq, qv, go, bias, gu, upb, gd = out
    return (mixed, tg, table, lead[0], gain, shift, gq, qv, go, bias, gu, upb[0], gd)


def solution(mesh):
    sizes = dict(mesh.shape)
    fast = sizes == {"samp": 4, "seq": 8}
    return jax.shard_map(
        local_fast if fast else local,
        mesh=mesh,
        in_specs=(
            P("samp", "seq", None),
            P("samp"),
            P("samp", None),
            P(None, ("samp", "seq")),
            P(("samp", "seq")),
            P(None, ("samp", "seq")),
            P(None, ("samp", "seq")),
            P(("samp", "seq"), None),
            P(None, ("samp", "seq")),
            P(("samp", "seq"), None),
            P(None, ("samp", "seq")),
            P(("samp", "seq"), None),
            P(("samp", "seq")),
            P(("samp", "seq"), None),
            P("samp", "seq", None),
        ),
        out_specs=(
            P("samp", "seq", None),
            P("samp", "seq", None),
            P(None, ("samp", "seq")),
            P(("samp", "seq")),
            P(None, ("samp", "seq")),
            P(None, ("samp", "seq")),
            P(("samp", "seq"), None),
            P(None, ("samp", "seq")),
            P(("samp", "seq"), None),
            P(None, ("samp", "seq")),
            P(("samp", "seq"), None),
            P(("samp", "seq")),
            P(("samp", "seq"), None),
        ),
        check_vma=False,
    )
```

```python
import jax
import jax.numpy as jnp
from jax import lax
from jax.experimental import pallas as pl
from jax.experimental.pallas import tpu as pltpu
from jax.sharding import PartitionSpec as P

HEADS = 16
HEAD_DIM = 64


epsilon = 1e-05
hours_scale = 1.0 / 168.0


def from_behind(block, axis, distance):
    devices = range(lax.axis_size(axis))
    route = [((i - distance) % len(devices), i) for i in devices]
    return lax.ppermute(block, axis, route)


def normalize(field, scaling, offsets):
    average = jnp.mean(field, axis=-1, keepdims=True)
    centred = field - average
    variance = jnp.mean(centred * centred, axis=-1, keepdims=True)
    return centred * lax.rsqrt(variance + epsilon) * scaling + offsets


def block_size(length):
    size_now = length
    while size_now > 512 and size_now % 2 == 0:
        size_now = size_now // 2
    return size_now


def over_blocks(advance, carried, segments):
    length = segments[0].shape[1]
    size_now = block_size(length)
    number = length // size_now
    stacked = tuple(
        (
            jnp.moveaxis(
                segment.reshape(segment.shape[0], number, size_now, segment.shape[2]), 1, 0
            )
            for segment in segments
        )
    )

    def visit(current, blocks):
        return (advance(current, blocks), None)

    carried, _ = lax.scan(visit, carried, stacked)
    return carried


def split_heads(matrix):
    return matrix.reshape(matrix.shape[0], matrix.shape[1], HEADS, HEAD_DIM)


def gelu_slope(upward):
    normal_cdf = 0.5 * (1.0 + lax.erf(upward * 0.7071067811865476))
    density = jnp.exp(-0.5 * upward * upward) * 0.3989422804014327
    return normal_cdf + upward * density


def pair_terms(query_heads, grad_heads, log_total, offset, key_heads, value_heads):
    scores = jnp.einsum(
        "sqhd,skhd->shqk", query_heads, key_heads, preferred_element_type=jnp.float32
    )
    shares = jnp.exp(scores - log_total[..., None])
    pressure = jnp.einsum(
        "sqhd,skhd->shqk", grad_heads, value_heads, preferred_element_type=jnp.float32
    )
    score_grad = (shares * (pressure - offset[..., None])).astype(jnp.bfloat16)
    query_part = jnp.einsum(
        "shqk,skhd->sqhd", score_grad, key_heads, preferred_element_type=jnp.float32
    )
    key_part = jnp.einsum(
        "shqk,sqhd->skhd", score_grad, query_heads, preferred_element_type=jnp.float32
    )
    value_part = jnp.einsum(
        "shqk,sqhd->skhd",
        shares.astype(jnp.bfloat16),
        grad_heads,
        preferred_element_type=jnp.float32,
    )
    return (query_part, key_part, value_part)


def local(
    tokens,
    lead_hours,
    var_mask,
    var_table,
    lead_weight,
    norm_gain,
    norm_shift,
    w_qkv,
    qv_bias,
    w_out,
    branch_bias,
    w_up,
    up_bias,
    w_down,
    cotangent,
):
    samples, patches, features = tokens.shape
    row_count = samples * patches
    factor = HEAD_DIM ** (-0.5)
    (
        table_full,
        lead_full,
        gain_all,
        shift_all,
        qkv_full,
        qv_all,
        out_full,
        bias_all,
        up_full,
        upb_full,
        down_full,
    ) = (
        lax.all_gather(var_table, ("samp", "seq"), axis=1, tiled=True),
        lax.all_gather(lead_weight, ("samp", "seq"), axis=0, tiled=True),
        lax.all_gather(norm_gain, ("samp", "seq"), axis=1, tiled=True),
        lax.all_gather(norm_shift, ("samp", "seq"), axis=1, tiled=True),
        lax.all_gather(w_qkv, ("samp", "seq"), axis=0, tiled=True),
        lax.all_gather(qv_bias, ("samp", "seq"), axis=1, tiled=True),
        lax.all_gather(w_out, ("samp", "seq"), axis=0, tiled=True),
        lax.all_gather(branch_bias, ("samp", "seq"), axis=1, tiled=True),
        lax.all_gather(w_up, ("samp", "seq"), axis=0, tiled=True),
        lax.all_gather(up_bias, ("samp", "seq"), axis=0, tiled=True),
        lax.all_gather(w_down, ("samp", "seq"), axis=0, tiled=True),
    )
    gain_full = gain_all.astype(jnp.float32)
    shift_full = shift_all.astype(jnp.float32)
    qv_full = qv_all.astype(jnp.float32)
    bias_full = bias_all.astype(jnp.float32)
    lead_value = lead_hours.astype(jnp.float32) * hours_scale
    present = var_mask.astype(jnp.float32)
    variable_sum = jnp.dot(present, table_full.astype(jnp.float32), precision=lax.Precision.HIGHEST)
    stream = (
        tokens.astype(jnp.float32)
        + lead_value[:, None, None] * lead_full.astype(jnp.float32)
        + variable_sum[:, None, :]
    )
    stream_rows = stream.reshape(row_count, features)
    normed = normalize(stream_rows, gain_full[0], shift_full[0]).astype(jnp.bfloat16)
    projected = jnp.dot(normed, qkv_full, preferred_element_type=jnp.float32)
    queries = (
        ((projected[:, :features] + qv_full[0]) * factor)
        .astype(jnp.bfloat16)
        .reshape(samples, patches, features)
    )
    keys_all = (
        projected[:, features : 2 * features]
        .astype(jnp.bfloat16)
        .reshape(samples, patches, features)
    )
    values_all = (
        (projected[:, 2 * features :] + qv_full[1])
        .astype(jnp.bfloat16)
        .reshape(samples, patches, features)
    )
    query_heads = split_heads(queries)

    def scores_of(keys_block):
        return jnp.einsum(
            "sqhd,skhd->shqk",
            query_heads,
            split_heads(keys_block),
            preferred_element_type=jnp.float32,
        )

    def stats_step(carried, blocks):
        running_max, running_sum = carried
        scores = scores_of(blocks[0])
        new_max = jnp.maximum(running_max, jnp.max(scores, axis=-1))
        running_sum = running_sum * jnp.exp(running_max - new_max) + jnp.sum(
            jnp.exp(scores - new_max[..., None]), axis=-1
        )
        return (new_max, running_sum)

    stats_start = (
        jnp.full((samples, HEADS, patches), -jnp.inf, jnp.float32),
        jnp.zeros((samples, HEADS, patches), jnp.float32),
    )
    running_max, running_sum = over_blocks(
        stats_step, stats_start, (lax.all_gather(keys_all, "seq", axis=1, tiled=True),)
    )
    log_total = running_max + jnp.log(running_sum)

    def mix_step(collected, blocks):
        shares = jnp.exp(scores_of(blocks[0]) - log_total[..., None]).astype(jnp.bfloat16)
        return collected + jnp.einsum(
            "shqk,skhd->sqhd", shares, split_heads(blocks[1]), preferred_element_type=jnp.float32
        )

    zero_heads = jnp.zeros((samples, patches, HEADS, HEAD_DIM), jnp.float32)
    attended_f = over_blocks(
        mix_step,
        zero_heads,
        (
            lax.all_gather(keys_all, "seq", axis=1, tiled=True),
            lax.all_gather(values_all, "seq", axis=1, tiled=True),
        ),
    )
    attended = attended_f.reshape(row_count, features).astype(jnp.bfloat16)
    middle = stream_rows + (
        jnp.dot(attended, out_full, preferred_element_type=jnp.float32) + bias_full[0]
    )
    normed_two = normalize(middle, gain_full[1], shift_full[1]).astype(jnp.bfloat16)
    upward = jnp.dot(normed_two, up_full, preferred_element_type=jnp.float32) + upb_full.astype(
        jnp.float32
    )
    activated = jax.nn.gelu(upward, approximate=False).astype(jnp.bfloat16)
    downward = jnp.dot(activated, down_full, preferred_element_type=jnp.float32) + bias_full[1]
    mixed = (middle + downward).astype(jnp.bfloat16).reshape(samples, patches, features)
    gain_back, qkv_back, out_back, up_back, down_back = (
        lax.all_gather(norm_gain, ("samp", "seq"), axis=1, tiled=True),
        lax.all_gather(w_qkv, ("samp", "seq"), axis=0, tiled=True),
        lax.all_gather(w_out, ("samp", "seq"), axis=0, tiled=True),
        lax.all_gather(w_up, ("samp", "seq"), axis=0, tiled=True),
        lax.all_gather(w_down, ("samp", "seq"), axis=0, tiled=True),
    )
    gain_back = gain_back.astype(jnp.float32)
    incoming = cotangent.astype(jnp.float32).reshape(row_count, features)
    incoming_low = incoming.astype(jnp.bfloat16)
    down_grad = jnp.einsum("tf,td->fd", activated, incoming_low, preferred_element_type=jnp.float32)
    down_bias_grad = jnp.sum(incoming_low.astype(jnp.float32), axis=0)
    gelu_grad = jnp.einsum(
        "td,fd->tf", incoming_low, down_back, preferred_element_type=jnp.float32
    ) * gelu_slope(upward)
    up_low = gelu_grad.astype(jnp.bfloat16)
    up_grad = jnp.einsum("td,tf->df", normed_two, up_low, preferred_element_type=jnp.float32)
    up_bias_grad = jnp.sum(up_low.astype(jnp.float32), axis=0)
    normed_two_grad = jnp.einsum("tf,df->td", up_low, up_back, preferred_element_type=jnp.float32)
    _, pull_second = jax.vjp(normalize, middle, gain_back[1], shift_full[1])
    middle_part, gain_two_grad, shift_two_grad = pull_second(normed_two_grad)
    middle_grad = incoming + middle_part
    middle_low = middle_grad.astype(jnp.bfloat16)
    out_grad = jnp.einsum("te,td->ed", attended, middle_low, preferred_element_type=jnp.float32)
    out_bias_grad = jnp.sum(middle_low.astype(jnp.float32), axis=0)
    attended_grad = jnp.einsum(
        "td,ed->te", middle_low, out_back, preferred_element_type=jnp.float32
    ).astype(jnp.bfloat16)
    grad_rows = attended_grad.reshape(samples, patches, features)
    grad_heads = split_heads(grad_rows)
    offset = jnp.transpose(jnp.sum(grad_heads.astype(jnp.float32) * attended_f, axis=-1), (0, 2, 1))
    grads_start = jnp.zeros((2, samples, patches, HEADS, HEAD_DIM), jnp.float32)

    def visit_block(blocks, partial_grads, query_acc):
        query_part, key_part, value_part = pair_terms(
            query_heads,
            grad_heads,
            log_total,
            offset,
            split_heads(blocks[0]),
            split_heads(blocks[1]),
        )
        return (partial_grads + jnp.stack([key_part, value_part]), query_acc + query_part)

    def turn_grads(partial_grads):
        return from_behind(partial_grads.astype(jnp.bfloat16), "seq", 1).astype(partial_grads.dtype)

    def cycle_step(counter, carried):
        blocks, partial_grads, query_acc = carried
        partial_grads, query_acc = visit_block(blocks, partial_grads, query_acc)
        partial_grads = turn_grads(partial_grads)
        blocks = from_behind(blocks, "seq", 1)
        return (blocks, partial_grads, query_acc)

    blocks_start = jnp.stack([keys_all, values_all])
    blocks, partial_grads, query_acc = lax.fori_loop(
        0, lax.axis_size("seq") - 1, cycle_step, (blocks_start, grads_start, zero_heads)
    )
    partial_grads, query_acc = visit_block(blocks, partial_grads, query_acc)
    partial_grads = turn_grads(partial_grads)
    query_low = query_acc.astype(jnp.bfloat16).reshape(row_count, features) * factor
    key_low = partial_grads[0].astype(jnp.bfloat16).reshape(row_count, features)
    value_low = partial_grads[1].astype(jnp.bfloat16).reshape(row_count, features)
    proj_grad = jnp.concatenate([query_low, key_low, value_low], axis=1)
    qkv_grad = jnp.einsum("td,te->de", normed, proj_grad, preferred_element_type=jnp.float32)
    qv_bias_grad = jnp.stack(
        [
            jnp.sum(query_low.astype(jnp.float32), axis=0),
            jnp.sum(value_low.astype(jnp.float32), axis=0),
        ]
    )
    normed_grad = jnp.einsum("te,de->td", proj_grad, qkv_back, preferred_element_type=jnp.float32)
    _, pull_first = jax.vjp(normalize, stream_rows, gain_back[0], shift_full[0])
    stream_part, gain_one_grad, shift_one_grad = pull_first(normed_grad)
    stream_grad = (middle_grad + stream_part).reshape(samples, patches, features)
    per_sample = jnp.sum(stream_grad, axis=1)
    lead_grad = jnp.sum(lead_value[:, None] * per_sample, axis=0)
    table_grad = jnp.dot(present.T, per_sample, precision=lax.Precision.HIGHEST)
    gain_grad = jnp.stack([gain_one_grad, gain_two_grad])
    shift_grad = jnp.stack([shift_one_grad, shift_two_grad])
    bias_grad = jnp.stack([out_bias_grad, down_bias_grad])
    owned = (
        lax.psum_scatter(table_grad, ("samp", "seq"), scatter_dimension=1, tiled=True),
        lax.psum_scatter(lead_grad, ("samp", "seq"), scatter_dimension=0, tiled=True),
        lax.psum_scatter(gain_grad, ("samp", "seq"), scatter_dimension=1, tiled=True),
        lax.psum_scatter(shift_grad, ("samp", "seq"), scatter_dimension=1, tiled=True),
        lax.psum_scatter(qkv_grad, ("samp", "seq"), scatter_dimension=0, tiled=True),
        lax.psum_scatter(qv_bias_grad, ("samp", "seq"), scatter_dimension=1, tiled=True),
        lax.psum_scatter(out_grad, ("samp", "seq"), scatter_dimension=0, tiled=True),
        lax.psum_scatter(bias_grad, ("samp", "seq"), scatter_dimension=1, tiled=True),
        lax.psum_scatter(up_grad, ("samp", "seq"), scatter_dimension=0, tiled=True),
        lax.psum_scatter(up_bias_grad, ("samp", "seq"), scatter_dimension=0, tiled=True),
        lax.psum_scatter(down_grad, ("samp", "seq"), scatter_dimension=0, tiled=True),
    )
    return (
        mixed,
        stream_grad,
        owned[0],
        owned[1],
        owned[2],
        owned[3],
        owned[4],
        owned[5],
        owned[6],
        owned[7],
        owned[8],
        owned[9],
        owned[10],
    )


MESH = pl.DeviceIdType.MESH
BF = jnp.bfloat16
F32 = jnp.float32
D = 1024
ROWS = 128
LANES = 8
FFL = 512


def dot_nn(a, b):
    return lax.dot_general(a, b, (((1,), (0,)), ((), ())), preferred_element_type=F32)


def dot_nt(a, b):
    return lax.dot_general(a, b, (((1,), (1,)), ((), ())), preferred_element_type=F32)


def dot_tn(a, b):
    return lax.dot_general(a, b, (((0,), (0,)), ((), ())), preferred_element_type=F32)


def erf(v):
    v = jnp.clip(v, -4.0, 4.0)
    s = v * v
    p = jnp.full_like(s, -2.72614225801306e-10)
    for a in (2.77068142495902e-08, -2.10102402082508e-06, -5.69250639462346e-05,
              -7.34990630326855e-04, -2.95459980854025e-03, -1.60960333262415e-02):
        p = p * s + a
    q = jnp.full_like(s, -1.45660718464996e-05)
    for b in (-2.13374055278905e-04, -1.68282697438203e-03, -7.37332916720468e-03, -1.42647390514189e-02):
        q = q * s + b
    return v * p / q


def flip(a, d):
    return 1 - a if d else a


def many(n, m=1):
    return pl.ds(pl.multiple_of(n, m), m)


def center(v):
    mean = jnp.mean(v, axis=-1, keepdims=True)
    centred = v - mean
    var = jnp.mean(centred * centred, axis=-1, keepdims=True)
    rstd = lax.rsqrt(var + epsilon)
    return centred * rstd, rstd


def norm_back(xhat, rstd, gain, grad):
    dx = grad * gain
    return rstd * (dx - jnp.mean(dx, axis=-1, keepdims=True) - xhat * jnp.mean(dx * xhat, axis=-1, keepdims=True))


def fast_kernel(
    tokens_h, lead_hours, var_mask, var_table, lead_weight, norm_gain, norm_shift, wqkv_h, qv_bias, wout_h,
    branch_bias, wup_h, up_bias, wdown_h, cot_h,
    mixed_o, tg_o, gq_o, go_o, gu_o, gd_o, small_o,
    tokens, wqkv_in, wup_in, wout_in, cot, tok_all, cot_all, n2_all, ml_all,
    wqkv, wup, wdown, wout, raw, pack_in, pack_all, full,
    normed, q_s, k_s, v_s, shares, attf, att,
    rs_s1, rs_r1, rs_s2, rs_r2, own, kept,
    middle, mgrad, act, uplow, dproj, dog, dk_acc, dv_acc,
    gqkv, gup, gdown, gout, xqkv, xup, xdown, zqkv_s, zup_s, zdown_s, zqkv, zup, zdown,
    out_x, out_s, out_z, sq2, su2, rq2, ru2, so2, ro2,
    tgr, smallp, r_a, s_b, r_b, upb_g, r_upb,
    ss, rs, ls,
):
    s_i = lax.axis_index("samp")
    q_i = lax.axis_index("seq")
    y, x = s_i // 2, s_i % 2
    z, c = q_i // 2, q_i % 2
    k, w = z // 2, z % 2
    idx = 16 * y + 8 * x + 4 * k + 2 * w + c
    lane = 4 * y + 2 * w + c
    rank = 2 * x + k
    sample = 2 * k + x
    off_diag = y + k - 2 * y * k
    is_home = 1 - (x + w - 2 * x * w) - (k + c - 2 * k * c) + (x + w - 2 * x * w) * (k + c - 2 * k * c)
    my_rows = many(ROWS * lane, ROWS)

    def dev(y_, x_, k_, w_, c_):
        return (2 * y_ + x_, 4 * k_ + 2 * w_ + c_)

    count = [0, 0]
    items = []

    def sems(n):
        a, b = count
        count[0] += n
        count[1] += n
        return a, b

    def rc(src, dst, a, b, device):
        return pltpu.make_async_remote_copy(src_ref=src, dst_ref=dst, send_sem=ss.at[a], recv_sem=rs.at[b], device_id=device, device_id_type=MESH)

    group = [(d // 4, (d // 2) % 2, d % 2) for d in range(1, 8)]
    chips = [(0, 0), (0, 1), (1, 0), (1, 1)]
    ranks = [(0, 1), (1, 0), (1, 1)]

    def peer(d):
        dy, dw, dc = d
        y_, w_, c_ = flip(y, dy), flip(w, dw), flip(c, dc)
        return y_, w_, c_, 4 * y_ + 2 * w_ + c_, dev(y_, x, k, w_, c_)

    def partner(d):
        dx, dk = d
        x_, k_ = flip(x, dx), flip(k, dk)
        return x_, k_, 2 * x_ + k_, dev(y, x_, k_, w, c)

    swap_dev = dev(k, x, y, w, c)

    rank_rows = many(128 * rank, 128)
    barrier = pltpu.get_barrier_semaphore()
    for d in group:
        pl.semaphore_signal(barrier, inc=1, device_id=peer(d)[4], device_id_type=MESH)
    for d in ranks:
        pl.semaphore_signal(barrier, inc=1, device_id=partner(d)[3], device_id_type=MESH)

    @pl.when(off_diag == 1)
    def _():
        pl.semaphore_signal(barrier, inc=1, device_id=swap_dev, device_id_type=MESH)

    loads = [
        pltpu.make_async_copy(src, dst, ls.at[n])
        for n, (src, dst) in enumerate(((tokens_h, tokens), (wqkv_h, wqkv_in), (wup_h, wup_in), (wout_h, wout_in), (cot_h, cot), (wdown_h, wdown.at[rank_rows])))
    ]
    for load in loads:
        load.start()
    raw[...] = jnp.zeros_like(raw)
    raw[0:48, 0:32] = var_table[...].astype(F32)
    for n, rows in ((48, norm_gain), (50, norm_shift), (52, qv_bias), (54, branch_bias)):
        raw[n : n + 2, 0:32] = rows[...].astype(F32)
    raw[56:57, 0:32] = lead_weight[...].astype(F32)
    raw[64:65, :] = up_bias[...].astype(F32)
    raw[65:66, 0:48] = var_mask[...].astype(F32)
    raw[65:66, 64:65] = lead_hours[...].astype(F32)
    packed = raw[0:16, :]
    for t in range(1, 4):
        packed = packed + pltpu.roll(raw[16 * t : 16 * t + 16, :], 32 * t, 1)
    pack_in[0:16, :] = packed.astype(BF)
    pack_in[16:32, :] = raw[64:80, :].astype(BF)
    for load in loads[:4]:
        load.wait()
    pl.semaphore_wait(barrier, 10 + off_diag)

    def begun(item):
        items.append(item)
        item.got = False

    class Swap:
        def __init__(self, src, dst):
            self.copy = rc(src, dst, *sems(1), swap_dev)

        def start(self):
            begun(self)
            pl.when(off_diag == 1)(self.copy.start)

        def wait(self):
            self.got = True
            pl.when(off_diag == 1)(self.copy.wait_recv)

        def drain(self):
            pl.when(off_diag == 1)(self.copy.wait_send)

    class Only:
        def __init__(self, sends, outgoing, takes, incoming):
            self.sends, self.outgoing, self.takes, self.incoming = sends, outgoing, takes, incoming

        def each(self, flag, copies, name):
            @pl.when(flag == 1)
            def _():
                for copy in copies:
                    getattr(copy, name)()

        def start(self):
            begun(self)
            self.each(self.sends, self.outgoing, "start")

        def wait(self):
            self.got = True
            self.each(self.takes, self.incoming, "wait_recv")

        def drain(self):
            self.each(self.sends, self.outgoing, "wait_send")

    def finish_all():
        for item in items:
            if not item.got:
                item.wait()
        for item in items:
            item.drain()

    y_nbr, w_nbr, sibling = dev(1 - y, x, k, w, c), dev(y, x, k, 1 - w, c), dev(y, x, k, w, 1 - c)
    UP, LOW = pl.ds(0, 64), pl.ds(64, 64)

    class Gather:
        def __init__(self, buf):
            self.buf = buf
            self.a, self.b = sems(10)

        def copy(self, n):
            ly, lw = 4 * (1 - y) + 2 * w + c, 4 * y + 2 * (1 - w) + c
            ld = 4 * (1 - y) + 2 * (1 - w) + c
            from_row, rows, device = (
                (ROWS * lane, 128, sibling),
                (ROWS * lane, 64, y_nbr), (ROWS * lane + 64, 64, y_nbr),
                (ROWS * lane + 64, 64, w_nbr), (ROWS * lane, 64, w_nbr),
                (ROWS * ly, 64, w_nbr), (ROWS * lw + 64, 64, y_nbr),
                (ROWS * ly, 128, sibling), (ROWS * lw, 128, sibling), (ROWS * ld, 128, sibling),
            )[n]
            ref = self.buf.at[pl.ds(pl.multiple_of(from_row, 64), rows)]
            return rc(ref, ref, self.a + n, self.b + n, device)

        def start(self):
            begun(self)
            self.passed = False
            for n in (1, 3, 2, 4, 0):
                self.copy(n).start()

        def pass_on(self):
            self.passed = True
            for n, then in ((1, 5), (3, 6), (2, 7), (4, 8), (5, None), (6, 9)):
                self.copy(n).wait_recv()
                if then is not None:
                    self.copy(then).start()

        def wait(self):
            if not self.passed:
                self.pass_on()
            self.got = True
            for n in (0, 7, 8, 9):
                self.copy(n).wait_recv()

        def drain(self):
            for n in range(10):
                self.copy(n).wait_send()

    class Scatter:
        def __init__(self, slot, partial):
            self.slot = slot
            self.partial = partial
            self.a1, self.b1 = sems(4)
            self.a2, self.b2 = sems(6)

        def far(self, i):
            dy, dw = i // 2, i % 2
            y_, w_ = y + dy - 2 * y * dy, w + dw - 2 * w * dw
            return y_, w_

        def first(self, i):
            return rc(rs_s1.at[self.slot, i], rs_r1.at[self.slot, i], self.a1 + i, self.b1 + i, sibling)

        def second(self, n):
            src, half, dst, half_there, device = (
                (2, UP, 2, UP, y_nbr), (2, LOW, 2, LOW, w_nbr),
                (0, UP, 0, UP, y_nbr), (1, LOW, 1, LOW, w_nbr),
                (0, LOW, 0, LOW, y_nbr), (1, UP, 1, UP, w_nbr),
            )[n]
            return rc(rs_s2.at[self.slot, src, half], rs_r2.at[self.slot, dst, half_there], self.a2 + n, self.b2 + n, device)

        def start(self, hold=False):
            begun(self)
            self.passed = False

            @pl.loop(0, 4)
            def _(n):
                i = 3 - n
                y_, w_ = self.far(i)
                rs_s1[self.slot, i] = self.partial(4 * y_ + 2 * w_ + 1 - c).astype(BF)
                self.first(i).start()

            def total(i):
                y_, w_ = self.far(i)
                part = self.partial(4 * y_ + 2 * w_ + c)
                self.first(i).wait_recv()
                return part + rs_r1[self.slot, i].astype(F32)

            rs_s2[self.slot, 2] = total(3).astype(BF)
            if not hold:
                self.second(0).start()
                self.second(1).start()
            value = total(2)
            rs_s2[self.slot, 0, 0:64] = value[0:64].astype(BF)
            if not hold:
                self.second(2).start()
            kept[self.slot, 0] = value[64:128]
            value = total(1)
            rs_s2[self.slot, 1, 64:128] = value[64:128].astype(BF)
            if not hold:
                self.second(3).start()
            kept[self.slot, 1] = value[0:64]
            own[self.slot] = total(0)

        def release(self):
            for n in range(4):
                self.second(n).start()

        def pass_on(self):
            self.passed = True
            self.second(0).wait_recv()
            rs_s2[self.slot, 1, 0:64] = (kept[self.slot, 1] + rs_r2[self.slot, 2, 0:64].astype(F32)).astype(BF)
            self.second(5).start()
            self.second(1).wait_recv()
            rs_s2[self.slot, 0, 64:128] = (kept[self.slot, 0] + rs_r2[self.slot, 2, 64:128].astype(F32)).astype(BF)
            self.second(4).start()

        def wait(self):
            if not self.passed:
                self.pass_on()
            self.got = True
            for n in (2, 3, 4, 5):
                self.second(n).wait_recv()
            return own[self.slot] + rs_r2[self.slot, 0].astype(F32) + rs_r2[self.slot, 1].astype(F32)

        def drain(self):
            for i in range(4):
                self.first(i).wait_send()
            for n in range(6):
                self.second(n).wait_send()

    class Batch:
        def __init__(self, copies):
            self.copies = copies
            self.a, self.b = sems(len(copies))

        def copy(self, n):
            src, dst, device = self.copies[n]
            return rc(src, dst, self.a + n, self.b + n, device)

        def start(self):
            begun(self)
            for n in range(len(self.copies)):
                self.copy(n).start()

        def wait(self):
            self.got = True
            for n in range(len(self.copies)):
                self.copy(n).wait_recv()

        def drain(self):
            for n in range(len(self.copies)):
                self.copy(n).wait_send()

    hx, hk = x + w - 2 * x * w, k + c - 2 * k * c
    z_dev, x_dev = partner((0, 1))[3], partner((1, 0))[3]

    class Across:
        def __init__(self, views):
            self.views = views
            self.n = len(views(x, k))
            self.a, self.b = sems(3 * self.n)

        def copies(self, leg):
            refs = self.views(x, 1 - k) if leg == 2 else self.views(x, k)
            at = self.n * leg
            return [rc(v, v, self.a + at + i, self.b + at + i, z_dev if leg == 0 else x_dev) for i, v in enumerate(refs)]

        def arrivals(self, leg):
            refs = self.views(*((x, 1 - k), (1 - x, k), (1 - x, 1 - k))[leg])
            at = self.n * leg
            return [rc(v, v, self.a + at + i, self.b + at + i, z_dev if leg == 0 else x_dev) for i, v in enumerate(refs)]

        def start(self):
            begun(self)
            self.passed = False
            for leg in (0, 1):
                for copy in self.copies(leg):
                    copy.start()

        def pass_on(self):
            self.passed = True
            for copy in self.arrivals(0):
                copy.wait_recv()
            for copy in self.copies(2):
                copy.start()

        def wait(self):
            if not self.passed:
                self.pass_on()
            self.got = True
            for leg in (1, 2):
                for copy in self.arrivals(leg):
                    copy.wait_recv()

        def drain(self):
            for leg in range(3):
                for copy in self.copies(leg):
                    copy.wait_send()

    class Reduce:
        def __init__(self, grad, rx, sz, rz):
            self.grad, self.rx, self.sz, self.rz = grad, rx, sz, rz
            self.runs = rx.shape[0]
            self.a, self.b = sems(self.runs + 1)

        def run(self, n):
            return rc(self.grad.at[many(512 * n + 256 * (1 - x), 256)], self.rx.at[n], self.a + n, self.b + n, x_dev)

        def last(self):
            return rc(self.sz, self.rz, self.a + self.runs, self.b + self.runs, z_dev)

        def start(self):
            begun(self)
            self.passed = False
            for n in range(self.runs):
                self.run(n).start()

        def part(self, n, k_):
            return (
                self.grad[many(512 * n + 256 * x + 128 * k_, 128), :].astype(F32)
                + self.rx[n, many(128 * k_, 128), :].astype(F32)
            )

        def pass_on(self):
            self.passed = True
            for n in range(self.runs):
                self.run(n).wait_recv()
            for n in range(self.runs):
                self.sz[n] = self.part(n, 1 - k).astype(BF)
            self.last().start()

        def wait(self):
            if not self.passed:
                self.pass_on()
            self.got = True
            self.last().wait_recv()

        def total(self, n):
            return self.part(n, k) + self.rz[n].astype(F32)

        def drain(self):
            for n in range(self.runs):
                self.run(n).wait_send()
            self.last().wait_send()

    swap_rows = many(ROWS * (4 * k + 2 * w + c), ROWS)
    tok_swap = Swap(tokens, tok_all.at[swap_rows])
    cot_swap = Swap(cot, cot_all.at[swap_rows])
    tok_swap.start()
    own_rows = many(32 * idx, 32)

    def up_cols(r, y_, w_, c_):
        return many(128 * (16 * y_ + 8 * (r // 2) + 4 * (r % 2) + 2 * w_ + c_), 128)

    copies = []
    for d in group:
        y_, w_, c_, l_, dv = peer(d)
        copies.append((pack_in, pack_all.at[idx], dv))
        for p in range(3):
            copies.append((wqkv_in.at[:, many(128 * (8 * p + l_), 128)], wqkv.at[own_rows, pl.ds(128 * p, 128)], dv))
    in_qkv = Batch(copies)
    in_qkv.start()

    out_a, out_b = sems(4)
    place = 2 * w + c
    out_rows = many(32 * place, 32)
    home_dev = dev(y, x, k, x, k)
    pairs = ((0, 1), (1, 0), (1, 1))
    away = 1 - is_home
    out_in = []
    for dw, dc in pairs:
        m = 2 * flip(w, dw) + flip(c, dc)
        out_in.append(rc(wout_in, wout.at[many(32 * m, 32)], out_a, out_b + m, home_dev))
    to_home = Only(away, [rc(wout_in, wout.at[out_rows], out_a, out_b + place, home_dev)], is_home, out_in)
    copies = []
    for d in group:
        y_, w_, c_, l_, dv = peer(d)
        for r in range(4):
            copies.append((wup_in.at[:, up_cols(r, y_, w_, c_)], wup.at[own_rows, pl.ds(128 * r, 128)], dv))
    in_up = Batch(copies)
    in_up.start()
    to_home.start()

    @pl.when(off_diag == 0)
    def _():
        tok_all[my_rows, :] = tokens[...]

    pack_all[idx] = pack_in[...]
    for p in range(3):
        wqkv[own_rows, 128 * p : 128 * p + 128] = wqkv_in[:, many(128 * (8 * p + lane), 128)]
    for r in range(4):
        wup[own_rows, 128 * r : 128 * r + 128] = wup_in[:, up_cols(r, y, w, c)]

    @pl.when(is_home == 1)
    def _():
        wout[out_rows, :] = wout_in[...]

    for load in loads[4:]:
        load.wait()

    @pl.when(off_diag == 0)
    def _():
        cot_all[my_rows, :] = cot[...]

    def runs_of(ref, *more):
        def views(x_, k_):
            refs = [more[0].at[pl.ds(16 * y_ + 8 * x_ + 4 * k_, 4)] for y_ in range(2)] if more else []
            return refs + [ref.at[many(512 * y_ + 256 * x_ + 128 * k_, 128)] for y_ in range(2)]

        return views

    dp_qkv = Across(runs_of(wqkv, pack_all))
    dp_up = Across(runs_of(wup))
    dp_down = Across(lambda x_, k_: [wdown.at[many(128 * (2 * x_ + k_), 128)]])
    in_qkv.wait()
    dp_qkv.start()
    tok_swap.wait()
    tok = Gather(tok_all)
    tok.start()
    cot_swap.start()

    dpo_a, dpo_b = sems(2)
    out_z_copy = rc(wout, wout, dpo_a, dpo_b, z_dev)
    out_x_copy = rc(wout, wout, dpo_a + 1, dpo_b + 1, x_dev)
    dp_out = Only(is_home, [out_z_copy, out_x_copy], (1 - hx) * hk, [out_z_copy])
    dp_out_more = Only((1 - hx) * hk, [out_x_copy], hx, [out_x_copy])
    to_home.wait()
    in_up.wait()
    dp_qkv.pass_on()
    dp_out.start()
    dp_up.start()
    tok.pass_on()

    dp_qkv.wait()
    lane_id = lax.broadcasted_iota(jnp.int32, (16, 128), 1)
    for b in range(8):
        for t in range(4):
            block = None
            for m in range(4):
                piece = pack_all[4 * b + m].astype(F32)[0:16, :]
                shift = (32 * (m - t)) % 128
                if shift:
                    piece = pltpu.roll(piece, shift, 1)
                block = piece if block is None else jnp.where(lane_id // 32 == m, piece, block)
            full[16 * t : 16 * t + 16, 128 * b : 128 * b + 128] = block

    gain0, gain1 = full[48:49, :], full[49:50, :]
    shift0, shift1 = full[50:51, :], full[51:52, :]
    lane_cols = many(128 * lane, 128)
    bias_q, bias_v = full[52:53, lane_cols], full[53:54, lane_cols]
    bias_out, bias_down = full[54:55, :], full[55:56, :]
    bias_up = jnp.concatenate(
        [pack_all[16 * y + 8 * (r // 2) + 4 * (r % 2) + 2 * w + c].astype(F32)[16:17, :] for r in range(4)], axis=1
    )
    facts = pack_all[8 * sample].astype(F32)[17:18, :]
    one_lane = lax.broadcasted_iota(jnp.int32, (1, 128), 1)
    present = jnp.where(one_lane < 64, facts, 0.0)
    hours = jnp.sum(jnp.where(one_lane == 64, facts, 0.0), axis=-1, keepdims=True) * hours_scale
    present8 = jnp.broadcast_to(present, (8, 128))[:, :64].astype(BF)
    extra = dot_nn(present8, full[...].astype(BF))[0:1, :] + hours * full[56:57, :]

    tok.wait()

    @pl.loop(0, 8)
    def _(n):
        rows = many(128 * n, 128)
        xhat, _ = center(tok_all[rows, :].astype(F32) + extra)
        normed[rows, :] = (xhat * gain0 + shift0).astype(BF)

    @pl.loop(0, 4)
    def _(n):
        rows = many(256 * n, 256)
        proj = dot_nn(normed[rows, :], wqkv[...])
        q_s[rows, :] = ((proj[:, :128] + bias_q) * 0.125).astype(BF)
        k_s[rows, :] = proj[:, 128:256].astype(BF)
        v_s[rows, :] = (proj[:, 256:384] + bias_v).astype(BF)

    QB = 256
    cot_swap.wait()
    cg = Gather(cot_all)
    cg.start()
    dp_down.start()
    dp_out.wait()
    dp_out_more.start()
    head_lane = lax.broadcasted_iota(jnp.int32, (1, 128), 1) // 64

    def of_head(v, h):
        return jnp.where(head_lane == h, v, jnp.zeros_like(v))

    @pl.loop(0, D // QB)
    def _(n):
        rows = many(QB * n, QB)
        queries = q_s[rows, :]
        total = None
        for h in range(2):
            scores = dot_nt(of_head(queries, h), k_s[...])
            top = jnp.max(scores, axis=-1, keepdims=True)
            e = jnp.exp(scores - top)
            share = (e * (1.0 / jnp.sum(e, axis=-1, keepdims=True))).astype(BF)
            shares[h, rows, :] = share
            got = of_head(dot_nn(share, v_s[...]), h)
            total = got if total is None else total + got
        attf[rows, :] = total
        att[rows, :] = total.astype(BF)

    dp_out_more.wait()

    def rows_of(l_):
        return many(ROWS * l_, ROWS)

    rs_out = Scatter(0, lambda l_: dot_nn(att[rows_of(l_), :], wout[...]))
    rs_out.start()
    rs_out.pass_on()

    cg.pass_on()
    dp_up.pass_on()

    stream = tok_all[my_rows, :].astype(F32) + extra
    mid = stream + (rs_out.wait() + bias_out)
    middle[...] = mid
    xhat2, rstd2 = center(mid)
    n2_all[my_rows, :] = (xhat2 * gain1 + shift1).astype(BF)
    n2 = Gather(n2_all)
    n2.start()
    dp_down.pass_on()
    n2.pass_on()
    dp_up.wait()
    dp_down.wait()
    cg.wait()
    n2.wait()

    upb_g[...] = jnp.zeros_like(upb_g)

    @pl.loop(0, 8)
    def _(n):
        rows = many(128 * n, 128)
        up = dot_nn(n2_all[rows, :], wup[...]) + bias_up
        cdf = 0.5 * (1.0 + erf(up * 0.7071067811865476))
        act[rows, :] = (up * cdf).astype(BF)
        slope = cdf + up * (jnp.exp(-0.5 * up * up) * 0.3989422804014327)
        low = (dot_nt(cot_all[rows, :], wdown[...]) * slope).astype(BF)
        uplow[rows, :] = low
        upb_g[0:1, :] += jnp.sum(low.astype(F32), axis=0, keepdims=True)

    rs_n2 = Scatter(1, lambda l_: dot_nt(uplow[rows_of(l_), :], wup[...]))
    rs_n2.start()

    @pl.loop(0, 4)
    def _(r):
        cols = many(128 * r, 128)
        gdown[cols, :] = dot_tn(act[:, cols], cot_all[...]).astype(BF)

    down_red = Reduce(gdown, xdown, zdown_s, zdown)
    down_red.start()
    rs_n2.pass_on()
    upb_sends = Batch([(upb_g.at[:, many(128 * partner(d)[2], 128)], r_upb.at[n], partner(d)[3]) for n, d in enumerate(ranks)])
    upb_sends.start()

    @pl.loop(0, 4)
    def _(n):
        cols = many(256 * n, 256)
        gup[cols, :] = dot_tn(n2_all[:, cols], uplow[...]).astype(BF)

    up_red = Reduce(gup, xup, zup_s, zup)
    up_red.start()

    rs_mix = Scatter(2, lambda l_: dot_nn(act[rows_of(l_), :], wdown[...]))
    rs_mix.start(hold=True)
    n2_grad = rs_n2.wait()
    incoming = cot_all[my_rows, :].astype(F32)
    xhat2, rstd2 = center(middle[...])
    mg = incoming + norm_back(xhat2, rstd2, gain1, n2_grad)
    mgrad[...] = mg
    ml_all[my_rows, :] = mg.astype(BF)
    ml = Gather(ml_all)
    ml.start()
    smallp[7:16, :] = jnp.zeros((9, D), F32)
    smallp[2:3, :] = jnp.sum(n2_grad * xhat2, axis=0, keepdims=True)
    smallp[4:5, :] = jnp.sum(n2_grad, axis=0, keepdims=True)
    smallp[5:6, :] = jnp.sum(mg.astype(BF).astype(F32), axis=0, keepdims=True)
    smallp[6:7, :] = jnp.sum(incoming, axis=0, keepdims=True)

    down_red.pass_on()
    ml.pass_on()
    up_red.pass_on()
    ml.wait()
    rs_mix.release()

    @pl.loop(0, 4)
    def _(n):
        rows = many(256 * n, 256)
        dog[rows, :] = dot_nt(ml_all[rows, :], wout[...]).astype(BF)

    dk_acc[...] = jnp.zeros_like(dk_acc)
    dv_acc[...] = jnp.zeros_like(dv_acc)

    def attend_back(n):
        rows = many(QB * n, QB)
        queries = q_s[rows, :]
        grads = dog[rows, :]
        both = grads.astype(F32) * attf[rows, :]
        dq = None
        for h in range(2):
            share = shares[h, rows, :]
            pressure = dot_nt(of_head(grads, h), v_s[...])
            offset = jnp.sum(of_head(both, h), axis=-1, keepdims=True)
            ds = (share.astype(F32) * (pressure - offset)).astype(BF)
            got = of_head(dot_nn(ds, k_s[...]), h)
            dq = got if dq is None else dq + got
            dk_acc[...] += dot_tn(ds, of_head(queries, h))
            dv_acc[...] += dot_tn(share, of_head(grads, h))
        dproj[rows, 0:128] = (dq.astype(BF).astype(F32) * 0.125).astype(BF)

    pl.loop(0, 2)(attend_back)
    rs_mix.pass_on()
    pl.loop(2, 4)(attend_back)
    dproj[:, 128:256] = dk_acc[...].astype(BF)
    dproj[:, 256:384] = dv_acc[...].astype(BF)

    low = dproj[...].astype(F32)
    smallp[8:9, lane_cols] = jnp.sum(low[:, 0:128], axis=0, keepdims=True)
    smallp[9:10, lane_cols] = jnp.sum(low[:, 256:384], axis=0, keepdims=True)
    rs_n1 = Scatter(3, lambda l_: dot_nt(dproj[rows_of(l_), :], wqkv[...]))
    rs_n1.start()

    @pl.loop(0, 4)
    def _(n):
        cols = many(256 * n, 256)
        gqkv[cols, :] = dot_tn(normed[:, cols], dproj[...]).astype(BF)

    qkv_red = Reduce(gqkv, xqkv, zqkv_s, zqkv)
    qkv_red.start()
    rs_n1.pass_on()
    gout[...] = dot_tn(att[...], ml_all[...]).astype(BF)
    go_a, go_b = sems(2)
    grad_x = Only(hx, [rc(gout, out_x, go_a, go_b, x_dev)], 1 - hx, [rc(gout, out_x, go_a, go_b, x_dev)])
    grad_z = Only((1 - hx) * hk, [rc(out_s, out_z, go_a + 1, go_b + 1, z_dev)], is_home, [rc(out_s, out_z, go_a + 1, go_b + 1, z_dev)])
    grad_x.start()
    mixed_low = (middle[...] + (rs_mix.wait() + bias_down)).astype(BF)
    tgr[2] = mixed_low
    mix_swap = Swap(tgr.at[2], tgr.at[3])
    mix_swap.start()
    qkv_red.pass_on()
    grad_x.wait()

    @pl.when(hx == 0)
    def _():
        out_s[...] = (gout[...].astype(F32) + out_x[...].astype(F32)).astype(BF)

    grad_z.start()

    n1_grad = rs_n1.wait()
    xhat1, rstd1 = center(tok_all[my_rows, :].astype(F32) + extra)
    tg = mgrad[...] + norm_back(xhat1, rstd1, gain0, n1_grad)
    tgr[0] = tg.astype(BF)
    smallp[0:1, :] = jnp.sum(tg, axis=0, keepdims=True)
    smallp[1:2, :] = jnp.sum(n1_grad * xhat1, axis=0, keepdims=True)
    smallp[3:4, :] = jnp.sum(n1_grad, axis=0, keepdims=True)

    def block(y_, x_, k_):
        return smallp.at[:, many(128 * (4 * y_ + 2 * x_ + k_), 128)]

    copies = []
    for n, d in enumerate(ranks):
        x_, k_, r_, dv = partner(d)
        for y_ in range(2):
            copies.append((block(y_, x_, k_), r_b.at[n, y_], dv))
    small_ranks = Batch(copies)
    small_ranks.start()
    tg_swap = Swap(tgr.at[0], tgr.at[1])
    tg_swap.start()
    small_ranks.wait()
    for y_ in range(2):
        first = smallp[:, many(128 * (4 * y_ + 2 * x + k), 128)]
        s_b[y_, 0:1, :] = first[0:1, :]
        for n in range(3):
            s_b[y_, n + 1 : n + 2, :] = r_b[n, y_, 0:1, :]
        s_b[y_, 4:16, :] = (first + r_b[0, y_] + r_b[1, y_] + r_b[2, y_])[1:13, :]
    small_group = Batch([(s_b.at[peer(d)[0]], r_a.at[n], peer(d)[4]) for n, d in enumerate(group)])
    small_group.start()

    down_red.wait()
    gd_o[...] = down_red.total(0).astype(BF)

    def deal(low_sum, recv):
        copies = []
        for n, d in enumerate(group):
            y_, w_, c_, l_, dv = peer(d)
            copies.append((low_sum.at[many(128 * y_ + 64 * w_ + 32 * c_, 32)], recv.at[lane], dv))
        return Batch(copies)

    def collect(red, low_sum, recv):
        red.wait()
        for y_ in range(2):
            low_sum[128 * y_ : 128 * y_ + 128, :] = red.total(y_).astype(BF)
        batch = deal(low_sum, recv)
        batch.start()
        recv[lane] = low_sum[many(128 * y + 64 * w + 32 * c, 32), :]
        return batch

    up_deal = collect(up_red, su2, ru2)
    grad_z.wait()

    @pl.when(is_home == 1)
    def _():
        so2[...] = (out_s[...].astype(F32) + out_z[...].astype(F32)).astype(BF)
        go_o[...] = so2[out_rows, :]

    outs_a, outs_b = sems(3)
    copies = []
    for n, (dw, dc) in enumerate(pairs):
        w_, c_ = flip(w, dw), flip(c, dc)
        copies.append(rc(so2.at[many(32 * (2 * w_ + c_), 32)], ro2, outs_a + n, outs_b, dev(y, x, k, w_, c_)))
    out_deal = Only(is_home, copies, away, [rc(so2.at[pl.ds(0, 32)], ro2, outs_a, outs_b, home_dev)])
    out_deal.start()
    qkv_deal = collect(qkv_red, sq2, rq2)

    small_group.wait()
    total = s_b[y]
    for n in range(7):
        total = total + r_a[n]
    own_facts = [facts] + [pack_all[8 * (2 * partner(d)[1] + partner(d)[0])].astype(F32)[17:18, :] for d in ranks]
    facts_t = jnp.transpose(jnp.concatenate(own_facts + [jnp.zeros((4, 128), F32)], axis=0))
    table = None
    for n in range(4):
        part = facts_t[:, n : n + 1] * total[n : n + 1, :]
        table = part if table is None else table + part
    small_o[0:64, :] = table[0:64, :]
    small_o[64:80, :] = total
    small_o[80:81, :] = table[64:65, :] * hours_scale
    small_o[81:88, :] = jnp.zeros((7, 128), F32)
    upb_sends.wait()
    sum_upb = upb_g[:, rank_rows]
    for n in range(3):
        sum_upb = sum_upb + r_upb[n]
    small_o[88:96, :] = sum_upb

    out_deal.wait()

    @pl.when(is_home == 0)
    def _():
        go_o[...] = ro2[...]

    @pl.when(off_diag == 0)
    def _():
        tg_o[...] = tgr[0]
        mixed_o[...] = tgr[2]

    mix_swap.wait()
    tg_swap.wait()

    @pl.when(off_diag == 1)
    def _():
        tg_o[...] = tgr[1]
        mixed_o[...] = tgr[3]

    up_deal.wait()
    gu_o[...] = ru2[...]
    qkv_deal.wait()
    gq_o[...] = rq2[...]

    finish_all()


def finish_kernel(
    mixed_i, tg_i, gq_i, go_i, gu_i, gd_i, small_i,
    mixed_o, tg_o, table_o, lead_o, gain_o, shift_o, gq_o, qv_o, go_o, bias_o, gu_o, upb_o, gd_o,
):
    mixed_o[0] = mixed_i[...]
    tg_o[0] = tg_i[...].astype(F32)
    gd_o[...] = gd_i[...].astype(F32)
    go_o[...] = go_i[...].astype(F32)
    for l_ in range(8):
        part = gu_i[l_].astype(F32)
        y_, w_, c_ = l_ // 4, (l_ // 2) % 2, l_ % 2
        for r in range(4):
            at = 128 * (16 * y_ + 8 * (r // 2) + 4 * (r % 2) + 2 * w_ + c_)
            gu_o[:, at : at + 128] = part[:, 128 * r : 128 * r + 128]
        part = gq_i[l_].astype(F32)
        for p in range(3):
            at = 128 * (8 * p + l_)
            gq_o[:, at : at + 128] = part[:, 128 * p : 128 * p + 128]
    place = lax.rem(lax.axis_index("seq"), 4)
    small = small_i[0:88, :]
    mine = small
    for m in range(1, 4):
        mine = jnp.where(place == m, pltpu.roll(small, 128 - 32 * m, 1), mine)
    table_o[...] = mine[0:48, 0:32]
    gain_o[...] = mine[68:70, 0:32]
    shift_o[...] = mine[70:72, 0:32]
    bias_o[...] = mine[72:74, 0:32]
    qv_o[...] = mine[75:77, 0:32]
    lead_o[...] = mine[80:81, 0:32]
    upb_o[...] = small_i[88:89, :]


def local_fast(
    tokens, lead_hours, var_mask, var_table, lead_weight, norm_gain, norm_shift, w_qkv, qv_bias, w_out,
    branch_bias, w_up, up_bias, w_down, cotangent,
):
    vm = pltpu.VMEM
    scratch = [
        vm((128, D), BF), vm((32, 3 * D), BF), vm((32, 4 * D), BF), vm((32, D), BF), vm((128, D), BF),
        vm((D, D), BF), vm((D, D), BF), vm((D, D), BF), vm((D, D), BF),
        vm((D, 384), BF), vm((D, FFL), BF), vm((FFL, D), BF), vm((128, D), BF), vm((80, 128), F32), vm((32, 128), BF), vm((32, 32, 128), BF), vm((64, D), F32),
        vm((D, D), BF), vm((D, 128), BF), vm((D, 128), BF), vm((D, 128), BF), vm((2, D, D), BF), vm((D, 128), F32), vm((D, 128), BF),
        vm((4, 4, 128, D), BF), vm((4, 4, 128, D), BF), vm((4, 3, 128, D), BF), vm((4, 3, 128, D), BF), vm((4, 128, D), F32), vm((4, 2, 64, D), F32),
        vm((128, D), F32), vm((128, D), F32), vm((D, FFL), BF), vm((D, FFL), BF), vm((D, 384), BF), vm((D, 128), BF), vm((D, 128), F32), vm((D, 128), F32),
        vm((D, 384), BF), vm((D, FFL), BF), vm((FFL, D), BF), vm((128, D), BF),
        vm((2, 256, 384), BF), vm((2, 256, FFL), BF), vm((1, 256, D), BF),
        vm((2, 128, 384), BF), vm((2, 128, FFL), BF), vm((1, 128, D), BF),
        vm((2, 128, 384), BF), vm((2, 128, FFL), BF), vm((1, 128, D), BF),
        vm((128, D), BF), vm((128, D), BF), vm((128, D), BF),
        vm((256, 384), BF), vm((256, FFL), BF), vm((8, 32, 384), BF), vm((8, 32, FFL), BF), vm((128, D), BF), vm((32, D), BF),
        vm((4, 128, D), BF), vm((16, D), F32), vm((7, 16, 128), F32), vm((2, 16, 128), F32), vm((3, 2, 16, 128), F32),
        vm((8, FFL), F32), vm((3, 8, 128), F32),
        pltpu.SemaphoreType.DMA((320,)), pltpu.SemaphoreType.DMA((320,)), pltpu.SemaphoreType.DMA((8,)),
    ]
    shape = jax.ShapeDtypeStruct
    raw = pl.pallas_call(
        fast_kernel,
        out_shape=[
            shape((128, D), BF), shape((128, D), BF), shape((8, 32, 384), BF), shape((32, D), BF), shape((8, 32, FFL), BF),
            shape((128, D), BF), shape((96, 128), F32),
        ],
        in_specs=[pl.BlockSpec(memory_space=pl.ANY if n in (0, 7, 9, 11, 13, 14) else vm) for n in range(15)],
        out_specs=[pl.BlockSpec(memory_space=vm)] * 7,
        scratch_shapes=scratch,
        compiler_params=pltpu.CompilerParams(collective_id=0, has_side_effects=True, vmem_limit_bytes=62 * 2**20),
        cost_estimate=pl.CostEstimate(flops=14_000_000_000, bytes_accessed=4_000_000, transcendentals=6_000_000),
    )(
        tokens[0], lead_hours[None], var_mask, var_table, lead_weight[None], norm_gain, norm_shift, w_qkv, qv_bias, w_out,
        branch_bias, w_up, up_bias[None], w_down, cotangent[0],
    )
    out = pl.pallas_call(
        finish_kernel,
        out_shape=[
            shape((1, 128, D), BF), shape((1, 128, D), F32), shape((48, 32), F32), shape((1, 32), F32), shape((2, 32), F32),
            shape((2, 32), F32), shape((32, 3 * D), F32), shape((2, 32), F32), shape((32, D), F32), shape((2, 32), F32),
            shape((32, 4 * D), F32), shape((1, 128), F32), shape((128, D), F32),
        ],
        in_specs=[pl.BlockSpec(memory_space=vm)] * 7,
        out_specs=[pl.BlockSpec(memory_space=vm)] * 13,
        compiler_params=pltpu.CompilerParams(vmem_limit_bytes=62 * 2**20),
        cost_estimate=pl.CostEstimate(flops=1_000_000, bytes_accessed=4_000_000, transcendentals=0),
    )(*raw)
    mixed, tg, table, lead, gain, shift, gq, qv, go, bias, gu, upb, gd = out
    return (mixed, tg, table, lead[0], gain, shift, gq, qv, go, bias, gu, upb[0], gd)


def solution(mesh):
    sizes = dict(mesh.shape)
    fast = sizes == {"samp": 4, "seq": 8}
    return jax.shard_map(
        local_fast if fast else local,
        mesh=mesh,
        in_specs=(
            P("samp", "seq", None),
            P("samp"),
            P("samp", None),
            P(None, ("samp", "seq")),
            P(("samp", "seq")),
            P(None, ("samp", "seq")),
            P(None, ("samp", "seq")),
            P(("samp", "seq"), None),
            P(None, ("samp", "seq")),
            P(("samp", "seq"), None),
            P(None, ("samp", "seq")),
            P(("samp", "seq"), None),
            P(("samp", "seq")),
            P(("samp", "seq"), None),
            P("samp", "seq", None),
        ),
        out_specs=(
            P("samp", "seq", None),
            P("samp", "seq", None),
            P(None, ("samp", "seq")),
            P(("samp", "seq")),
            P(None, ("samp", "seq")),
            P(None, ("samp", "seq")),
            P(("samp", "seq"), None),
            P(None, ("samp", "seq")),
            P(("samp", "seq"), None),
            P(None, ("samp", "seq")),
            P(("samp", "seq"), None),
            P(("samp", "seq")),
            P(("samp", "seq"), None),
        ),
        check_vma=False,
    )
```

```python
import jax
import jax.numpy as jnp
from jax import lax
from jax.experimental import pallas as pl
from jax.experimental.pallas import tpu as pltpu
from jax.sharding import PartitionSpec as P

HEADS = 16
HEAD_DIM = 64


epsilon = 1e-05
hours_scale = 1.0 / 168.0


def from_behind(block, axis, distance):
    devices = range(lax.axis_size(axis))
    route = [((i - distance) % len(devices), i) for i in devices]
    return lax.ppermute(block, axis, route)


def normalize(field, scaling, offsets):
    average = jnp.mean(field, axis=-1, keepdims=True)
    centred = field - average
    variance = jnp.mean(centred * centred, axis=-1, keepdims=True)
    return centred * lax.rsqrt(variance + epsilon) * scaling + offsets


def block_size(length):
    size_now = length
    while size_now > 512 and size_now % 2 == 0:
        size_now = size_now // 2
    return size_now


def over_blocks(advance, carried, segments):
    length = segments[0].shape[1]
    size_now = block_size(length)
    number = length // size_now
    stacked = tuple(
        (
            jnp.moveaxis(
                segment.reshape(segment.shape[0], number, size_now, segment.shape[2]), 1, 0
            )
            for segment in segments
        )
    )

    def visit(current, blocks):
        return (advance(current, blocks), None)

    carried, _ = lax.scan(visit, carried, stacked)
    return carried


def split_heads(matrix):
    return matrix.reshape(matrix.shape[0], matrix.shape[1], HEADS, HEAD_DIM)


def gelu_slope(upward):
    normal_cdf = 0.5 * (1.0 + lax.erf(upward * 0.7071067811865476))
    density = jnp.exp(-0.5 * upward * upward) * 0.3989422804014327
    return normal_cdf + upward * density


def pair_terms(query_heads, grad_heads, log_total, offset, key_heads, value_heads):
    scores = jnp.einsum(
        "sqhd,skhd->shqk", query_heads, key_heads, preferred_element_type=jnp.float32
    )
    shares = jnp.exp(scores - log_total[..., None])
    pressure = jnp.einsum(
        "sqhd,skhd->shqk", grad_heads, value_heads, preferred_element_type=jnp.float32
    )
    score_grad = (shares * (pressure - offset[..., None])).astype(jnp.bfloat16)
    query_part = jnp.einsum(
        "shqk,skhd->sqhd", score_grad, key_heads, preferred_element_type=jnp.float32
    )
    key_part = jnp.einsum(
        "shqk,sqhd->skhd", score_grad, query_heads, preferred_element_type=jnp.float32
    )
    value_part = jnp.einsum(
        "shqk,sqhd->skhd",
        shares.astype(jnp.bfloat16),
        grad_heads,
        preferred_element_type=jnp.float32,
    )
    return (query_part, key_part, value_part)


def local(
    tokens,
    lead_hours,
    var_mask,
    var_table,
    lead_weight,
    norm_gain,
    norm_shift,
    w_qkv,
    qv_bias,
    w_out,
    branch_bias,
    w_up,
    up_bias,
    w_down,
    cotangent,
):
    samples, patches, features = tokens.shape
    row_count = samples * patches
    factor = HEAD_DIM ** (-0.5)
    (
        table_full,
        lead_full,
        gain_all,
        shift_all,
        qkv_full,
        qv_all,
        out_full,
        bias_all,
        up_full,
        upb_full,
        down_full,
    ) = (
        lax.all_gather(var_table, ("samp", "seq"), axis=1, tiled=True),
        lax.all_gather(lead_weight, ("samp", "seq"), axis=0, tiled=True),
        lax.all_gather(norm_gain, ("samp", "seq"), axis=1, tiled=True),
        lax.all_gather(norm_shift, ("samp", "seq"), axis=1, tiled=True),
        lax.all_gather(w_qkv, ("samp", "seq"), axis=0, tiled=True),
        lax.all_gather(qv_bias, ("samp", "seq"), axis=1, tiled=True),
        lax.all_gather(w_out, ("samp", "seq"), axis=0, tiled=True),
        lax.all_gather(branch_bias, ("samp", "seq"), axis=1, tiled=True),
        lax.all_gather(w_up, ("samp", "seq"), axis=0, tiled=True),
        lax.all_gather(up_bias, ("samp", "seq"), axis=0, tiled=True),
        lax.all_gather(w_down, ("samp", "seq"), axis=0, tiled=True),
    )
    gain_full = gain_all.astype(jnp.float32)
    shift_full = shift_all.astype(jnp.float32)
    qv_full = qv_all.astype(jnp.float32)
    bias_full = bias_all.astype(jnp.float32)
    lead_value = lead_hours.astype(jnp.float32) * hours_scale
    present = var_mask.astype(jnp.float32)
    variable_sum = jnp.dot(present, table_full.astype(jnp.float32), precision=lax.Precision.HIGHEST)
    stream = (
        tokens.astype(jnp.float32)
        + lead_value[:, None, None] * lead_full.astype(jnp.float32)
        + variable_sum[:, None, :]
    )
    stream_rows = stream.reshape(row_count, features)
    normed = normalize(stream_rows, gain_full[0], shift_full[0]).astype(jnp.bfloat16)
    projected = jnp.dot(normed, qkv_full, preferred_element_type=jnp.float32)
    queries = (
        ((projected[:, :features] + qv_full[0]) * factor)
        .astype(jnp.bfloat16)
        .reshape(samples, patches, features)
    )
    keys_all = (
        projected[:, features : 2 * features]
        .astype(jnp.bfloat16)
        .reshape(samples, patches, features)
    )
    values_all = (
        (projected[:, 2 * features :] + qv_full[1])
        .astype(jnp.bfloat16)
        .reshape(samples, patches, features)
    )
    query_heads = split_heads(queries)

    def scores_of(keys_block):
        return jnp.einsum(
            "sqhd,skhd->shqk",
            query_heads,
            split_heads(keys_block),
            preferred_element_type=jnp.float32,
        )

    def stats_step(carried, blocks):
        running_max, running_sum = carried
        scores = scores_of(blocks[0])
        new_max = jnp.maximum(running_max, jnp.max(scores, axis=-1))
        running_sum = running_sum * jnp.exp(running_max - new_max) + jnp.sum(
            jnp.exp(scores - new_max[..., None]), axis=-1
        )
        return (new_max, running_sum)

    stats_start = (
        jnp.full((samples, HEADS, patches), -jnp.inf, jnp.float32),
        jnp.zeros((samples, HEADS, patches), jnp.float32),
    )
    running_max, running_sum = over_blocks(
        stats_step, stats_start, (lax.all_gather(keys_all, "seq", axis=1, tiled=True),)
    )
    log_total = running_max + jnp.log(running_sum)

    def mix_step(collected, blocks):
        shares = jnp.exp(scores_of(blocks[0]) - log_total[..., None]).astype(jnp.bfloat16)
        return collected + jnp.einsum(
            "shqk,skhd->sqhd", shares, split_heads(blocks[1]), preferred_element_type=jnp.float32
        )

    zero_heads = jnp.zeros((samples, patches, HEADS, HEAD_DIM), jnp.float32)
    attended_f = over_blocks(
        mix_step,
        zero_heads,
        (
            lax.all_gather(keys_all, "seq", axis=1, tiled=True),
            lax.all_gather(values_all, "seq", axis=1, tiled=True),
        ),
    )
    attended = attended_f.reshape(row_count, features).astype(jnp.bfloat16)
    middle = stream_rows + (
        jnp.dot(attended, out_full, preferred_element_type=jnp.float32) + bias_full[0]
    )
    normed_two = normalize(middle, gain_full[1], shift_full[1]).astype(jnp.bfloat16)
    upward = jnp.dot(normed_two, up_full, preferred_element_type=jnp.float32) + upb_full.astype(
        jnp.float32
    )
    activated = jax.nn.gelu(upward, approximate=False).astype(jnp.bfloat16)
    downward = jnp.dot(activated, down_full, preferred_element_type=jnp.float32) + bias_full[1]
    mixed = (middle + downward).astype(jnp.bfloat16).reshape(samples, patches, features)
    gain_back, qkv_back, out_back, up_back, down_back = (
        lax.all_gather(norm_gain, ("samp", "seq"), axis=1, tiled=True),
        lax.all_gather(w_qkv, ("samp", "seq"), axis=0, tiled=True),
        lax.all_gather(w_out, ("samp", "seq"), axis=0, tiled=True),
        lax.all_gather(w_up, ("samp", "seq"), axis=0, tiled=True),
        lax.all_gather(w_down, ("samp", "seq"), axis=0, tiled=True),
    )
    gain_back = gain_back.astype(jnp.float32)
    incoming = cotangent.astype(jnp.float32).reshape(row_count, features)
    incoming_low = incoming.astype(jnp.bfloat16)
    down_grad = jnp.einsum("tf,td->fd", activated, incoming_low, preferred_element_type=jnp.float32)
    down_bias_grad = jnp.sum(incoming_low.astype(jnp.float32), axis=0)
    gelu_grad = jnp.einsum(
        "td,fd->tf", incoming_low, down_back, preferred_element_type=jnp.float32
    ) * gelu_slope(upward)
    up_low = gelu_grad.astype(jnp.bfloat16)
    up_grad = jnp.einsum("td,tf->df", normed_two, up_low, preferred_element_type=jnp.float32)
    up_bias_grad = jnp.sum(up_low.astype(jnp.float32), axis=0)
    normed_two_grad = jnp.einsum("tf,df->td", up_low, up_back, preferred_element_type=jnp.float32)
    _, pull_second = jax.vjp(normalize, middle, gain_back[1], shift_full[1])
    middle_part, gain_two_grad, shift_two_grad = pull_second(normed_two_grad)
    middle_grad = incoming + middle_part
    middle_low = middle_grad.astype(jnp.bfloat16)
    out_grad = jnp.einsum("te,td->ed", attended, middle_low, preferred_element_type=jnp.float32)
    out_bias_grad = jnp.sum(middle_low.astype(jnp.float32), axis=0)
    attended_grad = jnp.einsum(
        "td,ed->te", middle_low, out_back, preferred_element_type=jnp.float32
    ).astype(jnp.bfloat16)
    grad_rows = attended_grad.reshape(samples, patches, features)
    grad_heads = split_heads(grad_rows)
    offset = jnp.transpose(jnp.sum(grad_heads.astype(jnp.float32) * attended_f, axis=-1), (0, 2, 1))
    grads_start = jnp.zeros((2, samples, patches, HEADS, HEAD_DIM), jnp.float32)

    def visit_block(blocks, partial_grads, query_acc):
        query_part, key_part, value_part = pair_terms(
            query_heads,
            grad_heads,
            log_total,
            offset,
            split_heads(blocks[0]),
            split_heads(blocks[1]),
        )
        return (partial_grads + jnp.stack([key_part, value_part]), query_acc + query_part)

    def turn_grads(partial_grads):
        return from_behind(partial_grads.astype(jnp.bfloat16), "seq", 1).astype(partial_grads.dtype)

    def cycle_step(counter, carried):
        blocks, partial_grads, query_acc = carried
        partial_grads, query_acc = visit_block(blocks, partial_grads, query_acc)
        partial_grads = turn_grads(partial_grads)
        blocks = from_behind(blocks, "seq", 1)
        return (blocks, partial_grads, query_acc)

    blocks_start = jnp.stack([keys_all, values_all])
    blocks, partial_grads, query_acc = lax.fori_loop(
        0, lax.axis_size("seq") - 1, cycle_step, (blocks_start, grads_start, zero_heads)
    )
    partial_grads, query_acc = visit_block(blocks, partial_grads, query_acc)
    partial_grads = turn_grads(partial_grads)
    query_low = query_acc.astype(jnp.bfloat16).reshape(row_count, features) * factor
    key_low = partial_grads[0].astype(jnp.bfloat16).reshape(row_count, features)
    value_low = partial_grads[1].astype(jnp.bfloat16).reshape(row_count, features)
    proj_grad = jnp.concatenate([query_low, key_low, value_low], axis=1)
    qkv_grad = jnp.einsum("td,te->de", normed, proj_grad, preferred_element_type=jnp.float32)
    qv_bias_grad = jnp.stack(
        [
            jnp.sum(query_low.astype(jnp.float32), axis=0),
            jnp.sum(value_low.astype(jnp.float32), axis=0),
        ]
    )
    normed_grad = jnp.einsum("te,de->td", proj_grad, qkv_back, preferred_element_type=jnp.float32)
    _, pull_first = jax.vjp(normalize, stream_rows, gain_back[0], shift_full[0])
    stream_part, gain_one_grad, shift_one_grad = pull_first(normed_grad)
    stream_grad = (middle_grad + stream_part).reshape(samples, patches, features)
    per_sample = jnp.sum(stream_grad, axis=1)
    lead_grad = jnp.sum(lead_value[:, None] * per_sample, axis=0)
    table_grad = jnp.dot(present.T, per_sample, precision=lax.Precision.HIGHEST)
    gain_grad = jnp.stack([gain_one_grad, gain_two_grad])
    shift_grad = jnp.stack([shift_one_grad, shift_two_grad])
    bias_grad = jnp.stack([out_bias_grad, down_bias_grad])
    owned = (
        lax.psum_scatter(table_grad, ("samp", "seq"), scatter_dimension=1, tiled=True),
        lax.psum_scatter(lead_grad, ("samp", "seq"), scatter_dimension=0, tiled=True),
        lax.psum_scatter(gain_grad, ("samp", "seq"), scatter_dimension=1, tiled=True),
        lax.psum_scatter(shift_grad, ("samp", "seq"), scatter_dimension=1, tiled=True),
        lax.psum_scatter(qkv_grad, ("samp", "seq"), scatter_dimension=0, tiled=True),
        lax.psum_scatter(qv_bias_grad, ("samp", "seq"), scatter_dimension=1, tiled=True),
        lax.psum_scatter(out_grad, ("samp", "seq"), scatter_dimension=0, tiled=True),
        lax.psum_scatter(bias_grad, ("samp", "seq"), scatter_dimension=1, tiled=True),
        lax.psum_scatter(up_grad, ("samp", "seq"), scatter_dimension=0, tiled=True),
        lax.psum_scatter(up_bias_grad, ("samp", "seq"), scatter_dimension=0, tiled=True),
        lax.psum_scatter(down_grad, ("samp", "seq"), scatter_dimension=0, tiled=True),
    )
    return (
        mixed,
        stream_grad,
        owned[0],
        owned[1],
        owned[2],
        owned[3],
        owned[4],
        owned[5],
        owned[6],
        owned[7],
        owned[8],
        owned[9],
        owned[10],
    )


MESH = pl.DeviceIdType.MESH
BF = jnp.bfloat16
F32 = jnp.float32
D = 1024
ROWS = 128
LANES = 8
FFL = 512


def dot_nn(a, b):
    return lax.dot_general(a, b, (((1,), (0,)), ((), ())), preferred_element_type=F32)


def dot_nt(a, b):
    return lax.dot_general(a, b, (((1,), (1,)), ((), ())), preferred_element_type=F32)


def dot_tn(a, b):
    return lax.dot_general(a, b, (((0,), (0,)), ((), ())), preferred_element_type=F32)


def erf(v):
    v = jnp.clip(v, -4.0, 4.0)
    s = v * v
    p = jnp.full_like(s, -2.72614225801306e-10)
    for a in (2.77068142495902e-08, -2.10102402082508e-06, -5.69250639462346e-05,
              -7.34990630326855e-04, -2.95459980854025e-03, -1.60960333262415e-02):
        p = p * s + a
    q = jnp.full_like(s, -1.45660718464996e-05)
    for b in (-2.13374055278905e-04, -1.68282697438203e-03, -7.37332916720468e-03, -1.42647390514189e-02):
        q = q * s + b
    return v * p / q


def flip(a, d):
    return 1 - a if d else a


def many(n, m=1):
    return pl.ds(pl.multiple_of(n, m), m)


def center(v):
    mean = jnp.mean(v, axis=-1, keepdims=True)
    centred = v - mean
    var = jnp.mean(centred * centred, axis=-1, keepdims=True)
    rstd = lax.rsqrt(var + epsilon)
    return centred * rstd, rstd


def norm_back(xhat, rstd, gain, grad):
    dx = grad * gain
    return rstd * (dx - jnp.mean(dx, axis=-1, keepdims=True) - xhat * jnp.mean(dx * xhat, axis=-1, keepdims=True))


def fast_kernel(
    tokens_h, lead_hours_h, var_mask_h, var_table_h, lead_weight_h, norm_gain_h, norm_shift_h, wqkv_h, qv_bias_h, wout_h,
    branch_bias_h, wup_h, up_bias_h, wdown_h, cot_h,
    mixed_o, tg_o, gq_o, go_o, gu_o, gd_o, small_o,
    lead_hours, var_mask, var_table, lead_weight, norm_gain, norm_shift, qv_bias, branch_bias, up_bias,
    tokens, wqkv_in, wup_in, wout_in, cot, tok_all, cot_all, n2_all, ml_all,
    wqkv, wup, wdown, wout, raw, pack_in, pack_all, full,
    normed, q_s, k_s, v_s, shares, attf, att,
    rs_s1, rs_r1, rs_s2, rs_r2, own, kept,
    middle, mgrad, act, uplow, dproj, dog, dk_acc, dv_acc,
    gqkv, gup, gdown, gout, xqkv, xup, xdown, zqkv_s, zup_s, zdown_s, zqkv, zup, zdown,
    out_x, out_s, out_z, sq2, su2, rq2, ru2, so2, ro2,
    tgr, smallp, r_a, s_b, r_b, upb_g, r_upb,
    ss, rs, ls,
):
    s_i = lax.axis_index("samp")
    q_i = lax.axis_index("seq")
    y, x = s_i // 2, s_i % 2
    z, c = q_i // 2, q_i % 2
    k, w = z // 2, z % 2
    idx = 16 * y + 8 * x + 4 * k + 2 * w + c
    lane = 4 * y + 2 * w + c
    rank = 2 * x + k
    sample = 2 * k + x
    off_diag = y + k - 2 * y * k
    is_home = 1 - (x + w - 2 * x * w) - (k + c - 2 * k * c) + (x + w - 2 * x * w) * (k + c - 2 * k * c)
    my_rows = many(ROWS * lane, ROWS)

    def dev(y_, x_, k_, w_, c_):
        return (2 * y_ + x_, 4 * k_ + 2 * w_ + c_)

    count = [0, 0]
    items = []

    def sems(n):
        a, b = count
        count[0] += n
        count[1] += n
        return a, b

    def rc(src, dst, a, b, device):
        return pltpu.make_async_remote_copy(src_ref=src, dst_ref=dst, send_sem=ss.at[a], recv_sem=rs.at[b], device_id=device, device_id_type=MESH)

    group = [(d // 4, (d // 2) % 2, d % 2) for d in range(1, 8)]
    chips = [(0, 0), (0, 1), (1, 0), (1, 1)]
    ranks = [(0, 1), (1, 0), (1, 1)]

    def peer(d):
        dy, dw, dc = d
        y_, w_, c_ = flip(y, dy), flip(w, dw), flip(c, dc)
        return y_, w_, c_, 4 * y_ + 2 * w_ + c_, dev(y_, x, k, w_, c_)

    def partner(d):
        dx, dk = d
        x_, k_ = flip(x, dx), flip(k, dk)
        return x_, k_, 2 * x_ + k_, dev(y, x_, k_, w, c)

    swap_dev = dev(k, x, y, w, c)

    rank_rows = many(128 * rank, 128)
    barrier = pltpu.get_barrier_semaphore()
    for d in group:
        pl.semaphore_signal(barrier, inc=1, device_id=peer(d)[4], device_id_type=MESH)
    for d in ranks:
        pl.semaphore_signal(barrier, inc=1, device_id=partner(d)[3], device_id_type=MESH)

    @pl.when(off_diag == 1)
    def _():
        pl.semaphore_signal(barrier, inc=1, device_id=swap_dev, device_id_type=MESH)

    loads = [
        pltpu.make_async_copy(src, dst, ls.at[n])
        for n, (src, dst) in enumerate(((tokens_h, tokens), (wqkv_h, wqkv_in), (wup_h, wup_in), (wout_h, wout_in), (cot_h, cot), (wdown_h, wdown.at[rank_rows])))
    ]
    small_loads = [
        pltpu.make_async_copy(src, dst, ls.at[8 + n])
        for n, (src, dst) in enumerate((
            (lead_hours_h, lead_hours), (var_mask_h, var_mask), (var_table_h, var_table), (lead_weight_h, lead_weight),
            (norm_gain_h, norm_gain), (norm_shift_h, norm_shift), (qv_bias_h, qv_bias), (branch_bias_h, branch_bias), (up_bias_h, up_bias),
        ))
    ]
    for load in small_loads + loads:
        load.start()
    raw[...] = jnp.zeros_like(raw)
    for load in small_loads:
        load.wait()
    raw[0:48, 0:32] = var_table[...].astype(F32)
    for n, rows in ((48, norm_gain), (50, norm_shift), (52, qv_bias), (54, branch_bias)):
        raw[n : n + 2, 0:32] = rows[...].astype(F32)
    raw[56:57, 0:32] = lead_weight[...].astype(F32)
    raw[64:65, :] = up_bias[...].astype(F32)
    raw[65:66, 0:48] = var_mask[...].astype(F32)
    raw[65:66, 64:65] = lead_hours[...].astype(F32)
    packed = raw[0:16, :]
    for t in range(1, 4):
        packed = packed + pltpu.roll(raw[16 * t : 16 * t + 16, :], 32 * t, 1)
    pack_in[0:16, :] = packed.astype(BF)
    pack_in[16:32, :] = raw[64:80, :].astype(BF)
    for load in loads[:4]:
        load.wait()
    pl.semaphore_wait(barrier, 10 + off_diag)

    def begun(item):
        items.append(item)
        item.got = False

    class Swap:
        def __init__(self, src, dst):
            self.copy = rc(src, dst, *sems(1), swap_dev)

        def start(self):
            begun(self)
            pl.when(off_diag == 1)(self.copy.start)

        def wait(self):
            self.got = True
            pl.when(off_diag == 1)(self.copy.wait_recv)

        def drain(self):
            pl.when(off_diag == 1)(self.copy.wait_send)

    class Only:
        def __init__(self, sends, outgoing, takes, incoming):
            self.sends, self.outgoing, self.takes, self.incoming = sends, outgoing, takes, incoming

        def each(self, flag, copies, name):
            @pl.when(flag == 1)
            def _():
                for copy in copies:
                    getattr(copy, name)()

        def start(self):
            begun(self)
            self.each(self.sends, self.outgoing, "start")

        def wait(self):
            self.got = True
            self.each(self.takes, self.incoming, "wait_recv")

        def drain(self):
            self.each(self.sends, self.outgoing, "wait_send")

    def finish_all():
        for item in items:
            if not item.got:
                item.wait()
        for item in items:
            item.drain()

    y_nbr, w_nbr, sibling = dev(1 - y, x, k, w, c), dev(y, x, k, 1 - w, c), dev(y, x, k, w, 1 - c)
    UP, LOW = pl.ds(0, 64), pl.ds(64, 64)

    class Gather:
        def __init__(self, buf):
            self.buf = buf
            self.a, self.b = sems(10)

        def copy(self, n):
            ly, lw = 4 * (1 - y) + 2 * w + c, 4 * y + 2 * (1 - w) + c
            ld = 4 * (1 - y) + 2 * (1 - w) + c
            from_row, rows, device = (
                (ROWS * lane, 128, sibling),
                (ROWS * lane, 64, y_nbr), (ROWS * lane + 64, 64, y_nbr),
                (ROWS * lane + 64, 64, w_nbr), (ROWS * lane, 64, w_nbr),
                (ROWS * ly, 64, w_nbr), (ROWS * lw + 64, 64, y_nbr),
                (ROWS * ly, 128, sibling), (ROWS * lw, 128, sibling), (ROWS * ld, 128, sibling),
            )[n]
            ref = self.buf.at[pl.ds(pl.multiple_of(from_row, 64), rows)]
            return rc(ref, ref, self.a + n, self.b + n, device)

        def start(self):
            begun(self)
            self.passed = False
            for n in (1, 3, 2, 4, 0):
                self.copy(n).start()

        def pass_on(self):
            self.passed = True
            for n, then in ((1, 5), (3, 6), (2, 7), (4, 8), (5, None), (6, 9)):
                self.copy(n).wait_recv()
                if then is not None:
                    self.copy(then).start()

        def wait(self):
            if not self.passed:
                self.pass_on()
            self.got = True
            for n in (0, 7, 8, 9):
                self.copy(n).wait_recv()

        def drain(self):
            for n in range(10):
                self.copy(n).wait_send()

    class Scatter:
        def __init__(self, slot, partial):
            self.slot = slot
            self.partial = partial
            self.a1, self.b1 = sems(4)
            self.a2, self.b2 = sems(6)

        def far(self, i):
            dy, dw = i // 2, i % 2
            y_, w_ = y + dy - 2 * y * dy, w + dw - 2 * w * dw
            return y_, w_

        def first(self, i):
            return rc(rs_s1.at[self.slot, i], rs_r1.at[self.slot, i], self.a1 + i, self.b1 + i, sibling)

        def second(self, n):
            src, half, dst, half_there, device = (
                (2, UP, 2, UP, y_nbr), (2, LOW, 2, LOW, w_nbr),
                (0, UP, 0, UP, y_nbr), (1, LOW, 1, LOW, w_nbr),
                (0, LOW, 0, LOW, y_nbr), (1, UP, 1, UP, w_nbr),
            )[n]
            return rc(rs_s2.at[self.slot, src, half], rs_r2.at[self.slot, dst, half_there], self.a2 + n, self.b2 + n, device)

        def start(self, hold=False):
            begun(self)
            self.passed = False

            @pl.loop(0, 4)
            def _(n):
                i = 3 - n
                y_, w_ = self.far(i)
                rs_s1[self.slot, i] = self.partial(4 * y_ + 2 * w_ + 1 - c).astype(BF)
                self.first(i).start()

            def total(i):
                y_, w_ = self.far(i)
                part = self.partial(4 * y_ + 2 * w_ + c)
                self.first(i).wait_recv()
                return part + rs_r1[self.slot, i].astype(F32)

            rs_s2[self.slot, 2] = total(3).astype(BF)
            if not hold:
                self.second(0).start()
                self.second(1).start()
            value = total(2)
            rs_s2[self.slot, 0, 0:64] = value[0:64].astype(BF)
            if not hold:
                self.second(2).start()
            kept[self.slot, 0] = value[64:128]
            value = total(1)
            rs_s2[self.slot, 1, 64:128] = value[64:128].astype(BF)
            if not hold:
                self.second(3).start()
            kept[self.slot, 1] = value[0:64]
            own[self.slot] = total(0)

        def release(self):
            for n in range(4):
                self.second(n).start()

        def pass_on(self):
            self.passed = True
            self.second(0).wait_recv()
            rs_s2[self.slot, 1, 0:64] = (kept[self.slot, 1] + rs_r2[self.slot, 2, 0:64].astype(F32)).astype(BF)
            self.second(5).start()
            self.second(1).wait_recv()
            rs_s2[self.slot, 0, 64:128] = (kept[self.slot, 0] + rs_r2[self.slot, 2, 64:128].astype(F32)).astype(BF)
            self.second(4).start()

        def wait(self):
            if not self.passed:
                self.pass_on()
            self.got = True
            for n in (2, 3, 4, 5):
                self.second(n).wait_recv()
            return own[self.slot] + rs_r2[self.slot, 0].astype(F32) + rs_r2[self.slot, 1].astype(F32)

        def drain(self):
            for i in range(4):
                self.first(i).wait_send()
            for n in range(6):
                self.second(n).wait_send()

    class Batch:
        def __init__(self, copies):
            self.copies = copies
            self.a, self.b = sems(len(copies))

        def copy(self, n):
            src, dst, device = self.copies[n]
            return rc(src, dst, self.a + n, self.b + n, device)

        def start(self):
            begun(self)
            for n in range(len(self.copies)):
                self.copy(n).start()

        def wait(self):
            self.got = True
            for n in range(len(self.copies)):
                self.copy(n).wait_recv()

        def drain(self):
            for n in range(len(self.copies)):
                self.copy(n).wait_send()

    hx, hk = x + w - 2 * x * w, k + c - 2 * k * c
    z_dev, x_dev = partner((0, 1))[3], partner((1, 0))[3]

    class Across:
        def __init__(self, views):
            self.views = views
            self.n = len(views(x, k))
            self.a, self.b = sems(3 * self.n)

        def copies(self, leg):
            refs = self.views(x, 1 - k) if leg == 2 else self.views(x, k)
            at = self.n * leg
            return [rc(v, v, self.a + at + i, self.b + at + i, z_dev if leg == 0 else x_dev) for i, v in enumerate(refs)]

        def arrivals(self, leg):
            refs = self.views(*((x, 1 - k), (1 - x, k), (1 - x, 1 - k))[leg])
            at = self.n * leg
            return [rc(v, v, self.a + at + i, self.b + at + i, z_dev if leg == 0 else x_dev) for i, v in enumerate(refs)]

        def start(self):
            begun(self)
            self.passed = False
            for leg in (0, 1):
                for copy in self.copies(leg):
                    copy.start()

        def pass_on(self):
            self.passed = True
            for copy in self.arrivals(0):
                copy.wait_recv()
            for copy in self.copies(2):
                copy.start()

        def wait(self):
            if not self.passed:
                self.pass_on()
            self.got = True
            for leg in (1, 2):
                for copy in self.arrivals(leg):
                    copy.wait_recv()

        def drain(self):
            for leg in range(3):
                for copy in self.copies(leg):
                    copy.wait_send()

    class Reduce:
        def __init__(self, grad, rx, sz, rz):
            self.grad, self.rx, self.sz, self.rz = grad, rx, sz, rz
            self.runs = rx.shape[0]
            self.a, self.b = sems(self.runs + 1)

        def run(self, n):
            return rc(self.grad.at[many(512 * n + 256 * (1 - x), 256)], self.rx.at[n], self.a + n, self.b + n, x_dev)

        def last(self):
            return rc(self.sz, self.rz, self.a + self.runs, self.b + self.runs, z_dev)

        def start(self):
            begun(self)
            self.passed = False
            for n in range(self.runs):
                self.run(n).start()

        def part(self, n, k_):
            return (
                self.grad[many(512 * n + 256 * x + 128 * k_, 128), :].astype(F32)
                + self.rx[n, many(128 * k_, 128), :].astype(F32)
            )

        def pass_on(self):
            self.passed = True
            for n in range(self.runs):
                self.run(n).wait_recv()
            for n in range(self.runs):
                self.sz[n] = self.part(n, 1 - k).astype(BF)
            self.last().start()

        def wait(self):
            if not self.passed:
                self.pass_on()
            self.got = True
            self.last().wait_recv()

        def total(self, n):
            return self.part(n, k) + self.rz[n].astype(F32)

        def drain(self):
            for n in range(self.runs):
                self.run(n).wait_send()
            self.last().wait_send()

    swap_rows = many(ROWS * (4 * k + 2 * w + c), ROWS)
    tok_swap = Swap(tokens, tok_all.at[swap_rows])
    cot_swap = Swap(cot, cot_all.at[swap_rows])
    tok_swap.start()
    own_rows = many(32 * idx, 32)

    def up_cols(r, y_, w_, c_):
        return many(128 * (16 * y_ + 8 * (r // 2) + 4 * (r % 2) + 2 * w_ + c_), 128)

    copies = []
    for d in group:
        y_, w_, c_, l_, dv = peer(d)
        copies.append((pack_in, pack_all.at[idx], dv))
        for p in range(3):
            copies.append((wqkv_in.at[:, many(128 * (8 * p + l_), 128)], wqkv.at[own_rows, pl.ds(128 * p, 128)], dv))
    in_qkv = Batch(copies)
    in_qkv.start()

    out_a, out_b = sems(4)
    place = 2 * w + c
    out_rows = many(32 * place, 32)
    home_dev = dev(y, x, k, x, k)
    pairs = ((0, 1), (1, 0), (1, 1))
    away = 1 - is_home
    out_in = []
    for dw, dc in pairs:
        m = 2 * flip(w, dw) + flip(c, dc)
        out_in.append(rc(wout_in, wout.at[many(32 * m, 32)], out_a, out_b + m, home_dev))
    to_home = Only(away, [rc(wout_in, wout.at[out_rows], out_a, out_b + place, home_dev)], is_home, out_in)
    copies = []
    for d in group:
        y_, w_, c_, l_, dv = peer(d)
        for r in range(4):
            copies.append((wup_in.at[:, up_cols(r, y_, w_, c_)], wup.at[own_rows, pl.ds(128 * r, 128)], dv))
    in_up = Batch(copies)
    in_up.start()
    to_home.start()

    @pl.when(off_diag == 0)
    def _():
        tok_all[my_rows, :] = tokens[...]

    pack_all[idx] = pack_in[...]
    for p in range(3):
        wqkv[own_rows, 128 * p : 128 * p + 128] = wqkv_in[:, many(128 * (8 * p + lane), 128)]
    for r in range(4):
        wup[own_rows, 128 * r : 128 * r + 128] = wup_in[:, up_cols(r, y, w, c)]

    @pl.when(is_home == 1)
    def _():
        wout[out_rows, :] = wout_in[...]

    for load in loads[4:]:
        load.wait()

    @pl.when(off_diag == 0)
    def _():
        cot_all[my_rows, :] = cot[...]

    def runs_of(ref, *more):
        def views(x_, k_):
            refs = [more[0].at[pl.ds(16 * y_ + 8 * x_ + 4 * k_, 4)] for y_ in range(2)] if more else []
            return refs + [ref.at[many(512 * y_ + 256 * x_ + 128 * k_, 128)] for y_ in range(2)]

        return views

    dp_qkv = Across(runs_of(wqkv, pack_all))
    dp_up = Across(runs_of(wup))
    dp_down = Across(lambda x_, k_: [wdown.at[many(128 * (2 * x_ + k_), 128)]])
    in_qkv.wait()
    dp_qkv.start()
    tok_swap.wait()
    tok = Gather(tok_all)
    tok.start()
    cot_swap.start()

    dpo_a, dpo_b = sems(2)
    out_z_copy = rc(wout, wout, dpo_a, dpo_b, z_dev)
    out_x_copy = rc(wout, wout, dpo_a + 1, dpo_b + 1, x_dev)
    dp_out = Only(is_home, [out_z_copy, out_x_copy], (1 - hx) * hk, [out_z_copy])
    dp_out_more = Only((1 - hx) * hk, [out_x_copy], hx, [out_x_copy])
    to_home.wait()
    in_up.wait()
    dp_qkv.pass_on()
    dp_out.start()
    dp_up.start()
    tok.pass_on()

    dp_qkv.wait()
    lane_id = lax.broadcasted_iota(jnp.int32, (16, 128), 1)
    for b in range(8):
        for t in range(4):
            block = None
            for m in range(4):
                piece = pack_all[4 * b + m].astype(F32)[0:16, :]
                shift = (32 * (m - t)) % 128
                if shift:
                    piece = pltpu.roll(piece, shift, 1)
                block = piece if block is None else jnp.where(lane_id // 32 == m, piece, block)
            full[16 * t : 16 * t + 16, 128 * b : 128 * b + 128] = block

    gain0, gain1 = full[48:49, :], full[49:50, :]
    shift0, shift1 = full[50:51, :], full[51:52, :]
    lane_cols = many(128 * lane, 128)
    bias_q, bias_v = full[52:53, lane_cols], full[53:54, lane_cols]
    bias_out, bias_down = full[54:55, :], full[55:56, :]
    bias_up = jnp.concatenate(
        [pack_all[16 * y + 8 * (r // 2) + 4 * (r % 2) + 2 * w + c].astype(F32)[16:17, :] for r in range(4)], axis=1
    )
    facts = pack_all[8 * sample].astype(F32)[17:18, :]
    one_lane = lax.broadcasted_iota(jnp.int32, (1, 128), 1)
    present = jnp.where(one_lane < 64, facts, 0.0)
    hours = jnp.sum(jnp.where(one_lane == 64, facts, 0.0), axis=-1, keepdims=True) * hours_scale
    present8 = jnp.broadcast_to(present, (8, 128))[:, :64].astype(BF)
    extra = dot_nn(present8, full[...].astype(BF))[0:1, :] + hours * full[56:57, :]

    tok.wait()

    @pl.loop(0, 8)
    def _(n):
        rows = many(128 * n, 128)
        xhat, _ = center(tok_all[rows, :].astype(F32) + extra)
        normed[rows, :] = (xhat * gain0 + shift0).astype(BF)

    @pl.loop(0, 4)
    def _(n):
        rows = many(256 * n, 256)
        proj = dot_nn(normed[rows, :], wqkv[...])
        q_s[rows, :] = ((proj[:, :128] + bias_q) * 0.125).astype(BF)
        k_s[rows, :] = proj[:, 128:256].astype(BF)
        v_s[rows, :] = (proj[:, 256:384] + bias_v).astype(BF)

    QB = 256
    cot_swap.wait()
    cg = Gather(cot_all)
    cg.start()
    dp_down.start()
    dp_out.wait()
    dp_out_more.start()
    head_lane = lax.broadcasted_iota(jnp.int32, (1, 128), 1) // 64

    def of_head(v, h):
        return jnp.where(head_lane == h, v, jnp.zeros_like(v))

    @pl.loop(0, D // QB)
    def _(n):
        rows = many(QB * n, QB)
        queries = q_s[rows, :]
        total = None
        for h in range(2):
            scores = dot_nt(of_head(queries, h), k_s[...])
            top = jnp.max(scores, axis=-1, keepdims=True)
            e = jnp.exp(scores - top)
            share = (e * (1.0 / jnp.sum(e, axis=-1, keepdims=True))).astype(BF)
            shares[h, rows, :] = share
            got = of_head(dot_nn(share, v_s[...]), h)
            total = got if total is None else total + got
        attf[rows, :] = total
        att[rows, :] = total.astype(BF)

    dp_out_more.wait()

    def rows_of(l_):
        return many(ROWS * l_, ROWS)

    rs_out = Scatter(0, lambda l_: dot_nn(att[rows_of(l_), :], wout[...]))
    rs_out.start()
    rs_out.pass_on()

    cg.pass_on()
    dp_up.pass_on()

    stream = tok_all[my_rows, :].astype(F32) + extra
    mid = stream + (rs_out.wait() + bias_out)
    middle[...] = mid
    xhat2, rstd2 = center(mid)
    n2_all[my_rows, :] = (xhat2 * gain1 + shift1).astype(BF)
    n2 = Gather(n2_all)
    n2.start()
    dp_down.pass_on()
    n2.pass_on()
    dp_up.wait()
    dp_down.wait()
    cg.wait()
    n2.wait()

    upb_g[...] = jnp.zeros_like(upb_g)

    @pl.loop(0, 4)
    def _(n):
        rows = many(256 * n, 256)
        up = dot_nn(n2_all[rows, :], wup[...]) + bias_up
        cdf = 0.5 * (1.0 + erf(up * 0.7071067811865476))
        act[rows, :] = (up * cdf).astype(BF)
        slope = cdf + up * (jnp.exp(-0.5 * up * up) * 0.3989422804014327)
        low = (dot_nt(cot_all[rows, :], wdown[...]) * slope).astype(BF)
        uplow[rows, :] = low
        upb_g[0:1, :] += jnp.sum(low.astype(F32), axis=0, keepdims=True)

    rs_n2 = Scatter(1, lambda l_: dot_nt(uplow[rows_of(l_), :], wup[...]))
    rs_n2.start()

    @pl.loop(0, 4)
    def _(r):
        cols = many(128 * r, 128)
        gdown[cols, :] = dot_tn(act[:, cols], cot_all[...]).astype(BF)

    down_red = Reduce(gdown, xdown, zdown_s, zdown)
    down_red.start()
    rs_n2.pass_on()
    upb_sends = Batch([(upb_g.at[:, many(128 * partner(d)[2], 128)], r_upb.at[n], partner(d)[3]) for n, d in enumerate(ranks)])
    upb_sends.start()

    @pl.loop(0, 4)
    def _(n):
        cols = many(256 * n, 256)
        gup[cols, :] = dot_tn(n2_all[:, cols], uplow[...]).astype(BF)

    up_red = Reduce(gup, xup, zup_s, zup)
    up_red.start()

    rs_mix = Scatter(2, lambda l_: dot_nn(act[rows_of(l_), :], wdown[...]))
    rs_mix.start()
    n2_grad = rs_n2.wait()
    incoming = cot_all[my_rows, :].astype(F32)
    xhat2, rstd2 = center(middle[...])
    mg = incoming + norm_back(xhat2, rstd2, gain1, n2_grad)
    mgrad[...] = mg
    ml_all[my_rows, :] = mg.astype(BF)
    ml = Gather(ml_all)
    ml.start()
    rs_mix.pass_on()
    smallp[7:16, :] = jnp.zeros((9, D), F32)
    smallp[2:3, :] = jnp.sum(n2_grad * xhat2, axis=0, keepdims=True)
    smallp[4:5, :] = jnp.sum(n2_grad, axis=0, keepdims=True)
    smallp[5:6, :] = jnp.sum(mg.astype(BF).astype(F32), axis=0, keepdims=True)
    smallp[6:7, :] = jnp.sum(incoming, axis=0, keepdims=True)

    down_red.pass_on()
    ml.pass_on()
    up_red.pass_on()
    ml.wait()
    mixed_low = (middle[...] + (rs_mix.wait() + bias_down)).astype(BF)
    tgr[2] = mixed_low
    mix_swap = Swap(tgr.at[2], tgr.at[3])
    mix_swap.start()

    @pl.loop(0, 4)
    def _(n):
        rows = many(256 * n, 256)
        dog[rows, :] = dot_nt(ml_all[rows, :], wout[...]).astype(BF)

    dk_acc[...] = jnp.zeros_like(dk_acc)
    dv_acc[...] = jnp.zeros_like(dv_acc)

    def attend_back(n):
        rows = many(QB * n, QB)
        queries = q_s[rows, :]
        grads = dog[rows, :]
        both = grads.astype(F32) * attf[rows, :]
        dq = None
        for h in range(2):
            share = shares[h, rows, :]
            pressure = dot_nt(of_head(grads, h), v_s[...])
            offset = jnp.sum(of_head(both, h), axis=-1, keepdims=True)
            ds = (share.astype(F32) * (pressure - offset)).astype(BF)
            got = of_head(dot_nn(ds, k_s[...]), h)
            dq = got if dq is None else dq + got
            dk_acc[...] += dot_tn(ds, of_head(queries, h))
            dv_acc[...] += dot_tn(share, of_head(grads, h))
        dproj[rows, 0:128] = (dq.astype(BF).astype(F32) * 0.125).astype(BF)

    pl.loop(0, 2)(attend_back)
    pl.loop(2, 4)(attend_back)
    dproj[:, 128:256] = dk_acc[...].astype(BF)
    dproj[:, 256:384] = dv_acc[...].astype(BF)

    @pl.loop(0, 4)
    def _(n):
        cols = many(256 * n, 256)
        gqkv[cols, :] = dot_tn(normed[:, cols], dproj[...]).astype(BF)

    qkv_red = Reduce(gqkv, xqkv, zqkv_s, zqkv)
    qkv_red.start()
    low = dproj[...].astype(F32)
    smallp[8:9, lane_cols] = jnp.sum(low[:, 0:128], axis=0, keepdims=True)
    smallp[9:10, lane_cols] = jnp.sum(low[:, 256:384], axis=0, keepdims=True)
    rs_n1 = Scatter(3, lambda l_: dot_nt(dproj[rows_of(l_), :], wqkv[...]))
    rs_n1.start()

    rs_n1.pass_on()
    gout[...] = dot_tn(att[...], ml_all[...]).astype(BF)
    go_a, go_b = sems(2)
    grad_x = Only(hx, [rc(gout, out_x, go_a, go_b, x_dev)], 1 - hx, [rc(gout, out_x, go_a, go_b, x_dev)])
    grad_z = Only((1 - hx) * hk, [rc(out_s, out_z, go_a + 1, go_b + 1, z_dev)], is_home, [rc(out_s, out_z, go_a + 1, go_b + 1, z_dev)])
    grad_x.start()
    qkv_red.pass_on()
    grad_x.wait()

    @pl.when(hx == 0)
    def _():
        out_s[...] = (gout[...].astype(F32) + out_x[...].astype(F32)).astype(BF)

    grad_z.start()

    n1_grad = rs_n1.wait()
    xhat1, rstd1 = center(tok_all[my_rows, :].astype(F32) + extra)
    tg = mgrad[...] + norm_back(xhat1, rstd1, gain0, n1_grad)
    tgr[0] = tg.astype(BF)
    smallp[0:1, :] = jnp.sum(tg, axis=0, keepdims=True)
    smallp[1:2, :] = jnp.sum(n1_grad * xhat1, axis=0, keepdims=True)
    smallp[3:4, :] = jnp.sum(n1_grad, axis=0, keepdims=True)

    def block(y_, x_, k_):
        return smallp.at[:, many(128 * (4 * y_ + 2 * x_ + k_), 128)]

    copies = []
    for n, d in enumerate(ranks):
        x_, k_, r_, dv = partner(d)
        for y_ in range(2):
            copies.append((block(y_, x_, k_), r_b.at[n, y_], dv))
    small_ranks = Batch(copies)
    small_ranks.start()
    tg_swap = Swap(tgr.at[0], tgr.at[1])
    tg_swap.start()
    small_ranks.wait()
    for y_ in range(2):
        first = smallp[:, many(128 * (4 * y_ + 2 * x + k), 128)]
        s_b[y_, 0:1, :] = first[0:1, :]
        for n in range(3):
            s_b[y_, n + 1 : n + 2, :] = r_b[n, y_, 0:1, :]
        s_b[y_, 4:16, :] = (first + r_b[0, y_] + r_b[1, y_] + r_b[2, y_])[1:13, :]
    small_group = Batch([(s_b.at[peer(d)[0]], r_a.at[n], peer(d)[4]) for n, d in enumerate(group)])
    small_group.start()

    down_red.wait()
    gd_o[...] = down_red.total(0).astype(BF)

    def deal(low_sum, recv):
        copies = []
        for n, d in enumerate(group):
            y_, w_, c_, l_, dv = peer(d)
            copies.append((low_sum.at[many(128 * y_ + 64 * w_ + 32 * c_, 32)], recv.at[lane], dv))
        return Batch(copies)

    def collect(red, low_sum, recv):
        red.wait()
        for y_ in range(2):
            low_sum[128 * y_ : 128 * y_ + 128, :] = red.total(y_).astype(BF)
        batch = deal(low_sum, recv)
        batch.start()
        recv[lane] = low_sum[many(128 * y + 64 * w + 32 * c, 32), :]
        return batch

    up_deal = collect(up_red, su2, ru2)
    grad_z.wait()

    @pl.when(is_home == 1)
    def _():
        so2[...] = (out_s[...].astype(F32) + out_z[...].astype(F32)).astype(BF)
        go_o[...] = so2[out_rows, :]

    outs_a, outs_b = sems(3)
    copies = []
    for n, (dw, dc) in enumerate(pairs):
        w_, c_ = flip(w, dw), flip(c, dc)
        copies.append(rc(so2.at[many(32 * (2 * w_ + c_), 32)], ro2, outs_a + n, outs_b, dev(y, x, k, w_, c_)))
    out_deal = Only(is_home, copies, away, [rc(so2.at[pl.ds(0, 32)], ro2, outs_a, outs_b, home_dev)])
    out_deal.start()
    qkv_deal = collect(qkv_red, sq2, rq2)

    small_group.wait()
    total = s_b[y]
    for n in range(7):
        total = total + r_a[n]
    own_facts = [facts] + [pack_all[8 * (2 * partner(d)[1] + partner(d)[0])].astype(F32)[17:18, :] for d in ranks]
    facts_t = jnp.transpose(jnp.concatenate(own_facts + [jnp.zeros((4, 128), F32)], axis=0))
    table = None
    for n in range(4):
        part = facts_t[:, n : n + 1] * total[n : n + 1, :]
        table = part if table is None else table + part
    small_o[0:64, :] = table[0:64, :]
    small_o[64:80, :] = total
    small_o[80:81, :] = table[64:65, :] * hours_scale
    small_o[81:88, :] = jnp.zeros((7, 128), F32)
    upb_sends.wait()
    sum_upb = upb_g[:, rank_rows]
    for n in range(3):
        sum_upb = sum_upb + r_upb[n]
    small_o[88:96, :] = sum_upb

    out_deal.wait()

    @pl.when(is_home == 0)
    def _():
        go_o[...] = ro2[...]

    @pl.when(off_diag == 0)
    def _():
        tg_o[...] = tgr[0]
        mixed_o[...] = tgr[2]

    mix_swap.wait()
    tg_swap.wait()

    @pl.when(off_diag == 1)
    def _():
        tg_o[...] = tgr[1]
        mixed_o[...] = tgr[3]

    up_deal.wait()
    gu_o[...] = ru2[...]
    qkv_deal.wait()
    gq_o[...] = rq2[...]

    finish_all()


def finish_kernel(
    mixed_i, tg_i, gq_i, go_i, gu_i, gd_i, small_i,
    mixed_o, tg_o, table_o, lead_o, gain_o, shift_o, gq_o, qv_o, go_o, bias_o, gu_o, upb_o, gd_o,
):
    mixed_o[0] = mixed_i[...]
    tg_o[0] = tg_i[...].astype(F32)
    gd_o[...] = gd_i[...].astype(F32)
    go_o[...] = go_i[...].astype(F32)
    for l_ in range(8):
        part = gu_i[l_].astype(F32)
        y_, w_, c_ = l_ // 4, (l_ // 2) % 2, l_ % 2
        for r in range(4):
            at = 128 * (16 * y_ + 8 * (r // 2) + 4 * (r % 2) + 2 * w_ + c_)
            gu_o[:, at : at + 128] = part[:, 128 * r : 128 * r + 128]
        part = gq_i[l_].astype(F32)
        for p in range(3):
            at = 128 * (8 * p + l_)
            gq_o[:, at : at + 128] = part[:, 128 * p : 128 * p + 128]
    place = lax.rem(lax.axis_index("seq"), 4)
    small = small_i[0:88, :]
    mine = small
    for m in range(1, 4):
        mine = jnp.where(place == m, pltpu.roll(small, 128 - 32 * m, 1), mine)
    table_o[...] = mine[0:48, 0:32]
    gain_o[...] = mine[68:70, 0:32]
    shift_o[...] = mine[70:72, 0:32]
    bias_o[...] = mine[72:74, 0:32]
    qv_o[...] = mine[75:77, 0:32]
    lead_o[...] = mine[80:81, 0:32]
    upb_o[...] = small_i[88:89, :]


def local_fast(
    tokens, lead_hours, var_mask, var_table, lead_weight, norm_gain, norm_shift, w_qkv, qv_bias, w_out,
    branch_bias, w_up, up_bias, w_down, cotangent,
):
    vm = pltpu.VMEM
    scratch = [
        vm((1, 1), jnp.int32), vm((1, 48), jnp.int32), vm((48, 32), BF), vm((1, 32), BF), vm((2, 32), BF), vm((2, 32), BF),
        vm((2, 32), BF), vm((2, 32), BF), vm((1, 128), BF),
        vm((128, D), BF), vm((32, 3 * D), BF), vm((32, 4 * D), BF), vm((32, D), BF), vm((128, D), BF),
        vm((D, D), BF), vm((D, D), BF), vm((D, D), BF), vm((D, D), BF),
        vm((D, 384), BF), vm((D, FFL), BF), vm((FFL, D), BF), vm((128, D), BF), vm((80, 128), F32), vm((32, 128), BF), vm((32, 32, 128), BF), vm((64, D), F32),
        vm((D, D), BF), vm((D, 128), BF), vm((D, 128), BF), vm((D, 128), BF), vm((2, D, D), BF), vm((D, 128), F32), vm((D, 128), BF),
        vm((4, 4, 128, D), BF), vm((4, 4, 128, D), BF), vm((4, 3, 128, D), BF), vm((4, 3, 128, D), BF), vm((4, 128, D), F32), vm((4, 2, 64, D), F32),
        vm((128, D), F32), vm((128, D), F32), vm((D, FFL), BF), vm((D, FFL), BF), vm((D, 384), BF), vm((D, 128), BF), vm((D, 128), F32), vm((D, 128), F32),
        vm((D, 384), BF), vm((D, FFL), BF), vm((FFL, D), BF), vm((128, D), BF),
        vm((2, 256, 384), BF), vm((2, 256, FFL), BF), vm((1, 256, D), BF),
        vm((2, 128, 384), BF), vm((2, 128, FFL), BF), vm((1, 128, D), BF),
        vm((2, 128, 384), BF), vm((2, 128, FFL), BF), vm((1, 128, D), BF),
        vm((128, D), BF), vm((128, D), BF), vm((128, D), BF),
        vm((256, 384), BF), vm((256, FFL), BF), vm((8, 32, 384), BF), vm((8, 32, FFL), BF), vm((128, D), BF), vm((32, D), BF),
        vm((4, 128, D), BF), vm((16, D), F32), vm((7, 16, 128), F32), vm((2, 16, 128), F32), vm((3, 2, 16, 128), F32),
        vm((8, FFL), F32), vm((3, 8, 128), F32),
        pltpu.SemaphoreType.DMA((320,)), pltpu.SemaphoreType.DMA((320,)), pltpu.SemaphoreType.DMA((24,)),
    ]
    shape = jax.ShapeDtypeStruct
    raw = pl.pallas_call(
        fast_kernel,
        out_shape=[
            shape((128, D), BF), shape((128, D), BF), shape((8, 32, 384), BF), shape((32, D), BF), shape((8, 32, FFL), BF),
            shape((128, D), BF), shape((96, 128), F32),
        ],
        in_specs=[pl.BlockSpec(memory_space=pl.ANY)] * 15,
        out_specs=[pl.BlockSpec(memory_space=vm)] * 7,
        scratch_shapes=scratch,
        compiler_params=pltpu.CompilerParams(collective_id=0, has_side_effects=True, vmem_limit_bytes=62 * 2**20),
        cost_estimate=pl.CostEstimate(flops=14_000_000_000, bytes_accessed=4_000_000, transcendentals=6_000_000),
    )(
        tokens[0], lead_hours[None], var_mask, var_table, lead_weight[None], norm_gain, norm_shift, w_qkv, qv_bias, w_out,
        branch_bias, w_up, up_bias[None], w_down, cotangent[0],
    )
    out = pl.pallas_call(
        finish_kernel,
        out_shape=[
            shape((1, 128, D), BF), shape((1, 128, D), F32), shape((48, 32), F32), shape((1, 32), F32), shape((2, 32), F32),
            shape((2, 32), F32), shape((32, 3 * D), F32), shape((2, 32), F32), shape((32, D), F32), shape((2, 32), F32),
            shape((32, 4 * D), F32), shape((1, 128), F32), shape((128, D), F32),
        ],
        in_specs=[pl.BlockSpec(memory_space=vm)] * 7,
        out_specs=[pl.BlockSpec(memory_space=vm)] * 13,
        compiler_params=pltpu.CompilerParams(vmem_limit_bytes=62 * 2**20),
        cost_estimate=pl.CostEstimate(flops=1_000_000, bytes_accessed=4_000_000, transcendentals=0),
    )(*raw)
    mixed, tg, table, lead, gain, shift, gq, qv, go, bias, gu, upb, gd = out
    return (mixed, tg, table, lead[0], gain, shift, gq, qv, go, bias, gu, upb[0], gd)


def solution(mesh):
    sizes = dict(mesh.shape)
    fast = sizes == {"samp": 4, "seq": 8}
    return jax.shard_map(
        local_fast if fast else local,
        mesh=mesh,
        in_specs=(
            P("samp", "seq", None),
            P("samp"),
            P("samp", None),
            P(None, ("samp", "seq")),
            P(("samp", "seq")),
            P(None, ("samp", "seq")),
            P(None, ("samp", "seq")),
            P(("samp", "seq"), None),
            P(None, ("samp", "seq")),
            P(("samp", "seq"), None),
            P(None, ("samp", "seq")),
            P(("samp", "seq"), None),
            P(("samp", "seq")),
            P(("samp", "seq"), None),
            P("samp", "seq", None),
        ),
        out_specs=(
            P("samp", "seq", None),
            P("samp", "seq", None),
            P(None, ("samp", "seq")),
            P(("samp", "seq")),
            P(None, ("samp", "seq")),
            P(None, ("samp", "seq")),
            P(("samp", "seq"), None),
            P(None, ("samp", "seq")),
            P(("samp", "seq"), None),
            P(None, ("samp", "seq")),
            P(("samp", "seq"), None),
            P(("samp", "seq")),
            P(("samp", "seq"), None),
        ),
        check_vma=False,
    )
```

```python
import jax
import jax.numpy as jnp
from jax import lax
from jax.experimental import pallas as pl
from jax.experimental.pallas import tpu as pltpu
from jax.sharding import PartitionSpec as P

HEADS = 16
HEAD_DIM = 64


epsilon = 1e-05
hours_scale = 1.0 / 168.0


def from_behind(block, axis, distance):
    devices = range(lax.axis_size(axis))
    route = [((i - distance) % len(devices), i) for i in devices]
    return lax.ppermute(block, axis, route)


def normalize(field, scaling, offsets):
    average = jnp.mean(field, axis=-1, keepdims=True)
    centred = field - average
    variance = jnp.mean(centred * centred, axis=-1, keepdims=True)
    return centred * lax.rsqrt(variance + epsilon) * scaling + offsets


def block_size(length):
    size_now = length
    while size_now > 512 and size_now % 2 == 0:
        size_now = size_now // 2
    return size_now


def over_blocks(advance, carried, segments):
    length = segments[0].shape[1]
    size_now = block_size(length)
    number = length // size_now
    stacked = tuple(
        (
            jnp.moveaxis(
                segment.reshape(segment.shape[0], number, size_now, segment.shape[2]), 1, 0
            )
            for segment in segments
        )
    )

    def visit(current, blocks):
        return (advance(current, blocks), None)

    carried, _ = lax.scan(visit, carried, stacked)
    return carried


def split_heads(matrix):
    return matrix.reshape(matrix.shape[0], matrix.shape[1], HEADS, HEAD_DIM)


def gelu_slope(upward):
    normal_cdf = 0.5 * (1.0 + lax.erf(upward * 0.7071067811865476))
    density = jnp.exp(-0.5 * upward * upward) * 0.3989422804014327
    return normal_cdf + upward * density


def pair_terms(query_heads, grad_heads, log_total, offset, key_heads, value_heads):
    scores = jnp.einsum(
        "sqhd,skhd->shqk", query_heads, key_heads, preferred_element_type=jnp.float32
    )
    shares = jnp.exp(scores - log_total[..., None])
    pressure = jnp.einsum(
        "sqhd,skhd->shqk", grad_heads, value_heads, preferred_element_type=jnp.float32
    )
    score_grad = (shares * (pressure - offset[..., None])).astype(jnp.bfloat16)
    query_part = jnp.einsum(
        "shqk,skhd->sqhd", score_grad, key_heads, preferred_element_type=jnp.float32
    )
    key_part = jnp.einsum(
        "shqk,sqhd->skhd", score_grad, query_heads, preferred_element_type=jnp.float32
    )
    value_part = jnp.einsum(
        "shqk,sqhd->skhd",
        shares.astype(jnp.bfloat16),
        grad_heads,
        preferred_element_type=jnp.float32,
    )
    return (query_part, key_part, value_part)


def local(
    tokens,
    lead_hours,
    var_mask,
    var_table,
    lead_weight,
    norm_gain,
    norm_shift,
    w_qkv,
    qv_bias,
    w_out,
    branch_bias,
    w_up,
    up_bias,
    w_down,
    cotangent,
):
    samples, patches, features = tokens.shape
    row_count = samples * patches
    factor = HEAD_DIM ** (-0.5)
    (
        table_full,
        lead_full,
        gain_all,
        shift_all,
        qkv_full,
        qv_all,
        out_full,
        bias_all,
        up_full,
        upb_full,
        down_full,
    ) = (
        lax.all_gather(var_table, ("samp", "seq"), axis=1, tiled=True),
        lax.all_gather(lead_weight, ("samp", "seq"), axis=0, tiled=True),
        lax.all_gather(norm_gain, ("samp", "seq"), axis=1, tiled=True),
        lax.all_gather(norm_shift, ("samp", "seq"), axis=1, tiled=True),
        lax.all_gather(w_qkv, ("samp", "seq"), axis=0, tiled=True),
        lax.all_gather(qv_bias, ("samp", "seq"), axis=1, tiled=True),
        lax.all_gather(w_out, ("samp", "seq"), axis=0, tiled=True),
        lax.all_gather(branch_bias, ("samp", "seq"), axis=1, tiled=True),
        lax.all_gather(w_up, ("samp", "seq"), axis=0, tiled=True),
        lax.all_gather(up_bias, ("samp", "seq"), axis=0, tiled=True),
        lax.all_gather(w_down, ("samp", "seq"), axis=0, tiled=True),
    )
    gain_full = gain_all.astype(jnp.float32)
    shift_full = shift_all.astype(jnp.float32)
    qv_full = qv_all.astype(jnp.float32)
    bias_full = bias_all.astype(jnp.float32)
    lead_value = lead_hours.astype(jnp.float32) * hours_scale
    present = var_mask.astype(jnp.float32)
    variable_sum = jnp.dot(present, table_full.astype(jnp.float32), precision=lax.Precision.HIGHEST)
    stream = (
        tokens.astype(jnp.float32)
        + lead_value[:, None, None] * lead_full.astype(jnp.float32)
        + variable_sum[:, None, :]
    )
    stream_rows = stream.reshape(row_count, features)
    normed = normalize(stream_rows, gain_full[0], shift_full[0]).astype(jnp.bfloat16)
    projected = jnp.dot(normed, qkv_full, preferred_element_type=jnp.float32)
    queries = (
        ((projected[:, :features] + qv_full[0]) * factor)
        .astype(jnp.bfloat16)
        .reshape(samples, patches, features)
    )
    keys_all = (
        projected[:, features : 2 * features]
        .astype(jnp.bfloat16)
        .reshape(samples, patches, features)
    )
    values_all = (
        (projected[:, 2 * features :] + qv_full[1])
        .astype(jnp.bfloat16)
        .reshape(samples, patches, features)
    )
    query_heads = split_heads(queries)

    def scores_of(keys_block):
        return jnp.einsum(
            "sqhd,skhd->shqk",
            query_heads,
            split_heads(keys_block),
            preferred_element_type=jnp.float32,
        )

    def stats_step(carried, blocks):
        running_max, running_sum = carried
        scores = scores_of(blocks[0])
        new_max = jnp.maximum(running_max, jnp.max(scores, axis=-1))
        running_sum = running_sum * jnp.exp(running_max - new_max) + jnp.sum(
            jnp.exp(scores - new_max[..., None]), axis=-1
        )
        return (new_max, running_sum)

    stats_start = (
        jnp.full((samples, HEADS, patches), -jnp.inf, jnp.float32),
        jnp.zeros((samples, HEADS, patches), jnp.float32),
    )
    running_max, running_sum = over_blocks(
        stats_step, stats_start, (lax.all_gather(keys_all, "seq", axis=1, tiled=True),)
    )
    log_total = running_max + jnp.log(running_sum)

    def mix_step(collected, blocks):
        shares = jnp.exp(scores_of(blocks[0]) - log_total[..., None]).astype(jnp.bfloat16)
        return collected + jnp.einsum(
            "shqk,skhd->sqhd", shares, split_heads(blocks[1]), preferred_element_type=jnp.float32
        )

    zero_heads = jnp.zeros((samples, patches, HEADS, HEAD_DIM), jnp.float32)
    attended_f = over_blocks(
        mix_step,
        zero_heads,
        (
            lax.all_gather(keys_all, "seq", axis=1, tiled=True),
            lax.all_gather(values_all, "seq", axis=1, tiled=True),
        ),
    )
    attended = attended_f.reshape(row_count, features).astype(jnp.bfloat16)
    middle = stream_rows + (
        jnp.dot(attended, out_full, preferred_element_type=jnp.float32) + bias_full[0]
    )
    normed_two = normalize(middle, gain_full[1], shift_full[1]).astype(jnp.bfloat16)
    upward = jnp.dot(normed_two, up_full, preferred_element_type=jnp.float32) + upb_full.astype(
        jnp.float32
    )
    activated = jax.nn.gelu(upward, approximate=False).astype(jnp.bfloat16)
    downward = jnp.dot(activated, down_full, preferred_element_type=jnp.float32) + bias_full[1]
    mixed = (middle + downward).astype(jnp.bfloat16).reshape(samples, patches, features)
    gain_back, qkv_back, out_back, up_back, down_back = (
        lax.all_gather(norm_gain, ("samp", "seq"), axis=1, tiled=True),
        lax.all_gather(w_qkv, ("samp", "seq"), axis=0, tiled=True),
        lax.all_gather(w_out, ("samp", "seq"), axis=0, tiled=True),
        lax.all_gather(w_up, ("samp", "seq"), axis=0, tiled=True),
        lax.all_gather(w_down, ("samp", "seq"), axis=0, tiled=True),
    )
    gain_back = gain_back.astype(jnp.float32)
    incoming = cotangent.astype(jnp.float32).reshape(row_count, features)
    incoming_low = incoming.astype(jnp.bfloat16)
    down_grad = jnp.einsum("tf,td->fd", activated, incoming_low, preferred_element_type=jnp.float32)
    down_bias_grad = jnp.sum(incoming_low.astype(jnp.float32), axis=0)
    gelu_grad = jnp.einsum(
        "td,fd->tf", incoming_low, down_back, preferred_element_type=jnp.float32
    ) * gelu_slope(upward)
    up_low = gelu_grad.astype(jnp.bfloat16)
    up_grad = jnp.einsum("td,tf->df", normed_two, up_low, preferred_element_type=jnp.float32)
    up_bias_grad = jnp.sum(up_low.astype(jnp.float32), axis=0)
    normed_two_grad = jnp.einsum("tf,df->td", up_low, up_back, preferred_element_type=jnp.float32)
    _, pull_second = jax.vjp(normalize, middle, gain_back[1], shift_full[1])
    middle_part, gain_two_grad, shift_two_grad = pull_second(normed_two_grad)
    middle_grad = incoming + middle_part
    middle_low = middle_grad.astype(jnp.bfloat16)
    out_grad = jnp.einsum("te,td->ed", attended, middle_low, preferred_element_type=jnp.float32)
    out_bias_grad = jnp.sum(middle_low.astype(jnp.float32), axis=0)
    attended_grad = jnp.einsum(
        "td,ed->te", middle_low, out_back, preferred_element_type=jnp.float32
    ).astype(jnp.bfloat16)
    grad_rows = attended_grad.reshape(samples, patches, features)
    grad_heads = split_heads(grad_rows)
    offset = jnp.transpose(jnp.sum(grad_heads.astype(jnp.float32) * attended_f, axis=-1), (0, 2, 1))
    grads_start = jnp.zeros((2, samples, patches, HEADS, HEAD_DIM), jnp.float32)

    def visit_block(blocks, partial_grads, query_acc):
        query_part, key_part, value_part = pair_terms(
            query_heads,
            grad_heads,
            log_total,
            offset,
            split_heads(blocks[0]),
            split_heads(blocks[1]),
        )
        return (partial_grads + jnp.stack([key_part, value_part]), query_acc + query_part)

    def turn_grads(partial_grads):
        return from_behind(partial_grads.astype(jnp.bfloat16), "seq", 1).astype(partial_grads.dtype)

    def cycle_step(counter, carried):
        blocks, partial_grads, query_acc = carried
        partial_grads, query_acc = visit_block(blocks, partial_grads, query_acc)
        partial_grads = turn_grads(partial_grads)
        blocks = from_behind(blocks, "seq", 1)
        return (blocks, partial_grads, query_acc)

    blocks_start = jnp.stack([keys_all, values_all])
    blocks, partial_grads, query_acc = lax.fori_loop(
        0, lax.axis_size("seq") - 1, cycle_step, (blocks_start, grads_start, zero_heads)
    )
    partial_grads, query_acc = visit_block(blocks, partial_grads, query_acc)
    partial_grads = turn_grads(partial_grads)
    query_low = query_acc.astype(jnp.bfloat16).reshape(row_count, features) * factor
    key_low = partial_grads[0].astype(jnp.bfloat16).reshape(row_count, features)
    value_low = partial_grads[1].astype(jnp.bfloat16).reshape(row_count, features)
    proj_grad = jnp.concatenate([query_low, key_low, value_low], axis=1)
    qkv_grad = jnp.einsum("td,te->de", normed, proj_grad, preferred_element_type=jnp.float32)
    qv_bias_grad = jnp.stack(
        [
            jnp.sum(query_low.astype(jnp.float32), axis=0),
            jnp.sum(value_low.astype(jnp.float32), axis=0),
        ]
    )
    normed_grad = jnp.einsum("te,de->td", proj_grad, qkv_back, preferred_element_type=jnp.float32)
    _, pull_first = jax.vjp(normalize, stream_rows, gain_back[0], shift_full[0])
    stream_part, gain_one_grad, shift_one_grad = pull_first(normed_grad)
    stream_grad = (middle_grad + stream_part).reshape(samples, patches, features)
    per_sample = jnp.sum(stream_grad, axis=1)
    lead_grad = jnp.sum(lead_value[:, None] * per_sample, axis=0)
    table_grad = jnp.dot(present.T, per_sample, precision=lax.Precision.HIGHEST)
    gain_grad = jnp.stack([gain_one_grad, gain_two_grad])
    shift_grad = jnp.stack([shift_one_grad, shift_two_grad])
    bias_grad = jnp.stack([out_bias_grad, down_bias_grad])
    owned = (
        lax.psum_scatter(table_grad, ("samp", "seq"), scatter_dimension=1, tiled=True),
        lax.psum_scatter(lead_grad, ("samp", "seq"), scatter_dimension=0, tiled=True),
        lax.psum_scatter(gain_grad, ("samp", "seq"), scatter_dimension=1, tiled=True),
        lax.psum_scatter(shift_grad, ("samp", "seq"), scatter_dimension=1, tiled=True),
        lax.psum_scatter(qkv_grad, ("samp", "seq"), scatter_dimension=0, tiled=True),
        lax.psum_scatter(qv_bias_grad, ("samp", "seq"), scatter_dimension=1, tiled=True),
        lax.psum_scatter(out_grad, ("samp", "seq"), scatter_dimension=0, tiled=True),
        lax.psum_scatter(bias_grad, ("samp", "seq"), scatter_dimension=1, tiled=True),
        lax.psum_scatter(up_grad, ("samp", "seq"), scatter_dimension=0, tiled=True),
        lax.psum_scatter(up_bias_grad, ("samp", "seq"), scatter_dimension=0, tiled=True),
        lax.psum_scatter(down_grad, ("samp", "seq"), scatter_dimension=0, tiled=True),
    )
    return (
        mixed,
        stream_grad,
        owned[0],
        owned[1],
        owned[2],
        owned[3],
        owned[4],
        owned[5],
        owned[6],
        owned[7],
        owned[8],
        owned[9],
        owned[10],
    )


MESH = pl.DeviceIdType.MESH
BF = jnp.bfloat16
F32 = jnp.float32
D = 1024
ROWS = 128
LANES = 8
FFL = 512


def dot_nn(a, b):
    return lax.dot_general(a, b, (((1,), (0,)), ((), ())), preferred_element_type=F32)


def dot_nt(a, b):
    return lax.dot_general(a, b, (((1,), (1,)), ((), ())), preferred_element_type=F32)


def dot_tn(a, b):
    return lax.dot_general(a, b, (((0,), (0,)), ((), ())), preferred_element_type=F32)


def erf(v):
    v = jnp.clip(v, -4.0, 4.0)
    s = v * v
    p = jnp.full_like(s, -2.72614225801306e-10)
    for a in (2.77068142495902e-08, -2.10102402082508e-06, -5.69250639462346e-05,
              -7.34990630326855e-04, -2.95459980854025e-03, -1.60960333262415e-02):
        p = p * s + a
    q = jnp.full_like(s, -1.45660718464996e-05)
    for b in (-2.13374055278905e-04, -1.68282697438203e-03, -7.37332916720468e-03, -1.42647390514189e-02):
        q = q * s + b
    return v * p / q


def flip(a, d):
    return 1 - a if d else a


def many(n, m=1):
    return pl.ds(pl.multiple_of(n, m), m)


def center(v):
    mean = jnp.mean(v, axis=-1, keepdims=True)
    centred = v - mean
    var = jnp.mean(centred * centred, axis=-1, keepdims=True)
    rstd = lax.rsqrt(var + epsilon)
    return centred * rstd, rstd


def norm_back(xhat, rstd, gain, grad):
    dx = grad * gain
    return rstd * (dx - jnp.mean(dx, axis=-1, keepdims=True) - xhat * jnp.mean(dx * xhat, axis=-1, keepdims=True))


def fast_kernel(
    tokens_h, lead_hours_h, var_mask_h, var_table_h, lead_weight_h, norm_gain_h, norm_shift_h, wqkv_h, qv_bias_h, wout_h,
    branch_bias_h, wup_h, up_bias_h, wdown_h, cot_h,
    mixed_o, tg_o, gq_o, go_o, gu_o, gd_o, small_o,
    lead_hours, var_mask, var_table, lead_weight, norm_gain, norm_shift, qv_bias, branch_bias, up_bias,
    tokens, wqkv_in, wup_in, wout_in, cot, tok_all, cot_all, n2_all, ml_all,
    wqkv, wup, wdown, wout, raw, square, pack_in, pack_all, full,
    normed, q_s, k_s, v_s, shares, attf, att,
    rs_s1, rs_r1, rs_s2, rs_r2, own, kept,
    middle, mgrad, act, uplow, dproj, dog, dk_acc, dv_acc,
    gqkv, gup, gdown, gout, xqkv, xup, xdown, zqkv_s, zup_s, zdown_s, zqkv, zup, zdown,
    out_x, out_s, out_z, sq2, su2, rq2, ru2, so2, ro2,
    tgr, smallp, r_a, s_b, r_b, upb_g, r_upb,
    ss, rs, ls,
):
    s_i = lax.axis_index("samp")
    q_i = lax.axis_index("seq")
    y, x = s_i // 2, s_i % 2
    z, c = q_i // 2, q_i % 2
    k, w = z // 2, z % 2
    idx = 16 * y + 8 * x + 4 * k + 2 * w + c
    lane = 4 * y + 2 * w + c
    rank = 2 * x + k
    sample = 2 * k + x
    off_diag = y + k - 2 * y * k
    is_home = 1 - (x + w - 2 * x * w) - (k + c - 2 * k * c) + (x + w - 2 * x * w) * (k + c - 2 * k * c)
    my_rows = many(ROWS * lane, ROWS)

    def dev(y_, x_, k_, w_, c_):
        return (2 * y_ + x_, 4 * k_ + 2 * w_ + c_)

    count = [0, 0]
    items = []

    def sems(n):
        a, b = count
        count[0] += n
        count[1] += n
        return a, b

    def rc(src, dst, a, b, device):
        return pltpu.make_async_remote_copy(src_ref=src, dst_ref=dst, send_sem=ss.at[a], recv_sem=rs.at[b], device_id=device, device_id_type=MESH)

    group = [(d // 4, (d // 2) % 2, d % 2) for d in range(1, 8)]
    chips = [(0, 0), (0, 1), (1, 0), (1, 1)]
    ranks = [(0, 1), (1, 0), (1, 1)]

    def peer(d):
        dy, dw, dc = d
        y_, w_, c_ = flip(y, dy), flip(w, dw), flip(c, dc)
        return y_, w_, c_, 4 * y_ + 2 * w_ + c_, dev(y_, x, k, w_, c_)

    def partner(d):
        dx, dk = d
        x_, k_ = flip(x, dx), flip(k, dk)
        return x_, k_, 2 * x_ + k_, dev(y, x_, k_, w, c)

    swap_dev = dev(k, x, y, w, c)

    rank_rows = many(128 * rank, 128)
    barrier = pltpu.get_barrier_semaphore()
    for d in group:
        pl.semaphore_signal(barrier, inc=1, device_id=peer(d)[4], device_id_type=MESH)
    for d in ranks:
        pl.semaphore_signal(barrier, inc=1, device_id=partner(d)[3], device_id_type=MESH)

    @pl.when(off_diag == 1)
    def _():
        pl.semaphore_signal(barrier, inc=1, device_id=swap_dev, device_id_type=MESH)

    loads = [
        pltpu.make_async_copy(src, dst, ls.at[n])
        for n, (src, dst) in enumerate(((tokens_h, tokens), (wqkv_h, wqkv_in), (wup_h, wup_in), (wout_h, wout_in), (cot_h, cot), (wdown_h, wdown.at[rank_rows])))
    ]
    small_loads = [
        pltpu.make_async_copy(src, dst, ls.at[8 + n])
        for n, (src, dst) in enumerate((
            (lead_hours_h, lead_hours), (var_mask_h, var_mask), (var_table_h, var_table), (lead_weight_h, lead_weight),
            (norm_gain_h, norm_gain), (norm_shift_h, norm_shift), (qv_bias_h, qv_bias), (branch_bias_h, branch_bias), (up_bias_h, up_bias),
        ))
    ]
    for load in small_loads + loads:
        load.start()
    raw[...] = jnp.zeros_like(raw)
    for load in small_loads:
        load.wait()
    square[...] = jnp.zeros_like(square)
    square[0:32, 0:48] = var_table[...].astype(F32)
    raw[0:48, 0:32] = jnp.transpose(square[...])[0:48, 0:32]
    for n, rows in ((48, norm_gain), (50, norm_shift), (52, qv_bias), (54, branch_bias)):
        raw[n : n + 2, 0:32] = rows[...].astype(F32)
    raw[56:57, 0:32] = lead_weight[...].astype(F32)
    raw[64:65, :] = up_bias[...].astype(F32)
    raw[65:66, 0:48] = var_mask[...].astype(F32)
    raw[65:66, 64:65] = lead_hours[...].astype(F32)
    packed = raw[0:16, :]
    for t in range(1, 4):
        packed = packed + pltpu.roll(raw[16 * t : 16 * t + 16, :], 32 * t, 1)
    pack_in[0:16, :] = packed.astype(BF)
    pack_in[16:32, :] = raw[64:80, :].astype(BF)
    for load in loads[:4]:
        load.wait()
    pl.semaphore_wait(barrier, 10 + off_diag)

    def begun(item):
        items.append(item)
        item.got = False

    class Swap:
        def __init__(self, src, dst):
            self.copy = rc(src, dst, *sems(1), swap_dev)

        def start(self):
            begun(self)
            pl.when(off_diag == 1)(self.copy.start)

        def wait(self):
            self.got = True
            pl.when(off_diag == 1)(self.copy.wait_recv)

        def drain(self):
            pl.when(off_diag == 1)(self.copy.wait_send)

    class Only:
        def __init__(self, sends, outgoing, takes, incoming):
            self.sends, self.outgoing, self.takes, self.incoming = sends, outgoing, takes, incoming

        def each(self, flag, copies, name):
            @pl.when(flag == 1)
            def _():
                for copy in copies:
                    getattr(copy, name)()

        def start(self):
            begun(self)
            self.each(self.sends, self.outgoing, "start")

        def wait(self):
            self.got = True
            self.each(self.takes, self.incoming, "wait_recv")

        def drain(self):
            self.each(self.sends, self.outgoing, "wait_send")

    def finish_all():
        for item in items:
            if not item.got:
                item.wait()
        for item in items:
            item.drain()

    y_nbr, w_nbr, sibling = dev(1 - y, x, k, w, c), dev(y, x, k, 1 - w, c), dev(y, x, k, w, 1 - c)
    UP, LOW = pl.ds(0, 64), pl.ds(64, 64)

    class Gather:
        def __init__(self, buf):
            self.buf = buf
            self.a, self.b = sems(10)

        def copy(self, n):
            ly, lw = 4 * (1 - y) + 2 * w + c, 4 * y + 2 * (1 - w) + c
            ld = 4 * (1 - y) + 2 * (1 - w) + c
            from_row, rows, device = (
                (ROWS * lane, 128, sibling),
                (ROWS * lane, 64, y_nbr), (ROWS * lane + 64, 64, y_nbr),
                (ROWS * lane + 64, 64, w_nbr), (ROWS * lane, 64, w_nbr),
                (ROWS * ly, 64, w_nbr), (ROWS * lw + 64, 64, y_nbr),
                (ROWS * ly, 128, sibling), (ROWS * lw, 128, sibling), (ROWS * ld, 128, sibling),
            )[n]
            ref = self.buf.at[pl.ds(pl.multiple_of(from_row, 64), rows)]
            return rc(ref, ref, self.a + n, self.b + n, device)

        def start(self):
            begun(self)
            self.passed = False
            for n in (1, 3, 2, 4, 0):
                self.copy(n).start()

        def pass_on(self):
            self.passed = True
            for n, then in ((1, 5), (3, 6), (2, 7), (4, 8), (5, None), (6, 9)):
                self.copy(n).wait_recv()
                if then is not None:
                    self.copy(then).start()

        def wait(self):
            if not self.passed:
                self.pass_on()
            self.got = True
            for n in (0, 7, 8, 9):
                self.copy(n).wait_recv()

        def drain(self):
            for n in range(10):
                self.copy(n).wait_send()

    class Scatter:
        def __init__(self, slot, partial):
            self.slot = slot
            self.partial = partial
            self.a1, self.b1 = sems(4)
            self.a2, self.b2 = sems(6)

        def far(self, i):
            dy, dw = i // 2, i % 2
            y_, w_ = y + dy - 2 * y * dy, w + dw - 2 * w * dw
            return y_, w_

        def first(self, i):
            return rc(rs_s1.at[self.slot, i], rs_r1.at[self.slot, i], self.a1 + i, self.b1 + i, sibling)

        def second(self, n):
            src, half, dst, half_there, device = (
                (2, UP, 2, UP, y_nbr), (2, LOW, 2, LOW, w_nbr),
                (0, UP, 0, UP, y_nbr), (1, LOW, 1, LOW, w_nbr),
                (0, LOW, 0, LOW, y_nbr), (1, UP, 1, UP, w_nbr),
            )[n]
            return rc(rs_s2.at[self.slot, src, half], rs_r2.at[self.slot, dst, half_there], self.a2 + n, self.b2 + n, device)

        def start(self, hold=False):
            begun(self)
            self.passed = False

            @pl.loop(0, 4)
            def _(n):
                i = 3 - n
                y_, w_ = self.far(i)
                rs_s1[self.slot, i] = self.partial(4 * y_ + 2 * w_ + 1 - c).astype(BF)
                self.first(i).start()

            def total(i):
                y_, w_ = self.far(i)
                part = self.partial(4 * y_ + 2 * w_ + c)
                self.first(i).wait_recv()
                return part + rs_r1[self.slot, i].astype(F32)

            rs_s2[self.slot, 2] = total(3).astype(BF)
            if not hold:
                self.second(0).start()
                self.second(1).start()
            value = total(2)
            rs_s2[self.slot, 0, 0:64] = value[0:64].astype(BF)
            if not hold:
                self.second(2).start()
            kept[self.slot, 0] = value[64:128]
            value = total(1)
            rs_s2[self.slot, 1, 64:128] = value[64:128].astype(BF)
            if not hold:
                self.second(3).start()
            kept[self.slot, 1] = value[0:64]
            own[self.slot] = total(0)

        def release(self):
            for n in range(4):
                self.second(n).start()

        def pass_on(self):
            self.passed = True
            self.second(0).wait_recv()
            rs_s2[self.slot, 1, 0:64] = (kept[self.slot, 1] + rs_r2[self.slot, 2, 0:64].astype(F32)).astype(BF)
            self.second(5).start()
            self.second(1).wait_recv()
            rs_s2[self.slot, 0, 64:128] = (kept[self.slot, 0] + rs_r2[self.slot, 2, 64:128].astype(F32)).astype(BF)
            self.second(4).start()

        def wait(self):
            if not self.passed:
                self.pass_on()
            self.got = True
            for n in (2, 3, 4, 5):
                self.second(n).wait_recv()
            return own[self.slot] + rs_r2[self.slot, 0].astype(F32) + rs_r2[self.slot, 1].astype(F32)

        def drain(self):
            for i in range(4):
                self.first(i).wait_send()
            for n in range(6):
                self.second(n).wait_send()

    class Batch:
        def __init__(self, copies):
            self.copies = copies
            self.a, self.b = sems(len(copies))

        def copy(self, n):
            src, dst, device = self.copies[n]
            return rc(src, dst, self.a + n, self.b + n, device)

        def start(self):
            begun(self)
            for n in range(len(self.copies)):
                self.copy(n).start()

        def wait(self):
            self.got = True
            for n in range(len(self.copies)):
                self.copy(n).wait_recv()

        def drain(self):
            for n in range(len(self.copies)):
                self.copy(n).wait_send()

    hx, hk = x + w - 2 * x * w, k + c - 2 * k * c
    z_dev, x_dev = partner((0, 1))[3], partner((1, 0))[3]

    class Across:
        def __init__(self, views):
            self.views = views
            self.n = len(views(x, k))
            self.a, self.b = sems(3 * self.n)

        def copies(self, leg):
            refs = self.views(x, 1 - k) if leg == 2 else self.views(x, k)
            at = self.n * leg
            return [rc(v, v, self.a + at + i, self.b + at + i, z_dev if leg == 0 else x_dev) for i, v in enumerate(refs)]

        def arrivals(self, leg):
            refs = self.views(*((x, 1 - k), (1 - x, k), (1 - x, 1 - k))[leg])
            at = self.n * leg
            return [rc(v, v, self.a + at + i, self.b + at + i, z_dev if leg == 0 else x_dev) for i, v in enumerate(refs)]

        def start(self):
            begun(self)
            self.passed = False
            for leg in (0, 1):
                for copy in self.copies(leg):
                    copy.start()

        def pass_on(self):
            self.passed = True
            for copy in self.arrivals(0):
                copy.wait_recv()
            for copy in self.copies(2):
                copy.start()

        def wait(self):
            if not self.passed:
                self.pass_on()
            self.got = True
            for leg in (1, 2):
                for copy in self.arrivals(leg):
                    copy.wait_recv()

        def drain(self):
            for leg in range(3):
                for copy in self.copies(leg):
                    copy.wait_send()

    class Reduce:
        def __init__(self, grad, rx, sz, rz):
            self.grad, self.rx, self.sz, self.rz = grad, rx, sz, rz
            self.runs = rx.shape[0]
            self.a, self.b = sems(self.runs + 1)

        def run(self, n):
            return rc(self.grad.at[many(512 * n + 256 * (1 - x), 256)], self.rx.at[n], self.a + n, self.b + n, x_dev)

        def last(self):
            return rc(self.sz, self.rz, self.a + self.runs, self.b + self.runs, z_dev)

        def start(self):
            begun(self)
            self.passed = False
            for n in range(self.runs):
                self.run(n).start()

        def part(self, n, k_):
            return (
                self.grad[many(512 * n + 256 * x + 128 * k_, 128), :].astype(F32)
                + self.rx[n, many(128 * k_, 128), :].astype(F32)
            )

        def pass_on(self):
            self.passed = True
            for n in range(self.runs):
                self.run(n).wait_recv()
            for n in range(self.runs):
                self.sz[n] = self.part(n, 1 - k).astype(BF)
            self.last().start()

        def wait(self):
            if not self.passed:
                self.pass_on()
            self.got = True
            self.last().wait_recv()

        def total(self, n):
            return self.part(n, k) + self.rz[n].astype(F32)

        def drain(self):
            for n in range(self.runs):
                self.run(n).wait_send()
            self.last().wait_send()

    swap_rows = many(ROWS * (4 * k + 2 * w + c), ROWS)
    tok_swap = Swap(tokens, tok_all.at[swap_rows])
    cot_swap = Swap(cot, cot_all.at[swap_rows])
    tok_swap.start()
    own_rows = many(32 * idx, 32)

    def up_cols(r, y_, w_, c_):
        return many(128 * (16 * y_ + 8 * (r // 2) + 4 * (r % 2) + 2 * w_ + c_), 128)

    copies = []
    for d in group:
        y_, w_, c_, l_, dv = peer(d)
        copies.append((pack_in, pack_all.at[idx], dv))
        for p in range(3):
            copies.append((wqkv_in.at[:, many(128 * (8 * p + l_), 128)], wqkv.at[own_rows, pl.ds(128 * p, 128)], dv))
    in_qkv = Batch(copies)
    in_qkv.start()

    out_a, out_b = sems(4)
    place = 2 * w + c
    out_rows = many(32 * place, 32)
    home_dev = dev(y, x, k, x, k)
    pairs = ((0, 1), (1, 0), (1, 1))
    away = 1 - is_home
    out_in = []
    for dw, dc in pairs:
        m = 2 * flip(w, dw) + flip(c, dc)
        out_in.append(rc(wout_in, wout.at[many(32 * m, 32)], out_a, out_b + m, home_dev))
    to_home = Only(away, [rc(wout_in, wout.at[out_rows], out_a, out_b + place, home_dev)], is_home, out_in)
    copies = []
    for d in group:
        y_, w_, c_, l_, dv = peer(d)
        for r in range(4):
            copies.append((wup_in.at[:, up_cols(r, y_, w_, c_)], wup.at[own_rows, pl.ds(128 * r, 128)], dv))
    in_up = Batch(copies)
    in_up.start()
    to_home.start()

    @pl.when(off_diag == 0)
    def _():
        tok_all[my_rows, :] = tokens[...]

    pack_all[idx] = pack_in[...]
    for p in range(3):
        wqkv[own_rows, 128 * p : 128 * p + 128] = wqkv_in[:, many(128 * (8 * p + lane), 128)]
    for r in range(4):
        wup[own_rows, 128 * r : 128 * r + 128] = wup_in[:, up_cols(r, y, w, c)]

    @pl.when(is_home == 1)
    def _():
        wout[out_rows, :] = wout_in[...]

    for load in loads[4:]:
        load.wait()

    @pl.when(off_diag == 0)
    def _():
        cot_all[my_rows, :] = cot[...]

    def runs_of(ref, *more):
        def views(x_, k_):
            refs = [more[0].at[pl.ds(16 * y_ + 8 * x_ + 4 * k_, 4)] for y_ in range(2)] if more else []
            return refs + [ref.at[many(512 * y_ + 256 * x_ + 128 * k_, 128)] for y_ in range(2)]

        return views

    dp_qkv = Across(runs_of(wqkv, pack_all))
    dp_up = Across(runs_of(wup))
    dp_down = Across(lambda x_, k_: [wdown.at[many(128 * (2 * x_ + k_), 128)]])
    in_qkv.wait()
    dp_qkv.start()
    tok_swap.wait()
    tok = Gather(tok_all)
    tok.start()
    cot_swap.start()

    dpo_a, dpo_b = sems(2)
    out_z_copy = rc(wout, wout, dpo_a, dpo_b, z_dev)
    out_x_copy = rc(wout, wout, dpo_a + 1, dpo_b + 1, x_dev)
    dp_out = Only(is_home, [out_z_copy, out_x_copy], (1 - hx) * hk, [out_z_copy])
    dp_out_more = Only((1 - hx) * hk, [out_x_copy], hx, [out_x_copy])
    to_home.wait()
    in_up.wait()
    dp_qkv.pass_on()
    dp_out.start()
    dp_up.start()
    tok.pass_on()

    dp_qkv.wait()
    lane_id = lax.broadcasted_iota(jnp.int32, (16, 128), 1)
    for b in range(8):
        for t in range(4):
            block = None
            for m in range(4):
                piece = pack_all[4 * b + m].astype(F32)[0:16, :]
                shift = (32 * (m - t)) % 128
                if shift:
                    piece = pltpu.roll(piece, shift, 1)
                block = piece if block is None else jnp.where(lane_id // 32 == m, piece, block)
            full[16 * t : 16 * t + 16, 128 * b : 128 * b + 128] = block

    gain0, gain1 = full[48:49, :], full[49:50, :]
    shift0, shift1 = full[50:51, :], full[51:52, :]
    lane_cols = many(128 * lane, 128)
    bias_q, bias_v = full[52:53, lane_cols], full[53:54, lane_cols]
    bias_out, bias_down = full[54:55, :], full[55:56, :]
    bias_up = jnp.concatenate(
        [pack_all[16 * y + 8 * (r // 2) + 4 * (r % 2) + 2 * w + c].astype(F32)[16:17, :] for r in range(4)], axis=1
    )
    facts = pack_all[8 * sample].astype(F32)[17:18, :]
    one_lane = lax.broadcasted_iota(jnp.int32, (1, 128), 1)
    present = jnp.where(one_lane < 64, facts, 0.0)
    hours = jnp.sum(jnp.where(one_lane == 64, facts, 0.0), axis=-1, keepdims=True) * hours_scale
    present8 = jnp.broadcast_to(present, (8, 128))[:, :64].astype(BF)
    extra = dot_nn(present8, full[...].astype(BF))[0:1, :] + hours * full[56:57, :]

    tok.wait()

    @pl.loop(0, 8)
    def _(n):
        rows = many(128 * n, 128)
        xhat, _ = center(tok_all[rows, :].astype(F32) + extra)
        normed[rows, :] = (xhat * gain0 + shift0).astype(BF)

    @pl.loop(0, 4)
    def _(n):
        rows = many(256 * n, 256)
        proj = dot_nn(normed[rows, :], wqkv[...])
        q_s[rows, :] = ((proj[:, :128] + bias_q) * 0.125).astype(BF)
        k_s[rows, :] = proj[:, 128:256].astype(BF)
        v_s[rows, :] = (proj[:, 256:384] + bias_v).astype(BF)

    QB = 256
    cot_swap.wait()
    cg = Gather(cot_all)
    cg.start()
    dp_down.start()
    dp_out.wait()
    dp_out_more.start()
    head_lane = lax.broadcasted_iota(jnp.int32, (1, 128), 1) // 64

    def of_head(v, h):
        return jnp.where(head_lane == h, v, jnp.zeros_like(v))

    @pl.loop(0, D // QB)
    def _(n):
        rows = many(QB * n, QB)
        queries = q_s[rows, :]
        total = None
        for h in range(2):
            scores = dot_nt(of_head(queries, h), k_s[...])
            top = jnp.max(scores, axis=-1, keepdims=True)
            e = jnp.exp(scores - top)
            share = (e * (1.0 / jnp.sum(e, axis=-1, keepdims=True))).astype(BF)
            shares[h, rows, :] = share
            got = of_head(dot_nn(share, v_s[...]), h)
            total = got if total is None else total + got
        attf[rows, :] = total
        att[rows, :] = total.astype(BF)

    dp_out_more.wait()

    def rows_of(l_):
        return many(ROWS * l_, ROWS)

    rs_out = Scatter(0, lambda l_: dot_nn(att[rows_of(l_), :], wout[...]))
    rs_out.start()
    rs_out.pass_on()

    cg.pass_on()
    dp_up.pass_on()

    stream = tok_all[my_rows, :].astype(F32) + extra
    mid = stream + (rs_out.wait() + bias_out)
    middle[...] = mid
    xhat2, rstd2 = center(mid)
    n2_all[my_rows, :] = (xhat2 * gain1 + shift1).astype(BF)
    n2 = Gather(n2_all)
    n2.start()
    dp_down.pass_on()
    n2.pass_on()
    dp_up.wait()
    dp_down.wait()
    cg.wait()
    n2.wait()

    upb_g[...] = jnp.zeros_like(upb_g)

    @pl.loop(0, 4)
    def _(n):
        rows = many(256 * n, 256)
        up = dot_nn(n2_all[rows, :], wup[...]) + bias_up
        cdf = 0.5 * (1.0 + erf(up * 0.7071067811865476))
        act[rows, :] = (up * cdf).astype(BF)
        slope = cdf + up * (jnp.exp(-0.5 * up * up) * 0.3989422804014327)
        low = (dot_nt(cot_all[rows, :], wdown[...]) * slope).astype(BF)
        uplow[rows, :] = low
        upb_g[0:1, :] += jnp.sum(low.astype(F32), axis=0, keepdims=True)

    rs_n2 = Scatter(1, lambda l_: dot_nt(uplow[rows_of(l_), :], wup[...]))
    rs_n2.start()

    @pl.loop(0, 4)
    def _(r):
        cols = many(128 * r, 128)
        gdown[cols, :] = dot_tn(act[:, cols], cot_all[...]).astype(BF)

    down_red = Reduce(gdown, xdown, zdown_s, zdown)
    down_red.start()
    rs_n2.pass_on()
    upb_sends = Batch([(upb_g.at[:, many(128 * partner(d)[2], 128)], r_upb.at[n], partner(d)[3]) for n, d in enumerate(ranks)])
    upb_sends.start()

    @pl.loop(0, 4)
    def _(n):
        cols = many(256 * n, 256)
        gup[cols, :] = dot_tn(n2_all[:, cols], uplow[...]).astype(BF)

    up_red = Reduce(gup, xup, zup_s, zup)
    up_red.start()

    rs_mix = Scatter(2, lambda l_: dot_nn(act[rows_of(l_), :], wdown[...]))
    rs_mix.start()
    n2_grad = rs_n2.wait()
    incoming = cot_all[my_rows, :].astype(F32)
    xhat2, rstd2 = center(middle[...])
    mg = incoming + norm_back(xhat2, rstd2, gain1, n2_grad)
    mgrad[...] = mg
    ml_all[my_rows, :] = mg.astype(BF)
    ml = Gather(ml_all)
    ml.start()
    rs_mix.pass_on()
    smallp[7:16, :] = jnp.zeros((9, D), F32)
    smallp[2:3, :] = jnp.sum(n2_grad * xhat2, axis=0, keepdims=True)
    smallp[4:5, :] = jnp.sum(n2_grad, axis=0, keepdims=True)
    smallp[5:6, :] = jnp.sum(mg.astype(BF).astype(F32), axis=0, keepdims=True)
    smallp[6:7, :] = jnp.sum(incoming, axis=0, keepdims=True)

    down_red.pass_on()
    ml.pass_on()
    up_red.pass_on()
    ml.wait()
    mixed_low = (middle[...] + (rs_mix.wait() + bias_down)).astype(BF)
    tgr[2] = mixed_low
    mix_swap = Swap(tgr.at[2], tgr.at[3])
    mix_swap.start()

    @pl.loop(0, 4)
    def _(n):
        rows = many(256 * n, 256)
        dog[rows, :] = dot_nt(ml_all[rows, :], wout[...]).astype(BF)

    dk_acc[...] = jnp.zeros_like(dk_acc)
    dv_acc[...] = jnp.zeros_like(dv_acc)

    def attend_back(n):
        rows = many(QB * n, QB)
        queries = q_s[rows, :]
        grads = dog[rows, :]
        both = grads.astype(F32) * attf[rows, :]
        dq = None
        for h in range(2):
            share = shares[h, rows, :]
            pressure = dot_nt(of_head(grads, h), v_s[...])
            offset = jnp.sum(of_head(both, h), axis=-1, keepdims=True)
            ds = (share.astype(F32) * (pressure - offset)).astype(BF)
            got = of_head(dot_nn(ds, k_s[...]), h)
            dq = got if dq is None else dq + got
            dk_acc[...] += dot_tn(ds, of_head(queries, h))
            dv_acc[...] += dot_tn(share, of_head(grads, h))
        dproj[rows, 0:128] = (dq.astype(BF).astype(F32) * 0.125).astype(BF)

    pl.loop(0, 2)(attend_back)
    pl.loop(2, 4)(attend_back)
    dproj[:, 128:256] = dk_acc[...].astype(BF)
    dproj[:, 256:384] = dv_acc[...].astype(BF)

    @pl.loop(0, 4)
    def _(n):
        cols = many(256 * n, 256)
        gqkv[cols, :] = dot_tn(normed[:, cols], dproj[...]).astype(BF)

    qkv_red = Reduce(gqkv, xqkv, zqkv_s, zqkv)
    qkv_red.start()
    low = dproj[...].astype(F32)
    smallp[8:9, lane_cols] = jnp.sum(low[:, 0:128], axis=0, keepdims=True)
    smallp[9:10, lane_cols] = jnp.sum(low[:, 256:384], axis=0, keepdims=True)
    rs_n1 = Scatter(3, lambda l_: dot_nt(dproj[rows_of(l_), :], wqkv[...]))
    rs_n1.start()

    rs_n1.pass_on()
    gout[...] = dot_tn(att[...], ml_all[...]).astype(BF)
    go_a, go_b = sems(2)
    grad_x = Only(hx, [rc(gout, out_x, go_a, go_b, x_dev)], 1 - hx, [rc(gout, out_x, go_a, go_b, x_dev)])
    grad_z = Only((1 - hx) * hk, [rc(out_s, out_z, go_a + 1, go_b + 1, z_dev)], is_home, [rc(out_s, out_z, go_a + 1, go_b + 1, z_dev)])
    grad_x.start()
    qkv_red.pass_on()
    grad_x.wait()

    @pl.when(hx == 0)
    def _():
        out_s[...] = (gout[...].astype(F32) + out_x[...].astype(F32)).astype(BF)

    grad_z.start()

    n1_grad = rs_n1.wait()
    xhat1, rstd1 = center(tok_all[my_rows, :].astype(F32) + extra)
    tg = mgrad[...] + norm_back(xhat1, rstd1, gain0, n1_grad)
    tgr[0] = tg.astype(BF)
    smallp[0:1, :] = jnp.sum(tg, axis=0, keepdims=True)
    smallp[1:2, :] = jnp.sum(n1_grad * xhat1, axis=0, keepdims=True)
    smallp[3:4, :] = jnp.sum(n1_grad, axis=0, keepdims=True)

    def block(y_, x_, k_):
        return smallp.at[:, many(128 * (4 * y_ + 2 * x_ + k_), 128)]

    copies = []
    for n, d in enumerate(ranks):
        x_, k_, r_, dv = partner(d)
        for y_ in range(2):
            copies.append((block(y_, x_, k_), r_b.at[n, y_], dv))
    small_ranks = Batch(copies)
    small_ranks.start()
    tg_swap = Swap(tgr.at[0], tgr.at[1])
    tg_swap.start()
    small_ranks.wait()
    for y_ in range(2):
        first = smallp[:, many(128 * (4 * y_ + 2 * x + k), 128)]
        s_b[y_, 0:1, :] = first[0:1, :]
        for n in range(3):
            s_b[y_, n + 1 : n + 2, :] = r_b[n, y_, 0:1, :]
        s_b[y_, 4:16, :] = (first + r_b[0, y_] + r_b[1, y_] + r_b[2, y_])[1:13, :]
    small_group = Batch([(s_b.at[peer(d)[0]], r_a.at[n], peer(d)[4]) for n, d in enumerate(group)])
    small_group.start()

    down_red.wait()
    gd_o[...] = down_red.total(0).astype(BF)

    def deal(low_sum, recv):
        copies = []
        for n, d in enumerate(group):
            y_, w_, c_, l_, dv = peer(d)
            copies.append((low_sum.at[many(128 * y_ + 64 * w_ + 32 * c_, 32)], recv.at[lane], dv))
        return Batch(copies)

    def collect(red, low_sum, recv):
        red.wait()
        for y_ in range(2):
            low_sum[128 * y_ : 128 * y_ + 128, :] = red.total(y_).astype(BF)
        batch = deal(low_sum, recv)
        batch.start()
        recv[lane] = low_sum[many(128 * y + 64 * w + 32 * c, 32), :]
        return batch

    up_deal = collect(up_red, su2, ru2)
    grad_z.wait()

    @pl.when(is_home == 1)
    def _():
        so2[...] = (out_s[...].astype(F32) + out_z[...].astype(F32)).astype(BF)
        go_o[...] = so2[out_rows, :]

    outs_a, outs_b = sems(3)
    copies = []
    for n, (dw, dc) in enumerate(pairs):
        w_, c_ = flip(w, dw), flip(c, dc)
        copies.append(rc(so2.at[many(32 * (2 * w_ + c_), 32)], ro2, outs_a + n, outs_b, dev(y, x, k, w_, c_)))
    out_deal = Only(is_home, copies, away, [rc(so2.at[pl.ds(0, 32)], ro2, outs_a, outs_b, home_dev)])
    out_deal.start()
    qkv_deal = collect(qkv_red, sq2, rq2)

    small_group.wait()
    total = s_b[y]
    for n in range(7):
        total = total + r_a[n]
    own_facts = [facts] + [pack_all[8 * (2 * partner(d)[1] + partner(d)[0])].astype(F32)[17:18, :] for d in ranks]
    facts_t = jnp.transpose(jnp.concatenate(own_facts + [jnp.zeros((4, 128), F32)], axis=0))
    table = None
    for n in range(4):
        part = facts_t[:, n : n + 1] * total[n : n + 1, :]
        table = part if table is None else table + part
    small_o[0:64, :] = table[0:64, :]
    small_o[64:80, :] = total
    small_o[80:81, :] = table[64:65, :] * hours_scale
    small_o[81:88, :] = jnp.zeros((7, 128), F32)
    upb_sends.wait()
    sum_upb = upb_g[:, rank_rows]
    for n in range(3):
        sum_upb = sum_upb + r_upb[n]
    small_o[88:96, :] = sum_upb

    out_deal.wait()

    @pl.when(is_home == 0)
    def _():
        go_o[...] = ro2[...]

    @pl.when(off_diag == 0)
    def _():
        tg_o[...] = tgr[0]
        mixed_o[...] = tgr[2]

    mix_swap.wait()
    tg_swap.wait()

    @pl.when(off_diag == 1)
    def _():
        tg_o[...] = tgr[1]
        mixed_o[...] = tgr[3]

    up_deal.wait()
    gu_o[...] = ru2[...]
    qkv_deal.wait()
    gq_o[...] = rq2[...]

    finish_all()


def finish_kernel(
    mixed_i, tg_i, gq_i, go_i, gu_i, gd_i, small_i,
    mixed_o, tg_o, table_o, lead_o, gain_o, shift_o, gq_o, qv_o, go_o, bias_o, gu_o, upb_o, gd_o,
):
    mixed_o[0] = mixed_i[...]
    tg_o[0] = tg_i[...].astype(F32)
    gd_o[...] = gd_i[...].astype(F32)
    go_o[...] = go_i[...].astype(F32)
    for l_ in range(8):
        part = gu_i[l_].astype(F32)
        y_, w_, c_ = l_ // 4, (l_ // 2) % 2, l_ % 2
        for r in range(4):
            at = 128 * (16 * y_ + 8 * (r // 2) + 4 * (r % 2) + 2 * w_ + c_)
            gu_o[:, at : at + 128] = part[:, 128 * r : 128 * r + 128]
        part = gq_i[l_].astype(F32)
        for p in range(3):
            at = 128 * (8 * p + l_)
            gq_o[:, at : at + 128] = part[:, 128 * p : 128 * p + 128]
    place = lax.rem(lax.axis_index("seq"), 4)
    small = small_i[0:88, :]
    mine = small
    for m in range(1, 4):
        mine = jnp.where(place == m, pltpu.roll(small, 128 - 32 * m, 1), mine)
    table_o[...] = jnp.transpose(jnp.concatenate([mine[0:64], jnp.zeros((64, 128), F32)], axis=0))[0:32, 0:48]
    gain_o[...] = mine[68:70, 0:32]
    shift_o[...] = mine[70:72, 0:32]
    bias_o[...] = mine[72:74, 0:32]
    qv_o[...] = mine[75:77, 0:32]
    lead_o[...] = mine[80:81, 0:32]
    upb_o[...] = small_i[88:89, :]


def local_fast(
    tokens, lead_hours, var_mask, var_table, lead_weight, norm_gain, norm_shift, w_qkv, qv_bias, w_out,
    branch_bias, w_up, up_bias, w_down, cotangent,
):
    vm = pltpu.VMEM
    scratch = [
        vm((1, 1), jnp.int32), vm((1, 48), jnp.int32), vm((32, 48), BF), vm((1, 32), BF), vm((2, 32), BF), vm((2, 32), BF),
        vm((2, 32), BF), vm((2, 32), BF), vm((1, 128), BF),
        vm((128, D), BF), vm((32, 3 * D), BF), vm((32, 4 * D), BF), vm((32, D), BF), vm((128, D), BF),
        vm((D, D), BF), vm((D, D), BF), vm((D, D), BF), vm((D, D), BF),
        vm((D, 384), BF), vm((D, FFL), BF), vm((FFL, D), BF), vm((128, D), BF), vm((80, 128), F32), vm((128, 128), F32), vm((32, 128), BF), vm((32, 32, 128), BF), vm((64, D), F32),
        vm((D, D), BF), vm((D, 128), BF), vm((D, 128), BF), vm((D, 128), BF), vm((2, D, D), BF), vm((D, 128), F32), vm((D, 128), BF),
        vm((4, 4, 128, D), BF), vm((4, 4, 128, D), BF), vm((4, 3, 128, D), BF), vm((4, 3, 128, D), BF), vm((4, 128, D), F32), vm((4, 2, 64, D), F32),
        vm((128, D), F32), vm((128, D), F32), vm((D, FFL), BF), vm((D, FFL), BF), vm((D, 384), BF), vm((D, 128), BF), vm((D, 128), F32), vm((D, 128), F32),
        vm((D, 384), BF), vm((D, FFL), BF), vm((FFL, D), BF), vm((128, D), BF),
        vm((2, 256, 384), BF), vm((2, 256, FFL), BF), vm((1, 256, D), BF),
        vm((2, 128, 384), BF), vm((2, 128, FFL), BF), vm((1, 128, D), BF),
        vm((2, 128, 384), BF), vm((2, 128, FFL), BF), vm((1, 128, D), BF),
        vm((128, D), BF), vm((128, D), BF), vm((128, D), BF),
        vm((256, 384), BF), vm((256, FFL), BF), vm((8, 32, 384), BF), vm((8, 32, FFL), BF), vm((128, D), BF), vm((32, D), BF),
        vm((4, 128, D), BF), vm((16, D), F32), vm((7, 16, 128), F32), vm((2, 16, 128), F32), vm((3, 2, 16, 128), F32),
        vm((8, FFL), F32), vm((3, 8, 128), F32),
        pltpu.SemaphoreType.DMA((320,)), pltpu.SemaphoreType.DMA((320,)), pltpu.SemaphoreType.DMA((24,)),
    ]
    shape = jax.ShapeDtypeStruct
    raw = pl.pallas_call(
        fast_kernel,
        out_shape=[
            shape((128, D), BF), shape((128, D), BF), shape((8, 32, 384), BF), shape((32, D), BF), shape((8, 32, FFL), BF),
            shape((128, D), BF), shape((96, 128), F32),
        ],
        in_specs=[pl.BlockSpec(memory_space=pl.ANY)] * 15,
        out_specs=[pl.BlockSpec(memory_space=vm)] * 7,
        scratch_shapes=scratch,
        compiler_params=pltpu.CompilerParams(collective_id=0, has_side_effects=True, vmem_limit_bytes=62 * 2**20),
        cost_estimate=pl.CostEstimate(flops=14_000_000_000, bytes_accessed=4_000_000, transcendentals=6_000_000),
    )(
        tokens[0], lead_hours[None], var_mask, var_table.T, lead_weight[None], norm_gain, norm_shift, w_qkv, qv_bias, w_out,
        branch_bias, w_up, up_bias[None], w_down, cotangent[0],
    )
    out = pl.pallas_call(
        finish_kernel,
        out_shape=[
            shape((1, 128, D), BF), shape((1, 128, D), F32), shape((32, 48), F32), shape((1, 32), F32), shape((2, 32), F32),
            shape((2, 32), F32), shape((32, 3 * D), F32), shape((2, 32), F32), shape((32, D), F32), shape((2, 32), F32),
            shape((32, 4 * D), F32), shape((1, 128), F32), shape((128, D), F32),
        ],
        in_specs=[pl.BlockSpec(memory_space=vm)] * 7,
        out_specs=[pl.BlockSpec(memory_space=vm)] * 13,
        compiler_params=pltpu.CompilerParams(vmem_limit_bytes=62 * 2**20),
        cost_estimate=pl.CostEstimate(flops=1_000_000, bytes_accessed=4_000_000, transcendentals=0),
    )(*raw)
    mixed, tg, table, lead, gain, shift, gq, qv, go, bias, gu, upb, gd = out
    return (mixed, tg, table.T, lead[0], gain, shift, gq, qv, go, bias, gu, upb[0], gd)


def solution(mesh):
    sizes = dict(mesh.shape)
    fast = sizes == {"samp": 4, "seq": 8}
    return jax.shard_map(
        local_fast if fast else local,
        mesh=mesh,
        in_specs=(
            P("samp", "seq", None),
            P("samp"),
            P("samp", None),
            P(None, ("samp", "seq")),
            P(("samp", "seq")),
            P(None, ("samp", "seq")),
            P(None, ("samp", "seq")),
            P(("samp", "seq"), None),
            P(None, ("samp", "seq")),
            P(("samp", "seq"), None),
            P(None, ("samp", "seq")),
            P(("samp", "seq"), None),
            P(("samp", "seq")),
            P(("samp", "seq"), None),
            P("samp", "seq", None),
        ),
        out_specs=(
            P("samp", "seq", None),
            P("samp", "seq", None),
            P(None, ("samp", "seq")),
            P(("samp", "seq")),
            P(None, ("samp", "seq")),
            P(None, ("samp", "seq")),
            P(("samp", "seq"), None),
            P(None, ("samp", "seq")),
            P(("samp", "seq"), None),
            P(None, ("samp", "seq")),
            P(("samp", "seq"), None),
            P(("samp", "seq")),
            P(("samp", "seq"), None),
        ),
        check_vma=False,
    )
```

```python
import jax
import jax.numpy as jnp
from jax import lax
from jax.experimental import pallas as pl
from jax.experimental.pallas import tpu as pltpu
from jax.sharding import PartitionSpec as P

HEADS = 16
HEAD_DIM = 64


epsilon = 1e-05
hours_scale = 1.0 / 168.0


def from_behind(block, axis, distance):
    devices = range(lax.axis_size(axis))
    route = [((i - distance) % len(devices), i) for i in devices]
    return lax.ppermute(block, axis, route)


def normalize(field, scaling, offsets):
    average = jnp.mean(field, axis=-1, keepdims=True)
    centred = field - average
    variance = jnp.mean(centred * centred, axis=-1, keepdims=True)
    return centred * lax.rsqrt(variance + epsilon) * scaling + offsets


def block_size(length):
    size_now = length
    while size_now > 512 and size_now % 2 == 0:
        size_now = size_now // 2
    return size_now


def over_blocks(advance, carried, segments):
    length = segments[0].shape[1]
    size_now = block_size(length)
    number = length // size_now
    stacked = tuple(
        (
            jnp.moveaxis(
                segment.reshape(segment.shape[0], number, size_now, segment.shape[2]), 1, 0
            )
            for segment in segments
        )
    )

    def visit(current, blocks):
        return (advance(current, blocks), None)

    carried, _ = lax.scan(visit, carried, stacked)
    return carried


def split_heads(matrix):
    return matrix.reshape(matrix.shape[0], matrix.shape[1], HEADS, HEAD_DIM)


def gelu_slope(upward):
    normal_cdf = 0.5 * (1.0 + lax.erf(upward * 0.7071067811865476))
    density = jnp.exp(-0.5 * upward * upward) * 0.3989422804014327
    return normal_cdf + upward * density


def pair_terms(query_heads, grad_heads, log_total, offset, key_heads, value_heads):
    scores = jnp.einsum(
        "sqhd,skhd->shqk", query_heads, key_heads, preferred_element_type=jnp.float32
    )
    shares = jnp.exp(scores - log_total[..., None])
    pressure = jnp.einsum(
        "sqhd,skhd->shqk", grad_heads, value_heads, preferred_element_type=jnp.float32
    )
    score_grad = (shares * (pressure - offset[..., None])).astype(jnp.bfloat16)
    query_part = jnp.einsum(
        "shqk,skhd->sqhd", score_grad, key_heads, preferred_element_type=jnp.float32
    )
    key_part = jnp.einsum(
        "shqk,sqhd->skhd", score_grad, query_heads, preferred_element_type=jnp.float32
    )
    value_part = jnp.einsum(
        "shqk,sqhd->skhd",
        shares.astype(jnp.bfloat16),
        grad_heads,
        preferred_element_type=jnp.float32,
    )
    return (query_part, key_part, value_part)


def local(
    tokens,
    lead_hours,
    var_mask,
    var_table,
    lead_weight,
    norm_gain,
    norm_shift,
    w_qkv,
    qv_bias,
    w_out,
    branch_bias,
    w_up,
    up_bias,
    w_down,
    cotangent,
):
    samples, patches, features = tokens.shape
    row_count = samples * patches
    factor = HEAD_DIM ** (-0.5)
    (
        table_full,
        lead_full,
        gain_all,
        shift_all,
        qkv_full,
        qv_all,
        out_full,
        bias_all,
        up_full,
        upb_full,
        down_full,
    ) = (
        lax.all_gather(var_table, ("samp", "seq"), axis=1, tiled=True),
        lax.all_gather(lead_weight, ("samp", "seq"), axis=0, tiled=True),
        lax.all_gather(norm_gain, ("samp", "seq"), axis=1, tiled=True),
        lax.all_gather(norm_shift, ("samp", "seq"), axis=1, tiled=True),
        lax.all_gather(w_qkv, ("samp", "seq"), axis=0, tiled=True),
        lax.all_gather(qv_bias, ("samp", "seq"), axis=1, tiled=True),
        lax.all_gather(w_out, ("samp", "seq"), axis=0, tiled=True),
        lax.all_gather(branch_bias, ("samp", "seq"), axis=1, tiled=True),
        lax.all_gather(w_up, ("samp", "seq"), axis=0, tiled=True),
        lax.all_gather(up_bias, ("samp", "seq"), axis=0, tiled=True),
        lax.all_gather(w_down, ("samp", "seq"), axis=0, tiled=True),
    )
    gain_full = gain_all.astype(jnp.float32)
    shift_full = shift_all.astype(jnp.float32)
    qv_full = qv_all.astype(jnp.float32)
    bias_full = bias_all.astype(jnp.float32)
    lead_value = lead_hours.astype(jnp.float32) * hours_scale
    present = var_mask.astype(jnp.float32)
    variable_sum = jnp.dot(present, table_full.astype(jnp.float32), precision=lax.Precision.HIGHEST)
    stream = (
        tokens.astype(jnp.float32)
        + lead_value[:, None, None] * lead_full.astype(jnp.float32)
        + variable_sum[:, None, :]
    )
    stream_rows = stream.reshape(row_count, features)
    normed = normalize(stream_rows, gain_full[0], shift_full[0]).astype(jnp.bfloat16)
    projected = jnp.dot(normed, qkv_full, preferred_element_type=jnp.float32)
    queries = (
        ((projected[:, :features] + qv_full[0]) * factor)
        .astype(jnp.bfloat16)
        .reshape(samples, patches, features)
    )
    keys_all = (
        projected[:, features : 2 * features]
        .astype(jnp.bfloat16)
        .reshape(samples, patches, features)
    )
    values_all = (
        (projected[:, 2 * features :] + qv_full[1])
        .astype(jnp.bfloat16)
        .reshape(samples, patches, features)
    )
    query_heads = split_heads(queries)

    def scores_of(keys_block):
        return jnp.einsum(
            "sqhd,skhd->shqk",
            query_heads,
            split_heads(keys_block),
            preferred_element_type=jnp.float32,
        )

    def stats_step(carried, blocks):
        running_max, running_sum = carried
        scores = scores_of(blocks[0])
        new_max = jnp.maximum(running_max, jnp.max(scores, axis=-1))
        running_sum = running_sum * jnp.exp(running_max - new_max) + jnp.sum(
            jnp.exp(scores - new_max[..., None]), axis=-1
        )
        return (new_max, running_sum)

    stats_start = (
        jnp.full((samples, HEADS, patches), -jnp.inf, jnp.float32),
        jnp.zeros((samples, HEADS, patches), jnp.float32),
    )
    running_max, running_sum = over_blocks(
        stats_step, stats_start, (lax.all_gather(keys_all, "seq", axis=1, tiled=True),)
    )
    log_total = running_max + jnp.log(running_sum)

    def mix_step(collected, blocks):
        shares = jnp.exp(scores_of(blocks[0]) - log_total[..., None]).astype(jnp.bfloat16)
        return collected + jnp.einsum(
            "shqk,skhd->sqhd", shares, split_heads(blocks[1]), preferred_element_type=jnp.float32
        )

    zero_heads = jnp.zeros((samples, patches, HEADS, HEAD_DIM), jnp.float32)
    attended_f = over_blocks(
        mix_step,
        zero_heads,
        (
            lax.all_gather(keys_all, "seq", axis=1, tiled=True),
            lax.all_gather(values_all, "seq", axis=1, tiled=True),
        ),
    )
    attended = attended_f.reshape(row_count, features).astype(jnp.bfloat16)
    middle = stream_rows + (
        jnp.dot(attended, out_full, preferred_element_type=jnp.float32) + bias_full[0]
    )
    normed_two = normalize(middle, gain_full[1], shift_full[1]).astype(jnp.bfloat16)
    upward = jnp.dot(normed_two, up_full, preferred_element_type=jnp.float32) + upb_full.astype(
        jnp.float32
    )
    activated = jax.nn.gelu(upward, approximate=False).astype(jnp.bfloat16)
    downward = jnp.dot(activated, down_full, preferred_element_type=jnp.float32) + bias_full[1]
    mixed = (middle + downward).astype(jnp.bfloat16).reshape(samples, patches, features)
    gain_back, qkv_back, out_back, up_back, down_back = (
        lax.all_gather(norm_gain, ("samp", "seq"), axis=1, tiled=True),
        lax.all_gather(w_qkv, ("samp", "seq"), axis=0, tiled=True),
        lax.all_gather(w_out, ("samp", "seq"), axis=0, tiled=True),
        lax.all_gather(w_up, ("samp", "seq"), axis=0, tiled=True),
        lax.all_gather(w_down, ("samp", "seq"), axis=0, tiled=True),
    )
    gain_back = gain_back.astype(jnp.float32)
    incoming = cotangent.astype(jnp.float32).reshape(row_count, features)
    incoming_low = incoming.astype(jnp.bfloat16)
    down_grad = jnp.einsum("tf,td->fd", activated, incoming_low, preferred_element_type=jnp.float32)
    down_bias_grad = jnp.sum(incoming_low.astype(jnp.float32), axis=0)
    gelu_grad = jnp.einsum(
        "td,fd->tf", incoming_low, down_back, preferred_element_type=jnp.float32
    ) * gelu_slope(upward)
    up_low = gelu_grad.astype(jnp.bfloat16)
    up_grad = jnp.einsum("td,tf->df", normed_two, up_low, preferred_element_type=jnp.float32)
    up_bias_grad = jnp.sum(up_low.astype(jnp.float32), axis=0)
    normed_two_grad = jnp.einsum("tf,df->td", up_low, up_back, preferred_element_type=jnp.float32)
    _, pull_second = jax.vjp(normalize, middle, gain_back[1], shift_full[1])
    middle_part, gain_two_grad, shift_two_grad = pull_second(normed_two_grad)
    middle_grad = incoming + middle_part
    middle_low = middle_grad.astype(jnp.bfloat16)
    out_grad = jnp.einsum("te,td->ed", attended, middle_low, preferred_element_type=jnp.float32)
    out_bias_grad = jnp.sum(middle_low.astype(jnp.float32), axis=0)
    attended_grad = jnp.einsum(
        "td,ed->te", middle_low, out_back, preferred_element_type=jnp.float32
    ).astype(jnp.bfloat16)
    grad_rows = attended_grad.reshape(samples, patches, features)
    grad_heads = split_heads(grad_rows)
    offset = jnp.transpose(jnp.sum(grad_heads.astype(jnp.float32) * attended_f, axis=-1), (0, 2, 1))
    grads_start = jnp.zeros((2, samples, patches, HEADS, HEAD_DIM), jnp.float32)

    def visit_block(blocks, partial_grads, query_acc):
        query_part, key_part, value_part = pair_terms(
            query_heads,
            grad_heads,
            log_total,
            offset,
            split_heads(blocks[0]),
            split_heads(blocks[1]),
        )
        return (partial_grads + jnp.stack([key_part, value_part]), query_acc + query_part)

    def turn_grads(partial_grads):
        return from_behind(partial_grads.astype(jnp.bfloat16), "seq", 1).astype(partial_grads.dtype)

    def cycle_step(counter, carried):
        blocks, partial_grads, query_acc = carried
        partial_grads, query_acc = visit_block(blocks, partial_grads, query_acc)
        partial_grads = turn_grads(partial_grads)
        blocks = from_behind(blocks, "seq", 1)
        return (blocks, partial_grads, query_acc)

    blocks_start = jnp.stack([keys_all, values_all])
    blocks, partial_grads, query_acc = lax.fori_loop(
        0, lax.axis_size("seq") - 1, cycle_step, (blocks_start, grads_start, zero_heads)
    )
    partial_grads, query_acc = visit_block(blocks, partial_grads, query_acc)
    partial_grads = turn_grads(partial_grads)
    query_low = query_acc.astype(jnp.bfloat16).reshape(row_count, features) * factor
    key_low = partial_grads[0].astype(jnp.bfloat16).reshape(row_count, features)
    value_low = partial_grads[1].astype(jnp.bfloat16).reshape(row_count, features)
    proj_grad = jnp.concatenate([query_low, key_low, value_low], axis=1)
    qkv_grad = jnp.einsum("td,te->de", normed, proj_grad, preferred_element_type=jnp.float32)
    qv_bias_grad = jnp.stack(
        [
            jnp.sum(query_low.astype(jnp.float32), axis=0),
            jnp.sum(value_low.astype(jnp.float32), axis=0),
        ]
    )
    normed_grad = jnp.einsum("te,de->td", proj_grad, qkv_back, preferred_element_type=jnp.float32)
    _, pull_first = jax.vjp(normalize, stream_rows, gain_back[0], shift_full[0])
    stream_part, gain_one_grad, shift_one_grad = pull_first(normed_grad)
    stream_grad = (middle_grad + stream_part).reshape(samples, patches, features)
    per_sample = jnp.sum(stream_grad, axis=1)
    lead_grad = jnp.sum(lead_value[:, None] * per_sample, axis=0)
    table_grad = jnp.dot(present.T, per_sample, precision=lax.Precision.HIGHEST)
    gain_grad = jnp.stack([gain_one_grad, gain_two_grad])
    shift_grad = jnp.stack([shift_one_grad, shift_two_grad])
    bias_grad = jnp.stack([out_bias_grad, down_bias_grad])
    owned = (
        lax.psum_scatter(table_grad, ("samp", "seq"), scatter_dimension=1, tiled=True),
        lax.psum_scatter(lead_grad, ("samp", "seq"), scatter_dimension=0, tiled=True),
        lax.psum_scatter(gain_grad, ("samp", "seq"), scatter_dimension=1, tiled=True),
        lax.psum_scatter(shift_grad, ("samp", "seq"), scatter_dimension=1, tiled=True),
        lax.psum_scatter(qkv_grad, ("samp", "seq"), scatter_dimension=0, tiled=True),
        lax.psum_scatter(qv_bias_grad, ("samp", "seq"), scatter_dimension=1, tiled=True),
        lax.psum_scatter(out_grad, ("samp", "seq"), scatter_dimension=0, tiled=True),
        lax.psum_scatter(bias_grad, ("samp", "seq"), scatter_dimension=1, tiled=True),
        lax.psum_scatter(up_grad, ("samp", "seq"), scatter_dimension=0, tiled=True),
        lax.psum_scatter(up_bias_grad, ("samp", "seq"), scatter_dimension=0, tiled=True),
        lax.psum_scatter(down_grad, ("samp", "seq"), scatter_dimension=0, tiled=True),
    )
    return (
        mixed,
        stream_grad,
        owned[0],
        owned[1],
        owned[2],
        owned[3],
        owned[4],
        owned[5],
        owned[6],
        owned[7],
        owned[8],
        owned[9],
        owned[10],
    )


MESH = pl.DeviceIdType.MESH
BF = jnp.bfloat16
F32 = jnp.float32
D = 1024
ROWS = 128
LANES = 8
FFL = 512


def dot_nn(a, b):
    return lax.dot_general(a, b, (((1,), (0,)), ((), ())), preferred_element_type=F32)


def dot_nt(a, b):
    return lax.dot_general(a, b, (((1,), (1,)), ((), ())), preferred_element_type=F32)


def dot_tn(a, b):
    return lax.dot_general(a, b, (((0,), (0,)), ((), ())), preferred_element_type=F32)


def erf(v):
    v = jnp.clip(v, -4.0, 4.0)
    s = v * v
    p = jnp.full_like(s, -2.72614225801306e-10)
    for a in (2.77068142495902e-08, -2.10102402082508e-06, -5.69250639462346e-05,
              -7.34990630326855e-04, -2.95459980854025e-03, -1.60960333262415e-02):
        p = p * s + a
    q = jnp.full_like(s, -1.45660718464996e-05)
    for b in (-2.13374055278905e-04, -1.68282697438203e-03, -7.37332916720468e-03, -1.42647390514189e-02):
        q = q * s + b
    return v * p / q


def flip(a, d):
    return 1 - a if d else a


def many(n, m=1):
    return pl.ds(pl.multiple_of(n, m), m)


def center(v):
    mean = jnp.mean(v, axis=-1, keepdims=True)
    centred = v - mean
    var = jnp.mean(centred * centred, axis=-1, keepdims=True)
    rstd = lax.rsqrt(var + epsilon)
    return centred * rstd, rstd


def norm_back(xhat, rstd, gain, grad):
    dx = grad * gain
    return rstd * (dx - jnp.mean(dx, axis=-1, keepdims=True) - xhat * jnp.mean(dx * xhat, axis=-1, keepdims=True))


def fast_kernel(
    tokens_h, lead_hours_h, var_mask_h, var_table_h, lead_weight_h, norm_gain_h, norm_shift_h, wqkv_h, qv_bias_h, wout_h,
    branch_bias_h, wup_h, up_bias_h, wdown_h, cot_h,
    mixed_o, tg_o, gq_o, go_o, gu_o, gd_o, small_o,
    lead_hours, var_mask, var_table, lead_weight, norm_gain, norm_shift, qv_bias, branch_bias, up_bias,
    tokens, wqkv_in, wup_in, wout_in, cot, tok_all, cot_all, n2_all, ml_all,
    wqkv, wup, wdown, wout, raw, square, pack_in, pack_all, full,
    normed, q_s, k_s, v_s, shares, attf, att,
    rs_s1, rs_r1, rs_s2, rs_r2, own, kept,
    middle, mgrad, act, uplow, dproj, dog, dk_acc, dv_acc,
    gqkv, gup, gdown, gout, xqkv, xup, xdown, zqkv_s, zup_s, zdown_s, zqkv, zup, zdown,
    out_x, out_s, out_z, sq2, su2, rq2, ru2, so2, ro2,
    tgr, smallp, r_a, s_b, r_b, upb_g, r_upb,
    ss, rs, ls,
):
    s_i = lax.axis_index("samp")
    q_i = lax.axis_index("seq")
    y, x = s_i // 2, s_i % 2
    z, c = q_i // 2, q_i % 2
    k, w = z // 2, z % 2
    idx = 16 * y + 8 * x + 4 * k + 2 * w + c
    lane = 4 * y + 2 * w + c
    rank = 2 * x + k
    sample = 2 * k + x
    off_diag = y + k - 2 * y * k
    is_home = 1 - (x + w - 2 * x * w) - (k + c - 2 * k * c) + (x + w - 2 * x * w) * (k + c - 2 * k * c)
    my_rows = many(ROWS * lane, ROWS)

    def dev(y_, x_, k_, w_, c_):
        return (2 * y_ + x_, 4 * k_ + 2 * w_ + c_)

    count = [0, 0]
    items = []

    def sems(n):
        a, b = count
        count[0] += n
        count[1] += n
        return a, b

    def rc(src, dst, a, b, device):
        return pltpu.make_async_remote_copy(src_ref=src, dst_ref=dst, send_sem=ss.at[a], recv_sem=rs.at[b], device_id=device, device_id_type=MESH)

    group = [(d // 4, (d // 2) % 2, d % 2) for d in range(1, 8)]
    chips = [(0, 0), (0, 1), (1, 0), (1, 1)]
    ranks = [(0, 1), (1, 0), (1, 1)]

    def peer(d):
        dy, dw, dc = d
        y_, w_, c_ = flip(y, dy), flip(w, dw), flip(c, dc)
        return y_, w_, c_, 4 * y_ + 2 * w_ + c_, dev(y_, x, k, w_, c_)

    def partner(d):
        dx, dk = d
        x_, k_ = flip(x, dx), flip(k, dk)
        return x_, k_, 2 * x_ + k_, dev(y, x_, k_, w, c)

    swap_dev = dev(k, x, y, w, c)

    rank_rows = many(128 * rank, 128)
    barrier = pltpu.get_barrier_semaphore()
    for d in group:
        pl.semaphore_signal(barrier, inc=1, device_id=peer(d)[4], device_id_type=MESH)
    for d in ranks:
        pl.semaphore_signal(barrier, inc=1, device_id=partner(d)[3], device_id_type=MESH)

    @pl.when(off_diag == 1)
    def _():
        pl.semaphore_signal(barrier, inc=1, device_id=swap_dev, device_id_type=MESH)

    loads = [
        pltpu.make_async_copy(src, dst, ls.at[n])
        for n, (src, dst) in enumerate(((tokens_h, tokens), (wqkv_h, wqkv_in), (wup_h, wup_in), (wout_h, wout_in), (cot_h, cot), (wdown_h, wdown.at[rank_rows])))
    ]
    small_loads = [
        pltpu.make_async_copy(src, dst, ls.at[8 + n])
        for n, (src, dst) in enumerate((
            (lead_hours_h, lead_hours), (var_mask_h, var_mask), (var_table_h, var_table), (lead_weight_h, lead_weight),
            (norm_gain_h, norm_gain), (norm_shift_h, norm_shift), (qv_bias_h, qv_bias), (branch_bias_h, branch_bias), (up_bias_h, up_bias),
        ))
    ]
    for load in small_loads + loads:
        load.start()
    raw[...] = jnp.zeros_like(raw)
    for load in small_loads:
        load.wait()
    square[...] = jnp.zeros_like(square)
    square[0:32, 0:48] = var_table[...].astype(F32)
    raw[0:48, 0:32] = jnp.transpose(square[...])[0:48, 0:32]
    for n, rows in ((48, norm_gain), (50, norm_shift), (52, qv_bias), (54, branch_bias)):
        raw[n : n + 2, 0:32] = rows[...].astype(F32)
    raw[56:57, 0:32] = lead_weight[...].astype(F32)
    raw[64:65, :] = up_bias[...].astype(F32)
    raw[65:66, 0:48] = var_mask[...].astype(F32)
    raw[65:66, 64:65] = lead_hours[...].astype(F32)
    packed = raw[0:16, :]
    for t in range(1, 4):
        packed = packed + pltpu.roll(raw[16 * t : 16 * t + 16, :], 32 * t, 1)
    pack_in[0:16, :] = packed.astype(BF)
    pack_in[16:32, :] = raw[64:80, :].astype(BF)
    for load in loads[:4]:
        load.wait()
    pl.semaphore_wait(barrier, 10 + off_diag)

    def begun(item):
        items.append(item)
        item.got = False

    class Swap:
        def __init__(self, src, dst):
            self.copy = rc(src, dst, *sems(1), swap_dev)

        def start(self):
            begun(self)
            pl.when(off_diag == 1)(self.copy.start)

        def wait(self):
            self.got = True
            pl.when(off_diag == 1)(self.copy.wait_recv)

        def drain(self):
            pl.when(off_diag == 1)(self.copy.wait_send)

    class Only:
        def __init__(self, sends, outgoing, takes, incoming):
            self.sends, self.outgoing, self.takes, self.incoming = sends, outgoing, takes, incoming

        def each(self, flag, copies, name):
            @pl.when(flag == 1)
            def _():
                for copy in copies:
                    getattr(copy, name)()

        def start(self):
            begun(self)
            self.each(self.sends, self.outgoing, "start")

        def wait(self):
            self.got = True
            self.each(self.takes, self.incoming, "wait_recv")

        def drain(self):
            self.each(self.sends, self.outgoing, "wait_send")

    def finish_all():
        for item in items:
            if not item.got:
                item.wait()
        for item in items:
            item.drain()

    y_nbr, w_nbr, sibling = dev(1 - y, x, k, w, c), dev(y, x, k, 1 - w, c), dev(y, x, k, w, 1 - c)
    UP, LOW = pl.ds(0, 64), pl.ds(64, 64)

    class Gather:
        def __init__(self, buf):
            self.buf = buf
            self.a, self.b = sems(10)

        def copy(self, n):
            ly, lw = 4 * (1 - y) + 2 * w + c, 4 * y + 2 * (1 - w) + c
            ld = 4 * (1 - y) + 2 * (1 - w) + c
            from_row, rows, device = (
                (ROWS * lane, 128, sibling),
                (ROWS * lane, 64, y_nbr), (ROWS * lane + 64, 64, y_nbr),
                (ROWS * lane + 64, 64, w_nbr), (ROWS * lane, 64, w_nbr),
                (ROWS * ly, 64, w_nbr), (ROWS * lw + 64, 64, y_nbr),
                (ROWS * ly, 128, sibling), (ROWS * lw, 128, sibling), (ROWS * ld, 128, sibling),
            )[n]
            ref = self.buf.at[pl.ds(pl.multiple_of(from_row, 64), rows)]
            return rc(ref, ref, self.a + n, self.b + n, device)

        def start(self):
            begun(self)
            self.passed = False
            for n in (1, 3, 2, 4, 0):
                self.copy(n).start()

        def pass_on(self):
            self.passed = True
            for n, then in ((1, 5), (3, 6), (2, 7), (4, 8), (5, None), (6, 9)):
                self.copy(n).wait_recv()
                if then is not None:
                    self.copy(then).start()

        def wait(self):
            if not self.passed:
                self.pass_on()
            self.got = True
            for n in (0, 7, 8, 9):
                self.copy(n).wait_recv()

        def drain(self):
            for n in range(10):
                self.copy(n).wait_send()

    class Scatter:
        def __init__(self, slot, partial):
            self.slot = slot
            self.partial = partial
            self.a1, self.b1 = sems(4)
            self.a2, self.b2 = sems(6)

        def far(self, i):
            dy, dw = i // 2, i % 2
            y_, w_ = y + dy - 2 * y * dy, w + dw - 2 * w * dw
            return y_, w_

        def first(self, i):
            return rc(rs_s1.at[self.slot, i], rs_r1.at[self.slot, i], self.a1 + i, self.b1 + i, sibling)

        def second(self, n):
            src, half, dst, half_there, device = (
                (2, UP, 2, UP, y_nbr), (2, LOW, 2, LOW, w_nbr),
                (0, UP, 0, UP, y_nbr), (1, LOW, 1, LOW, w_nbr),
                (0, LOW, 0, LOW, y_nbr), (1, UP, 1, UP, w_nbr),
            )[n]
            return rc(rs_s2.at[self.slot, src, half], rs_r2.at[self.slot, dst, half_there], self.a2 + n, self.b2 + n, device)

        def start(self, hold=False):
            begun(self)
            self.passed = False

            @pl.loop(0, 4)
            def _(n):
                i = 3 - n
                y_, w_ = self.far(i)
                rs_s1[self.slot, i] = self.partial(4 * y_ + 2 * w_ + 1 - c).astype(BF)
                self.first(i).start()

            def total(i):
                y_, w_ = self.far(i)
                part = self.partial(4 * y_ + 2 * w_ + c)
                self.first(i).wait_recv()
                return part + rs_r1[self.slot, i].astype(F32)

            rs_s2[self.slot, 2] = total(3).astype(BF)
            if not hold:
                self.second(0).start()
                self.second(1).start()
            value = total(2)
            rs_s2[self.slot, 0, 0:64] = value[0:64].astype(BF)
            if not hold:
                self.second(2).start()
            kept[self.slot, 0] = value[64:128]
            value = total(1)
            rs_s2[self.slot, 1, 64:128] = value[64:128].astype(BF)
            if not hold:
                self.second(3).start()
            kept[self.slot, 1] = value[0:64]
            own[self.slot] = total(0)

        def release(self):
            for n in range(4):
                self.second(n).start()

        def pass_on(self):
            self.passed = True
            self.second(0).wait_recv()
            rs_s2[self.slot, 1, 0:64] = (kept[self.slot, 1] + rs_r2[self.slot, 2, 0:64].astype(F32)).astype(BF)
            self.second(5).start()
            self.second(1).wait_recv()
            rs_s2[self.slot, 0, 64:128] = (kept[self.slot, 0] + rs_r2[self.slot, 2, 64:128].astype(F32)).astype(BF)
            self.second(4).start()

        def wait(self):
            if not self.passed:
                self.pass_on()
            self.got = True
            for n in (2, 3, 4, 5):
                self.second(n).wait_recv()
            return own[self.slot] + rs_r2[self.slot, 0].astype(F32) + rs_r2[self.slot, 1].astype(F32)

        def drain(self):
            for i in range(4):
                self.first(i).wait_send()
            for n in range(6):
                self.second(n).wait_send()

    class Batch:
        def __init__(self, copies):
            self.copies = copies
            self.a, self.b = sems(len(copies))

        def copy(self, n):
            src, dst, device = self.copies[n]
            return rc(src, dst, self.a + n, self.b + n, device)

        def start(self):
            begun(self)
            for n in range(len(self.copies)):
                self.copy(n).start()

        def wait(self):
            self.got = True
            for n in range(len(self.copies)):
                self.copy(n).wait_recv()

        def drain(self):
            for n in range(len(self.copies)):
                self.copy(n).wait_send()

    hx, hk = x + w - 2 * x * w, k + c - 2 * k * c
    z_dev, x_dev = partner((0, 1))[3], partner((1, 0))[3]

    class Across:
        def __init__(self, views):
            self.views = views
            self.n = len(views(x, k))
            self.a, self.b = sems(3 * self.n)

        def copies(self, leg):
            refs = self.views(x, 1 - k) if leg == 2 else self.views(x, k)
            at = self.n * leg
            return [rc(v, v, self.a + at + i, self.b + at + i, z_dev if leg == 0 else x_dev) for i, v in enumerate(refs)]

        def arrivals(self, leg):
            refs = self.views(*((x, 1 - k), (1 - x, k), (1 - x, 1 - k))[leg])
            at = self.n * leg
            return [rc(v, v, self.a + at + i, self.b + at + i, z_dev if leg == 0 else x_dev) for i, v in enumerate(refs)]

        def start(self):
            begun(self)
            self.passed = False
            for leg in (0, 1):
                for copy in self.copies(leg):
                    copy.start()

        def pass_on(self):
            self.passed = True
            for copy in self.arrivals(0):
                copy.wait_recv()
            for copy in self.copies(2):
                copy.start()

        def wait(self):
            if not self.passed:
                self.pass_on()
            self.got = True
            for leg in (1, 2):
                for copy in self.arrivals(leg):
                    copy.wait_recv()

        def drain(self):
            for leg in range(3):
                for copy in self.copies(leg):
                    copy.wait_send()

    class Reduce:
        def __init__(self, grad, rx, sz, rz):
            self.grad, self.rx, self.sz, self.rz = grad, rx, sz, rz
            self.runs = rx.shape[0]
            self.a, self.b = sems(self.runs + 1)

        def run(self, n):
            return rc(self.grad.at[many(512 * n + 256 * (1 - x), 256)], self.rx.at[n], self.a + n, self.b + n, x_dev)

        def last(self):
            return rc(self.sz, self.rz, self.a + self.runs, self.b + self.runs, z_dev)

        def start(self):
            begun(self)
            self.passed = False
            for n in range(self.runs):
                self.run(n).start()

        def part(self, n, k_):
            return (
                self.grad[many(512 * n + 256 * x + 128 * k_, 128), :].astype(F32)
                + self.rx[n, many(128 * k_, 128), :].astype(F32)
            )

        def pass_on(self):
            self.passed = True
            for n in range(self.runs):
                self.run(n).wait_recv()
            for n in range(self.runs):
                self.sz[n] = self.part(n, 1 - k).astype(BF)
            self.last().start()

        def wait(self):
            if not self.passed:
                self.pass_on()
            self.got = True
            self.last().wait_recv()

        def total(self, n):
            return self.part(n, k) + self.rz[n].astype(F32)

        def drain(self):
            for n in range(self.runs):
                self.run(n).wait_send()
            self.last().wait_send()

    swap_rows = many(ROWS * (4 * k + 2 * w + c), ROWS)
    tok_swap = Swap(tokens, tok_all.at[swap_rows])
    cot_swap = Swap(cot, cot_all.at[swap_rows])
    tok_swap.start()
    own_rows = many(32 * idx, 32)

    def up_cols(r, y_, w_, c_):
        return many(128 * (16 * y_ + 8 * (r // 2) + 4 * (r % 2) + 2 * w_ + c_), 128)

    copies = []
    for d in group:
        y_, w_, c_, l_, dv = peer(d)
        copies.append((pack_in, pack_all.at[idx], dv))
        for p in range(3):
            copies.append((wqkv_in.at[:, many(128 * (8 * p + l_), 128)], wqkv.at[own_rows, pl.ds(128 * p, 128)], dv))
    in_qkv = Batch(copies)
    in_qkv.start()

    out_a, out_b = sems(4)
    place = 2 * w + c
    out_rows = many(32 * place, 32)
    home_dev = dev(y, x, k, x, k)
    pairs = ((0, 1), (1, 0), (1, 1))
    away = 1 - is_home
    out_in = []
    for dw, dc in pairs:
        m = 2 * flip(w, dw) + flip(c, dc)
        out_in.append(rc(wout_in, wout.at[many(32 * m, 32)], out_a, out_b + m, home_dev))
    to_home = Only(away, [rc(wout_in, wout.at[out_rows], out_a, out_b + place, home_dev)], is_home, out_in)
    copies = []
    for d in group:
        y_, w_, c_, l_, dv = peer(d)
        for r in range(4):
            copies.append((wup_in.at[:, up_cols(r, y_, w_, c_)], wup.at[own_rows, pl.ds(128 * r, 128)], dv))
    in_up = Batch(copies)
    in_up.start()
    to_home.start()

    @pl.when(off_diag == 0)
    def _():
        tok_all[my_rows, :] = tokens[...]

    pack_all[idx] = pack_in[...]
    for p in range(3):
        wqkv[own_rows, 128 * p : 128 * p + 128] = wqkv_in[:, many(128 * (8 * p + lane), 128)]
    for r in range(4):
        wup[own_rows, 128 * r : 128 * r + 128] = wup_in[:, up_cols(r, y, w, c)]

    @pl.when(is_home == 1)
    def _():
        wout[out_rows, :] = wout_in[...]

    for load in loads[4:]:
        load.wait()

    @pl.when(off_diag == 0)
    def _():
        cot_all[my_rows, :] = cot[...]

    def runs_of(ref, *more):
        def views(x_, k_):
            refs = [more[0].at[pl.ds(16 * y_ + 8 * x_ + 4 * k_, 4)] for y_ in range(2)] if more else []
            return refs + [ref.at[many(512 * y_ + 256 * x_ + 128 * k_, 128)] for y_ in range(2)]

        return views

    dp_qkv = Across(runs_of(wqkv, pack_all))
    dp_up = Across(runs_of(wup))
    dp_down = Across(lambda x_, k_: [wdown.at[many(128 * (2 * x_ + k_), 128)]])
    in_qkv.wait()
    dp_qkv.start()
    tok_swap.wait()
    tok = Gather(tok_all)
    tok.start()
    cot_swap.start()

    dpo_a, dpo_b = sems(2)
    out_z_copy = rc(wout, wout, dpo_a, dpo_b, z_dev)
    out_x_copy = rc(wout, wout, dpo_a + 1, dpo_b + 1, x_dev)
    dp_out = Only(is_home, [out_z_copy, out_x_copy], (1 - hx) * hk, [out_z_copy])
    dp_out_more = Only((1 - hx) * hk, [out_x_copy], hx, [out_x_copy])
    to_home.wait()
    in_up.wait()
    dp_qkv.pass_on()
    dp_out.start()
    dp_up.start()
    tok.pass_on()

    dp_qkv.wait()
    lane_id = lax.broadcasted_iota(jnp.int32, (16, 128), 1)
    for b in range(8):
        for t in range(4):
            block = None
            for m in range(4):
                piece = pack_all[4 * b + m].astype(F32)[0:16, :]
                shift = (32 * (m - t)) % 128
                if shift:
                    piece = pltpu.roll(piece, shift, 1)
                block = piece if block is None else jnp.where(lane_id // 32 == m, piece, block)
            full[16 * t : 16 * t + 16, 128 * b : 128 * b + 128] = block

    gain0, gain1 = full[48:49, :], full[49:50, :]
    shift0, shift1 = full[50:51, :], full[51:52, :]
    lane_cols = many(128 * lane, 128)
    bias_q, bias_v = full[52:53, lane_cols], full[53:54, lane_cols]
    bias_out, bias_down = full[54:55, :], full[55:56, :]
    bias_up = jnp.concatenate(
        [pack_all[16 * y + 8 * (r // 2) + 4 * (r % 2) + 2 * w + c].astype(F32)[16:17, :] for r in range(4)], axis=1
    )
    facts = pack_all[8 * sample].astype(F32)[17:18, :]
    one_lane = lax.broadcasted_iota(jnp.int32, (1, 128), 1)
    present = jnp.where(one_lane < 64, facts, 0.0)
    hours = jnp.sum(jnp.where(one_lane == 64, facts, 0.0), axis=-1, keepdims=True) * hours_scale
    present8 = jnp.broadcast_to(present, (8, 128))[:, :64].astype(BF)
    extra = dot_nn(present8, full[...].astype(BF))[0:1, :] + hours * full[56:57, :]

    tok.wait()

    @pl.loop(0, 4)
    def _(n):
        rows = many(256 * n, 256)
        xhat, _ = center(tok_all[rows, :].astype(F32) + extra)
        normed[rows, :] = (xhat * gain0 + shift0).astype(BF)

    @pl.loop(0, 4)
    def _(n):
        rows = many(256 * n, 256)
        proj = dot_nn(normed[rows, :], wqkv[...])
        q_s[rows, :] = ((proj[:, :128] + bias_q) * 0.125).astype(BF)
        k_s[rows, :] = proj[:, 128:256].astype(BF)
        v_s[rows, :] = (proj[:, 256:384] + bias_v).astype(BF)

    QB = 256
    cot_swap.wait()
    cg = Gather(cot_all)
    cg.start()
    dp_down.start()
    dp_out.wait()
    dp_out_more.start()
    head_lane = lax.broadcasted_iota(jnp.int32, (1, 128), 1) // 64

    def of_head(v, h):
        return jnp.where(head_lane == h, v, jnp.zeros_like(v))

    @pl.loop(0, D // QB)
    def _(n):
        rows = many(QB * n, QB)
        queries = q_s[rows, :]
        total = None
        for h in range(2):
            scores = dot_nt(of_head(queries, h), k_s[...])
            top = jnp.max(scores, axis=-1, keepdims=True)
            e = jnp.exp(scores - top)
            share = (e * (1.0 / jnp.sum(e, axis=-1, keepdims=True))).astype(BF)
            shares[h, rows, :] = share
            got = of_head(dot_nn(share, v_s[...]), h)
            total = got if total is None else total + got
        attf[rows, :] = total
        att[rows, :] = total.astype(BF)

    dp_out_more.wait()

    def rows_of(l_):
        return many(ROWS * l_, ROWS)

    rs_out = Scatter(0, lambda l_: dot_nn(att[rows_of(l_), :], wout[...]))
    rs_out.start()
    rs_out.pass_on()

    cg.pass_on()
    dp_up.pass_on()

    stream = tok_all[my_rows, :].astype(F32) + extra
    mid = stream + (rs_out.wait() + bias_out)
    middle[...] = mid
    xhat2, rstd2 = center(mid)
    n2_all[my_rows, :] = (xhat2 * gain1 + shift1).astype(BF)
    n2 = Gather(n2_all)
    n2.start()
    dp_down.pass_on()
    n2.pass_on()
    dp_up.wait()
    dp_down.wait()
    cg.wait()
    n2.wait()

    upb_g[...] = jnp.zeros_like(upb_g)

    @pl.loop(0, 2)
    def _(n):
        rows = many(512 * n, 512)
        up = dot_nn(n2_all[rows, :], wup[...]) + bias_up
        cdf = 0.5 * (1.0 + erf(up * 0.7071067811865476))
        act[rows, :] = (up * cdf).astype(BF)
        slope = cdf + up * (jnp.exp(-0.5 * up * up) * 0.3989422804014327)
        low = (dot_nt(cot_all[rows, :], wdown[...]) * slope).astype(BF)
        uplow[rows, :] = low
        upb_g[0:1, :] += jnp.sum(low.astype(F32), axis=0, keepdims=True)

    rs_n2 = Scatter(1, lambda l_: dot_nt(uplow[rows_of(l_), :], wup[...]))
    rs_n2.start()

    @pl.loop(0, 4)
    def _(r):
        cols = many(128 * r, 128)
        gdown[cols, :] = dot_tn(act[:, cols], cot_all[...]).astype(BF)

    down_red = Reduce(gdown, xdown, zdown_s, zdown)
    down_red.start()
    rs_n2.pass_on()
    rs_mix = Scatter(2, lambda l_: dot_nn(act[rows_of(l_), :], wdown[...]))
    rs_mix.start()
    upb_sends = Batch([(upb_g.at[:, many(128 * partner(d)[2], 128)], r_upb.at[n], partner(d)[3]) for n, d in enumerate(ranks)])
    upb_sends.start()

    @pl.loop(0, 4)
    def _(n):
        cols = many(256 * n, 256)
        gup[cols, :] = dot_tn(n2_all[:, cols], uplow[...]).astype(BF)

    up_red = Reduce(gup, xup, zup_s, zup)
    up_red.start()

    n2_grad = rs_n2.wait()
    incoming = cot_all[my_rows, :].astype(F32)
    xhat2, rstd2 = center(middle[...])
    mg = incoming + norm_back(xhat2, rstd2, gain1, n2_grad)
    mgrad[...] = mg
    ml_all[my_rows, :] = mg.astype(BF)
    ml = Gather(ml_all)
    ml.start()
    rs_mix.pass_on()
    smallp[7:16, :] = jnp.zeros((9, D), F32)
    smallp[2:3, :] = jnp.sum(n2_grad * xhat2, axis=0, keepdims=True)
    smallp[4:5, :] = jnp.sum(n2_grad, axis=0, keepdims=True)
    smallp[5:6, :] = jnp.sum(mg.astype(BF).astype(F32), axis=0, keepdims=True)
    smallp[6:7, :] = jnp.sum(incoming, axis=0, keepdims=True)

    down_red.pass_on()
    ml.pass_on()
    up_red.pass_on()
    ml.wait()
    mixed_low = (middle[...] + (rs_mix.wait() + bias_down)).astype(BF)
    tgr[2] = mixed_low
    mix_swap = Swap(tgr.at[2], tgr.at[3])
    mix_swap.start()

    @pl.loop(0, 4)
    def _(n):
        rows = many(256 * n, 256)
        dog[rows, :] = dot_nt(ml_all[rows, :], wout[...]).astype(BF)

    dk_acc[...] = jnp.zeros_like(dk_acc)
    dv_acc[...] = jnp.zeros_like(dv_acc)

    def attend_back(n):
        rows = many(QB * n, QB)
        queries = q_s[rows, :]
        grads = dog[rows, :]
        both = grads.astype(F32) * attf[rows, :]
        dq = None
        for h in range(2):
            share = shares[h, rows, :]
            pressure = dot_nt(of_head(grads, h), v_s[...])
            offset = jnp.sum(of_head(both, h), axis=-1, keepdims=True)
            ds = (share.astype(F32) * (pressure - offset)).astype(BF)
            got = of_head(dot_nn(ds, k_s[...]), h)
            dq = got if dq is None else dq + got
            dk_acc[...] += dot_tn(ds, of_head(queries, h))
            dv_acc[...] += dot_tn(share, of_head(grads, h))
        dproj[rows, 0:128] = (dq.astype(BF).astype(F32) * 0.125).astype(BF)

    pl.loop(0, 2)(attend_back)
    pl.loop(2, 4)(attend_back)
    dproj[:, 128:256] = dk_acc[...].astype(BF)
    dproj[:, 256:384] = dv_acc[...].astype(BF)

    @pl.loop(0, 4)
    def _(n):
        cols = many(256 * n, 256)
        gqkv[cols, :] = dot_tn(normed[:, cols], dproj[...]).astype(BF)

    qkv_red = Reduce(gqkv, xqkv, zqkv_s, zqkv)
    qkv_red.start()
    low = dproj[...].astype(F32)
    smallp[8:9, lane_cols] = jnp.sum(low[:, 0:128], axis=0, keepdims=True)
    smallp[9:10, lane_cols] = jnp.sum(low[:, 256:384], axis=0, keepdims=True)
    rs_n1 = Scatter(3, lambda l_: dot_nt(dproj[rows_of(l_), :], wqkv[...]))
    rs_n1.start()

    rs_n1.pass_on()
    gout[...] = dot_tn(att[...], ml_all[...]).astype(BF)
    go_a, go_b = sems(2)
    grad_x = Only(hx, [rc(gout, out_x, go_a, go_b, x_dev)], 1 - hx, [rc(gout, out_x, go_a, go_b, x_dev)])
    grad_z = Only((1 - hx) * hk, [rc(out_s, out_z, go_a + 1, go_b + 1, z_dev)], is_home, [rc(out_s, out_z, go_a + 1, go_b + 1, z_dev)])
    grad_x.start()
    qkv_red.pass_on()
    grad_x.wait()

    @pl.when(hx == 0)
    def _():
        out_s[...] = (gout[...].astype(F32) + out_x[...].astype(F32)).astype(BF)

    grad_z.start()

    n1_grad = rs_n1.wait()
    xhat1, rstd1 = center(tok_all[my_rows, :].astype(F32) + extra)
    tg = mgrad[...] + norm_back(xhat1, rstd1, gain0, n1_grad)
    tgr[0] = tg.astype(BF)
    smallp[0:1, :] = jnp.sum(tg, axis=0, keepdims=True)
    smallp[1:2, :] = jnp.sum(n1_grad * xhat1, axis=0, keepdims=True)
    smallp[3:4, :] = jnp.sum(n1_grad, axis=0, keepdims=True)

    def block(y_, x_, k_):
        return smallp.at[:, many(128 * (4 * y_ + 2 * x_ + k_), 128)]

    copies = []
    for n, d in enumerate(ranks):
        x_, k_, r_, dv = partner(d)
        for y_ in range(2):
            copies.append((block(y_, x_, k_), r_b.at[n, y_], dv))
    small_ranks = Batch(copies)
    small_ranks.start()
    tg_swap = Swap(tgr.at[0], tgr.at[1])
    tg_swap.start()
    small_ranks.wait()
    for y_ in range(2):
        first = smallp[:, many(128 * (4 * y_ + 2 * x + k), 128)]
        s_b[y_, 0:1, :] = first[0:1, :]
        for n in range(3):
            s_b[y_, n + 1 : n + 2, :] = r_b[n, y_, 0:1, :]
        s_b[y_, 4:16, :] = (first + r_b[0, y_] + r_b[1, y_] + r_b[2, y_])[1:13, :]
    small_group = Batch([(s_b.at[peer(d)[0]], r_a.at[n], peer(d)[4]) for n, d in enumerate(group)])
    small_group.start()

    down_red.wait()
    gd_o[...] = down_red.total(0).astype(BF)

    def deal(low_sum, recv):
        copies = []
        for n, d in enumerate(group):
            y_, w_, c_, l_, dv = peer(d)
            copies.append((low_sum.at[many(128 * y_ + 64 * w_ + 32 * c_, 32)], recv.at[lane], dv))
        return Batch(copies)

    def collect(red, low_sum, recv):
        red.wait()
        for y_ in range(2):
            low_sum[128 * y_ : 128 * y_ + 128, :] = red.total(y_).astype(BF)
        batch = deal(low_sum, recv)
        batch.start()
        recv[lane] = low_sum[many(128 * y + 64 * w + 32 * c, 32), :]
        return batch

    up_deal = collect(up_red, su2, ru2)
    grad_z.wait()

    @pl.when(is_home == 1)
    def _():
        so2[...] = (out_s[...].astype(F32) + out_z[...].astype(F32)).astype(BF)
        go_o[...] = so2[out_rows, :]

    outs_a, outs_b = sems(3)
    copies = []
    for n, (dw, dc) in enumerate(pairs):
        w_, c_ = flip(w, dw), flip(c, dc)
        copies.append(rc(so2.at[many(32 * (2 * w_ + c_), 32)], ro2, outs_a + n, outs_b, dev(y, x, k, w_, c_)))
    out_deal = Only(is_home, copies, away, [rc(so2.at[pl.ds(0, 32)], ro2, outs_a, outs_b, home_dev)])
    out_deal.start()
    qkv_deal = collect(qkv_red, sq2, rq2)

    small_group.wait()
    total = s_b[y]
    for n in range(7):
        total = total + r_a[n]
    own_facts = [facts] + [pack_all[8 * (2 * partner(d)[1] + partner(d)[0])].astype(F32)[17:18, :] for d in ranks]
    facts_t = jnp.transpose(jnp.concatenate(own_facts + [jnp.zeros((4, 128), F32)], axis=0))
    table = None
    for n in range(4):
        part = facts_t[:, n : n + 1] * total[n : n + 1, :]
        table = part if table is None else table + part
    small_o[0:64, :] = table[0:64, :]
    small_o[64:80, :] = total
    small_o[80:81, :] = table[64:65, :] * hours_scale
    small_o[81:88, :] = jnp.zeros((7, 128), F32)
    upb_sends.wait()
    sum_upb = upb_g[:, rank_rows]
    for n in range(3):
        sum_upb = sum_upb + r_upb[n]
    small_o[88:96, :] = sum_upb

    out_deal.wait()

    @pl.when(is_home == 0)
    def _():
        go_o[...] = ro2[...]

    @pl.when(off_diag == 0)
    def _():
        tg_o[...] = tgr[0]
        mixed_o[...] = tgr[2]

    mix_swap.wait()
    tg_swap.wait()

    @pl.when(off_diag == 1)
    def _():
        tg_o[...] = tgr[1]
        mixed_o[...] = tgr[3]

    up_deal.wait()
    gu_o[...] = ru2[...]
    qkv_deal.wait()
    gq_o[...] = rq2[...]

    finish_all()


def finish_kernel(
    mixed_i, tg_i, gq_i, go_i, gu_i, gd_i, small_i,
    mixed_o, tg_o, table_o, lead_o, gain_o, shift_o, gq_o, qv_o, go_o, bias_o, gu_o, upb_o, gd_o,
):
    mixed_o[0] = mixed_i[...]
    tg_o[0] = tg_i[...].astype(F32)
    gd_o[...] = gd_i[...].astype(F32)
    go_o[...] = go_i[...].astype(F32)
    for l_ in range(8):
        part = gu_i[l_].astype(F32)
        y_, w_, c_ = l_ // 4, (l_ // 2) % 2, l_ % 2
        for r in range(4):
            at = 128 * (16 * y_ + 8 * (r // 2) + 4 * (r % 2) + 2 * w_ + c_)
            gu_o[:, at : at + 128] = part[:, 128 * r : 128 * r + 128]
        part = gq_i[l_].astype(F32)
        for p in range(3):
            at = 128 * (8 * p + l_)
            gq_o[:, at : at + 128] = part[:, 128 * p : 128 * p + 128]
    place = lax.rem(lax.axis_index("seq"), 4)
    small = small_i[0:88, :]
    mine = small
    for m in range(1, 4):
        mine = jnp.where(place == m, pltpu.roll(small, 128 - 32 * m, 1), mine)
    table_o[...] = jnp.transpose(jnp.concatenate([mine[0:64], jnp.zeros((64, 128), F32)], axis=0))[0:32, 0:48]
    gain_o[...] = mine[68:70, 0:32]
    shift_o[...] = mine[70:72, 0:32]
    bias_o[...] = mine[72:74, 0:32]
    qv_o[...] = mine[75:77, 0:32]
    lead_o[...] = mine[80:81, 0:32]
    upb_o[...] = small_i[88:89, :]


def local_fast(
    tokens, lead_hours, var_mask, var_table, lead_weight, norm_gain, norm_shift, w_qkv, qv_bias, w_out,
    branch_bias, w_up, up_bias, w_down, cotangent,
):
    vm = pltpu.VMEM
    scratch = [
        vm((1, 1), jnp.int32), vm((1, 48), jnp.int32), vm((32, 48), BF), vm((1, 32), BF), vm((2, 32), BF), vm((2, 32), BF),
        vm((2, 32), BF), vm((2, 32), BF), vm((1, 128), BF),
        vm((128, D), BF), vm((32, 3 * D), BF), vm((32, 4 * D), BF), vm((32, D), BF), vm((128, D), BF),
        vm((D, D), BF), vm((D, D), BF), vm((D, D), BF), vm((D, D), BF),
        vm((D, 384), BF), vm((D, FFL), BF), vm((FFL, D), BF), vm((128, D), BF), vm((80, 128), F32), vm((128, 128), F32), vm((32, 128), BF), vm((32, 32, 128), BF), vm((64, D), F32),
        vm((D, D), BF), vm((D, 128), BF), vm((D, 128), BF), vm((D, 128), BF), vm((2, D, D), BF), vm((D, 128), F32), vm((D, 128), BF),
        vm((4, 4, 128, D), BF), vm((4, 4, 128, D), BF), vm((4, 3, 128, D), BF), vm((4, 3, 128, D), BF), vm((4, 128, D), F32), vm((4, 2, 64, D), F32),
        vm((128, D), F32), vm((128, D), F32), vm((D, FFL), BF), vm((D, FFL), BF), vm((D, 384), BF), vm((D, 128), BF), vm((D, 128), F32), vm((D, 128), F32),
        vm((D, 384), BF), vm((D, FFL), BF), vm((FFL, D), BF), vm((128, D), BF),
        vm((2, 256, 384), BF), vm((2, 256, FFL), BF), vm((1, 256, D), BF),
        vm((2, 128, 384), BF), vm((2, 128, FFL), BF), vm((1, 128, D), BF),
        vm((2, 128, 384), BF), vm((2, 128, FFL), BF), vm((1, 128, D), BF),
        vm((128, D), BF), vm((128, D), BF), vm((128, D), BF),
        vm((256, 384), BF), vm((256, FFL), BF), vm((8, 32, 384), BF), vm((8, 32, FFL), BF), vm((128, D), BF), vm((32, D), BF),
        vm((4, 128, D), BF), vm((16, D), F32), vm((7, 16, 128), F32), vm((2, 16, 128), F32), vm((3, 2, 16, 128), F32),
        vm((8, FFL), F32), vm((3, 8, 128), F32),
        pltpu.SemaphoreType.DMA((320,)), pltpu.SemaphoreType.DMA((320,)), pltpu.SemaphoreType.DMA((24,)),
    ]
    shape = jax.ShapeDtypeStruct
    raw = pl.pallas_call(
        fast_kernel,
        out_shape=[
            shape((128, D), BF), shape((128, D), BF), shape((8, 32, 384), BF), shape((32, D), BF), shape((8, 32, FFL), BF),
            shape((128, D), BF), shape((96, 128), F32),
        ],
        in_specs=[pl.BlockSpec(memory_space=pl.ANY)] * 15,
        out_specs=[pl.BlockSpec(memory_space=vm)] * 7,
        scratch_shapes=scratch,
        compiler_params=pltpu.CompilerParams(collective_id=0, has_side_effects=True, vmem_limit_bytes=62 * 2**20),
        cost_estimate=pl.CostEstimate(flops=14_000_000_000, bytes_accessed=4_000_000, transcendentals=6_000_000),
    )(
        tokens[0], lead_hours[None], var_mask, var_table.T, lead_weight[None], norm_gain, norm_shift, w_qkv, qv_bias, w_out,
        branch_bias, w_up, up_bias[None], w_down, cotangent[0],
    )
    out = pl.pallas_call(
        finish_kernel,
        out_shape=[
            shape((1, 128, D), BF), shape((1, 128, D), F32), shape((32, 48), F32), shape((1, 32), F32), shape((2, 32), F32),
            shape((2, 32), F32), shape((32, 3 * D), F32), shape((2, 32), F32), shape((32, D), F32), shape((2, 32), F32),
            shape((32, 4 * D), F32), shape((1, 128), F32), shape((128, D), F32),
        ],
        in_specs=[pl.BlockSpec(memory_space=vm)] * 7,
        out_specs=[pl.BlockSpec(memory_space=vm)] * 13,
        compiler_params=pltpu.CompilerParams(vmem_limit_bytes=62 * 2**20),
        cost_estimate=pl.CostEstimate(flops=1_000_000, bytes_accessed=4_000_000, transcendentals=0),
    )(*raw)
    mixed, tg, table, lead, gain, shift, gq, qv, go, bias, gu, upb, gd = out
    return (mixed, tg, table.T, lead[0], gain, shift, gq, qv, go, bias, gu, upb[0], gd)


def solution(mesh):
    sizes = dict(mesh.shape)
    fast = sizes == {"samp": 4, "seq": 8}
    return jax.shard_map(
        local_fast if fast else local,
        mesh=mesh,
        in_specs=(
            P("samp", "seq", None),
            P("samp"),
            P("samp", None),
            P(None, ("samp", "seq")),
            P(("samp", "seq")),
            P(None, ("samp", "seq")),
            P(None, ("samp", "seq")),
            P(("samp", "seq"), None),
            P(None, ("samp", "seq")),
            P(("samp", "seq"), None),
            P(None, ("samp", "seq")),
            P(("samp", "seq"), None),
            P(("samp", "seq")),
            P(("samp", "seq"), None),
            P("samp", "seq", None),
        ),
        out_specs=(
            P("samp", "seq", None),
            P("samp", "seq", None),
            P(None, ("samp", "seq")),
            P(("samp", "seq")),
            P(None, ("samp", "seq")),
            P(None, ("samp", "seq")),
            P(("samp", "seq"), None),
            P(None, ("samp", "seq")),
            P(("samp", "seq"), None),
            P(None, ("samp", "seq")),
            P(("samp", "seq"), None),
            P(("samp", "seq")),
            P(("samp", "seq"), None),
        ),
        check_vma=False,
    )
```
